32 devices in a mesh: grid: 8 (over z, y), orb: 4 (over x, core).
Axes of the slice: x: 2, y: 2, z: 4, core: 2. Of those that a mesh axis runs over, the one named last changes fastest.
Arguments:
- orbitals: float32 [16, 64, 32, 128], P('orb', 'grid'), may hold values from -6 to 6
- potential: float32 [64, 32, 128], P('grid'), may hold values from -1 to 1
Outputs:
- filtered: float32 [16, 64, 32, 128], P('orb', 'grid')
- correlation: float32 [16, 16], P('orb')
- hamiltonian: float32 [16, 16], P('orb')
The draws below stay inside these ranges and needn't reach their ends.
All inputs are finite; a program needn't handle non-finite values.
Results may differ from the reference program's by a relative error of at most 0.00005.
Values sent between devices are 32-bit elements; how exact they have to be, the bound alone decides.
No kernel may reach another device: no remote copies, remote signals or barrier semaphores. Data moves between devices by JAX's collectives and lax.ppermute only.
A program may use at most 64 MiB of HBM per device.

```python
import jax
import jax.numpy as jnp
from jax import lax

NY = 32
NZ = 128
ORBS = 16
NX = 64


def block_levels(key, extent, shards, smallest, largest):
    level, own = 1.0, jax.random.fold_in(key, 6)
    for position, shards_of in shards:
        steps = jnp.exp(jax.random.uniform(jax.random.fold_in(own, position), (shards_of,), jnp.float32, smallest / len(shards), largest / len(shards)))
        level = level * jnp.repeat(steps, extent[position] // shards_of).reshape([-1 if axis == position else 1 for axis in range(len(extent))])
    return level


def gaussian(own_key, extent, scale, reach, split=(), held_as=jnp.bfloat16):
    loudness = block_levels(own_key, extent, split, -0.22, 0.18) if split else 1.0
    drawn = jax.random.normal(own_key, extent, jnp.float32) * scale * loudness
    return jnp.minimum(jnp.maximum(drawn, -reach), reach).astype(held_as)


def setup_inputs(seed: int = 0) -> dict:
    key_of = jax.random.split(jax.random.key(seed), 3)
    orbitals = gaussian(key_of[0], (ORBS, NX, NY, NZ), 1.0, 6.0, ((0, 4), (1, 8)), jnp.float32)
    potential = jnp.clip(jax.random.uniform(key_of[1], (NX, NY, NZ), jnp.float32, -1.0, 1.0) * block_levels(key_of[1], (NX, NY, NZ), ((0, 8),), -0.4, 0.0), -1.0, 1.0)
    return {"orbitals": orbitals, "potential": potential}


COEFS = (-205.0 / 72.0, 8.0 / 5.0, -1.0 / 5.0, 8.0 / 315.0, -1.0 / 560.0)
LOWER = -1.0
CUT = 4.0
UPPER = 10.0


def apply_ham(field, potential):
    lap = 3.0 * COEFS[0] * field
    for axis_pos in range(3):
        for shift_by in range(1, 5):
            lap = lap + COEFS[shift_by] * (jnp.roll(field, shift_by, axis_pos) + jnp.roll(field, -shift_by, axis_pos))
    return -0.5 * lap + potential * field


def filter_one(start, potential):
    half = (UPPER - CUT) / 2.0
    centre = (UPPER + CUT) / 2.0
    first_sigma = half / (LOWER - centre)
    previous = start
    current = (apply_ham(start, potential) - centre * start) * (first_sigma / half)
    sigma = first_sigma
    for step in range(3):
        sigma_new = 1.0 / (2.0 / first_sigma - sigma)
        following = (2.0 * sigma_new / half) * (apply_ham(current, potential) - centre * current) - (sigma * sigma_new) * previous
        previous = current
        current = following
        sigma = sigma_new
    return current, apply_ham(current, potential)


def reference(orbitals, potential):
    filtered, applied = lax.map(lambda start: filter_one(start, potential), orbitals)
    count = orbitals.shape[0]
    cells = orbitals.shape[1] * orbitals.shape[2] * orbitals.shape[3]
    flat_y = filtered.reshape(count, cells)
    flat_h = applied.reshape(count, cells)
    correlation = jnp.dot(flat_y, flat_y.T, precision=lax.Precision.HIGHEST) / cells
    hamiltonian = jnp.dot(flat_h, flat_y.T, precision=lax.Precision.HIGHEST) / cells
    return filtered, correlation, hamiltonian
```

```python
import functools

import jax
import jax.numpy as jnp
from jax import lax
from jax.experimental import pallas as pl
from jax.experimental.pallas import tpu as pltpu
from jax.sharding import Mesh, PartitionSpec as P

COEFS = (-205.0 / 72.0, 8.0 / 5.0, -1.0 / 5.0, 8.0 / 315.0, -1.0 / 560.0)
SCALE = 5040.0
WHOLE = (8064.0, -1008.0, 128.0, -9.0)
LOWER = -1.0
CUT = 4.0
UPPER = 10.0
HALF = (UPPER - CUT) / 2.0
CENTRE = (UPPER + CUT) / 2.0
S1 = HALF / (LOWER - CENTRE)
T2 = 2.0 / S1**2 - 1.0
T4 = 2.0 * T2 * T2 - 1.0
PEERS = (1, 6, 7, 4, 2, 5, 3, 0)
CHUNK = 4


def ring_matrix(rows, cols, ring):
    row = lax.broadcasted_iota(jnp.int32, (rows, cols), 0)
    col = lax.broadcasted_iota(jnp.int32, (rows, cols), 1)
    size = min(rows, cols)
    row, col = lax.rem(row, size), lax.rem(col, size)
    gap = jnp.abs(row - col)
    out = jnp.zeros((rows, cols), jnp.float32)
    for k, value in enumerate(WHOLE, 1):
        out = jnp.where((gap == k) | (gap == ring - k), value, out)
    return jnp.where(row // ring == col // ring, out, 0.0).astype(jnp.bfloat16)


def matrices(ymat, zmat, ring):
    ymat[...] = ring_matrix(*ymat.shape, ring)
    zmat[...] = ring_matrix(*zmat.shape, zmat.shape[1])


def sweep(at, count, v_at, gain, centre, emit, mats, yz, one_sided=False):
    ymat, zmat = mats
    ny, nz = ymat.shape[0] // CHUNK, zmat.shape[1]
    share = 0.5 * gain if one_sided else gain

    def along_yz(c):
        f = jnp.concatenate([at(c + j, slice(0, ny)) for j in range(CHUNK)], axis=0)
        high = f.astype(jnp.bfloat16)
        rest = f - high.astype(jnp.float32)
        mid = rest.astype(jnp.bfloat16)
        low = (rest - mid.astype(jnp.float32)).astype(jnp.bfloat16)
        z = jnp.dot(jnp.concatenate([high, mid, low], axis=1), zmat[...], preferred_element_type=jnp.float32)
        y = jnp.dot(ymat[...], jnp.concatenate([high, mid, low], axis=0), preferred_element_type=jnp.float32)
        yz[c // CHUNK] = y + z

    along_yz(0)
    for c in range(0, count, CHUNK):
        if c + CHUNK < count:
            along_yz(c + CHUNK)
        for r in range(0, ny, 8):
            rows = slice(r, r + 8)
            f = {i: at(i, rows) for i in range(c if one_sided else c - 4, c + CHUNK + 4)}
            for j in range(CHUNK):
                i = c + j
                total = (share * v_at(i, rows) + share * (-1.5 * COEFS[0] - centre)) * f[i]
                total = total + (-0.5 * share / SCALE) * yz[c // CHUNK, j * ny + r : j * ny + r + 8, :]
                for k in range(1, 5):
                    if one_sided:
                        total = total + (-0.5 * gain * COEFS[k]) * f[i + k]
                    else:
                        total = total + (-0.5 * gain * COEFS[k]) * (f[i - k] + f[i + k])
                emit(i, rows, total)


def places():
    m, place = lax.axis_index("mem"), lax.axis_index("orb")
    return m, place, m * lax.axis_size("orb") + place


def first_two(ymat, zmat, mine, ra, rb, rc, *refs):
    m = places()[0]
    mats = (ymat, zmat)
    n = rc.shape[1] if len(refs) == 7 else refs[0].shape[0]
    own, blocks = n + n * m, ((ra, 2 * n - n * m), (rb, 3 * n * m), (rc, 3 * n - 3 * n * m))
    if len(refs) == 7:
        v, lo_ref, hi_ref, y0_ref, y0, w, yz = refs
    else:
        potential, lo_ref, hi_ref, y0_ref, v, y0, w, yz = refs
        v[pl.ds(4 + n * m, n)] = potential[...]
        v[pl.ds(4 + n - n * m, n)] = ra[0, n:]
        v[pl.ds((2 * n + 4) * m, 4)] = rb[0, n:]
        v[pl.ds((2 * n + 4) * (1 - m), 4)] = rc[0, n:]
        lo_ref[0, n + 4 :] = v[8 : 4 + n]
    y0[pl.ds(own, n)] = mine[0, :n]
    for ref, at in blocks:
        y0[pl.ds(at, n)] = ref[0, :n]
    y0_ref[0] = y0[n : 3 * n + 4]

    def one(i, rows, total):
        w[i, rows, :] = total

    sweep(lambda i, r: y0[4 + i, r, :], 2 * n + 8, lambda i, r: v[i, r, :], 1.0 / HALF, CENTRE, one, mats, yz)

    def two(i, rows, total):
        y2 = total - (1.0 / T2) * y0[n + i, rows, :]
        if i < n + 4:
            lo_ref[0, i, rows, :] = y2
        if i >= n:
            hi_ref[0, i - n, rows, :] = y2

    sweep(
        lambda i, r: w[4 + i, r, :], 2 * n, lambda i, r: v[4 + i, r, :], 2.0 / (T2 * HALF), CENTRE, two, mats, yz
    )


def last_three(ymat, zmat, rlo, lo, hi, rhi, y0, v, v_above, *refs):
    outs, (both, u, f, yz) = refs[:-4], refs[-4:]
    mats = (ymat, zmat)
    n = hi.shape[1]

    def y2(i, rows):
        for ref, start in ((rlo, -n), (lo, 0), (hi, n)):
            if i < start + n:
                return ref[0, i - start, rows, :]
        return rhi[0, i - 2 * n, rows, :]

    def three(i, rows, total):
        u[i, rows, :] = total

    def v_at(i, rows):
        return v[i + 4, rows, :] if i < 2 * n + 4 else v_above[0, i - n, rows, :]

    sweep(lambda i, r: y2(i - 4, r), 2 * n + 12, lambda i, r: v_at(i - 4, r), 1.0 / HALF, CENTRE, three, mats, yz)

    def four(i, rows, total):
        f[i, rows, :] = total - (2.0 * T2 / T4) * y2(i, rows) - (1.0 / T4) * y0[0, i, rows, :]

    sweep(lambda i, r: u[4 + i, r, :], 2 * n + 4, v_at, 4.0 * T2 / (T4 * HALF), CENTRE, four, mats, yz)

    def five(i, rows, total):
        both[0, i, rows, :] = f[i, rows, :]
        both[1, i, rows, :] = total

    sweep(lambda i, r: f[i, r, :], 2 * n, v_at, 1.0, 0.0, five, mats, yz, one_sided=True)
    m, _, me = places()
    homes = (n * m, n - n * m)

    def cells(which, k, per):
        return both[which, pl.ds(per * jnp.bitwise_xor(me, k), per)]

    if len(outs) == 2:
        blocks, home = outs
        for k in range(blocks.shape[0]):
            for which in range(2):
                blocks[k, which] = cells(which, k, blocks.shape[2])
        for i, start in enumerate(homes):
            home[i] = both[0, pl.ds(start, n)]
    else:
        blocks_a, home_a, keep, send, *blocks = outs
        for k, block in enumerate(blocks):
            block[0] = blocks_a[k]
            for which in range(2):
                block[1, which] = cells(which, k, block.shape[2])
        for i, ref in enumerate((keep, send)):
            ref[0] = home_a[i]
            ref[1] = both[0, pl.ds(homes[i], n)]


def gram(*refs):
    *xs, out_ref, part = refs
    orbs = part.shape[1]
    half, _, per, ny, nz = xs[0].shape
    rows = per * ny // 2
    each = 4 * half
    size = len(xs) * each
    flat = [x.reshape(each * rows, nz) for x in xs]
    fields = jnp.concatenate(
        [
            jnp.concatenate([x[pl.ds(r, each, stride=rows), :] for x in flat], axis=0)
            for r in range(rows)
        ],
        axis=1,
    )

    def product(a, b, contract):
        return lax.dot_general(
            a, b, ((contract[:1], contract[1:]), ((), ())),
            precision=lax.Precision.HIGHEST, preferred_element_type=jnp.float32,
        )

    both = product(fields, fields, (1, 1))
    row = lax.broadcasted_iota(jnp.int32, (size, size), 0)
    col = lax.broadcasted_iota(jnp.int32, (size, size), 1)
    both = jnp.where(row % 2 == col % 2, both, 0.0)
    col = lax.broadcasted_iota(jnp.int32, (2 * orbs, size), 1)
    which_peer = col // each
    peer = jnp.zeros_like(col)
    for i, k in enumerate(PEERS):
        peer = jnp.where(which_peer == i, k, peer)
    peer = jnp.bitwise_xor(peer, places()[2])
    target = orbs * (col // 2 % 2) + 2 * half * (peer % 4) + half * (peer // 4) + col // 4 % half
    order = (lax.broadcasted_iota(jnp.int32, (2 * orbs, size), 0) == target).astype(jnp.float32)
    both = product(order, product(both, order, (1, 1)), (1, 0))
    part[...] = jnp.zeros_like(part)
    part[0, :, :orbs] = both[:orbs, :orbs]
    part[1, :, :orbs] = both[orbs:, :orbs] + both[:orbs, orbs:]
    own = nz // (2 * orbs)
    groups = orbs // own
    packed = part[0, pl.ds(0, groups, stride=own), :]
    for i in range(1, 2 * own):
        packed = packed + pltpu.roll(part[i // own, pl.ds(i % own, groups, stride=own), :], i * orbs, 1)

    def spread(g, _):
        out_ref[pl.ds(g * groups, groups)] = packed.reshape(groups, 1, nz)
        return 0

    lax.fori_loop(0, out_ref.shape[0] // groups, spread, 0)


def finish(cells, x_ref, c_ref, h_ref):
    sums = jnp.sum(x_ref[...], axis=0) * (1.0 / cells)
    own, count = c_ref.shape
    nz = sums.shape[1]
    for r in range(own):
        c_ref[r : r + 1, :] = pltpu.roll(sums, (nz - r * count) % nz, 1)[:, :count]
        h_ref[r : r + 1, :] = pltpu.roll(sums, (nz - (own + r) * count) % nz, 1)[:, :count]


VMEM = pl.BlockSpec(memory_space=pltpu.VMEM)


def call(body, operands, outs, scratch, us, name):
    return pl.pallas_call(
        body,
        out_shape=[s if isinstance(s, jax.ShapeDtypeStruct) else jax.ShapeDtypeStruct(s, jnp.float32) for s in outs],
        in_specs=[VMEM] * len(operands),
        out_specs=[VMEM] * len(outs),
        scratch_shapes=scratch,
        cost_estimate=pl.CostEstimate(flops=int(us * 1e9), bytes_accessed=int(us * 3.5e6), transcendentals=0),
        compiler_params=pltpu.CompilerParams(vmem_limit_bytes=32 << 20),
        name=name,
    )(*operands)


def per_device(cells_x, orbitals, potential):
    pairs, orbs = lax.axis_size("pair"), lax.axis_size("orb")
    size = 2 * pairs
    grid_axes = ("pair", "mem")
    m = lax.axis_index("mem")
    own_orbs, n, ny, nz = orbitals.shape
    half = own_orbs // 2
    count = orbs * own_orbs
    swap = [(g, g ^ 1) for g in range(size)]
    cross = [(g, (g + 1) % size if g % 2 else (g - 1) % size) for g in range(size)]
    along = [(g, (g + 2) % size if g % 2 else (g - 2) % size) for g in range(size)]
    up = [(g, (g + 2) % size) for g in range(size)]
    down = [(g, (g - 2) % size) for g in range(size)]
    f32, bf16 = jnp.float32, jnp.bfloat16
    rows = CHUNK * ny
    mats = call(
        functools.partial(lambda ring, ymat, zmat: matrices(ymat, zmat, ring), ny),
        (),
        [jax.ShapeDtypeStruct((rows, 3 * rows), bf16), jax.ShapeDtypeStruct((3 * nz, nz), bf16)],
        [],
        0.5,
        "matrices",
    )

    v = potential[None]
    v4 = jnp.where(m == 0, v[:, :4], v[:, n - 4 :])
    first = []
    for o in range(half):
        a = b = lax.dynamic_slice_in_dim(orbitals, half * (1 - m) + o, 1, 0)
        c = lax.dynamic_slice_in_dim(orbitals, half * m + o, 1, 0)
        if o == 0:
            a, b, c = jnp.concatenate([a, v], 1), jnp.concatenate([b, v4], 1), jnp.concatenate([c, v4], 1)
        ra = lax.ppermute(a, grid_axes, swap)
        rb = lax.ppermute(b, grid_axes, cross)
        rc = lax.ppermute(c, grid_axes, along)
        first.append((*mats, c, ra, rb, rc))

    def field(layers):
        return pltpu.VMEM((layers, ny, nz), f32)

    def products(layers):
        return pltpu.VMEM((layers // CHUNK, rows, nz), f32)

    second, v_above = [], None
    for o in range(half):
        outs = [(1, n + 4, ny, nz), (1, n, ny, nz), (1, 2 * n + 4, ny, nz)]
        scratch = [field(4 * n), field(2 * n + 8), products(2 * n + 8)]
        if o == 0:
            outs = [(1, 2 * n, ny, nz)] + outs[1:] + [(2 * n + 8, ny, nz)]
            lo, hi, y0, vext = call(first_two, first[o] + (potential,), outs, scratch, 1.0, "filter_1_2")
        else:
            lo, hi, y0 = call(first_two, first[o] + (vext,), outs, scratch, 10.0, "filter_1_2")
        rlo = lax.ppermute(hi, grid_axes, up)
        rhi = lax.ppermute(lo, grid_axes, down)
        v_above = rhi if o == 0 else v_above
        second.append((*mats, rlo, lo, hi, rhi, y0, vext, v_above))

    group = 2 * orbs
    per = 2 * n // group
    scratch = [pltpu.VMEM((2, 2 * n, ny, nz), f32), field(2 * n + 12), field(2 * n + 4), products(2 * n + 12)]
    outs = [(group, 2, per, ny, nz), (2, n, ny, nz)]
    results = call(last_three, second[0], outs, scratch, 1.5, "filter_3_4_hamiltonian")
    outs = [(half, n, ny, nz)] * 2 + [(half, 2, per, ny, nz)] * group
    results = call(last_three, (*second[1], *results), outs, scratch, 1.5, "filter_3_4_hamiltonian")
    keep, send, *blocks = results
    xs = [
        lax.ppermute(blocks[k], ("mem", "orb"), [(t, t ^ k) for t in range(group)]) if k else blocks[0] for k in PEERS
    ]
    send, xs[2] = lax.optimization_barrier((send, xs[2]))
    back = lax.ppermute(send, grid_axes, swap)
    (sums,) = call(
        gram,
        xs,
        [(size * orbs, 1, 2 * own_orbs * count)],
        [pltpu.VMEM((2, count, nz), f32)],
        1.3,
        "gram",
    )
    sums = lax.all_to_all(sums, ("pair", "mem", "orb"), 0, 0, tiled=True)
    filtered = jnp.where(m == 0, jnp.concatenate([keep, back]), jnp.concatenate([back, keep]))
    sums, filtered = lax.optimization_barrier((sums, filtered))
    corr, ham = call(
        functools.partial(finish, float(cells_x * ny * nz)), (sums,), [(own_orbs, count)] * 2, [], 0.3, "finish"
    )
    return filtered, corr, ham


def solution(mesh):
    devices = mesh.devices
    size, orbs = devices.shape
    fine = Mesh(devices.reshape(size // 2, 2, orbs), ("pair", "mem", "orb"))
    grid = ("pair", "mem")

    def whole(orbitals, potential):
        return jax.shard_map(
            functools.partial(per_device, orbitals.shape[1]),
            mesh=fine,
            in_specs=(P("orb", grid, None, None), P(grid, None, None)),
            out_specs=(P("orb", grid, None, None), P("orb", None), P("orb", None)),
            check_vma=False,
        )(orbitals, potential)

    return whole
```

```python
import functools

import jax
import jax.numpy as jnp
from jax import lax
from jax.experimental import pallas as pl
from jax.experimental.pallas import tpu as pltpu
from jax.sharding import Mesh, PartitionSpec as P

COEFS = (-205.0 / 72.0, 8.0 / 5.0, -1.0 / 5.0, 8.0 / 315.0, -1.0 / 560.0)
SCALE = 5040.0
WHOLE = (8064.0, -1008.0, 128.0, -9.0)
LOWER = -1.0
CUT = 4.0
UPPER = 10.0
HALF = (UPPER - CUT) / 2.0
CENTRE = (UPPER + CUT) / 2.0
S1 = HALF / (LOWER - CENTRE)
T2 = 2.0 / S1**2 - 1.0
T4 = 2.0 * T2 * T2 - 1.0
PEERS = (1, 6, 7, 4, 2, 5, 3, 0)
CHUNK = 4


def ring_matrix(rows, cols, ring):
    row = lax.broadcasted_iota(jnp.int32, (rows, cols), 0)
    col = lax.broadcasted_iota(jnp.int32, (rows, cols), 1)
    size = min(rows, cols)
    row, col = lax.rem(row, size), lax.rem(col, size)
    gap = jnp.abs(row - col)
    out = jnp.zeros((rows, cols), jnp.float32)
    for k, value in enumerate(WHOLE, 1):
        out = jnp.where((gap == k) | (gap == ring - k), value, out)
    return jnp.where(row // ring == col // ring, out, 0.0).astype(jnp.bfloat16)


def matrices(ymat, zmat, ring):
    ymat[...] = ring_matrix(*ymat.shape, ring)
    zmat[...] = ring_matrix(*zmat.shape, zmat.shape[1])


def sweep(at, count, v_at, gain, centre, emit, mats, yz, one_sided=False):
    ymat, zmat = mats
    ny, nz = ymat.shape[0] // CHUNK, zmat.shape[1]
    share = 0.5 * gain if one_sided else gain

    def along_yz(c):
        f = jnp.concatenate([at(c + j, slice(0, ny)) for j in range(CHUNK)], axis=0)
        high = f.astype(jnp.bfloat16)
        rest = f - high.astype(jnp.float32)
        mid = rest.astype(jnp.bfloat16)
        low = (rest - mid.astype(jnp.float32)).astype(jnp.bfloat16)
        z = jnp.dot(jnp.concatenate([high, mid, low], axis=1), zmat[...], preferred_element_type=jnp.float32)
        y = jnp.dot(ymat[...], jnp.concatenate([high, mid, low], axis=0), preferred_element_type=jnp.float32)
        yz[c // CHUNK] = y + z

    along_yz(0)
    for c in range(0, count, CHUNK):
        if c + CHUNK < count:
            along_yz(c + CHUNK)
        for r in range(0, ny, 8):
            rows = slice(r, r + 8)
            f = {i: at(i, rows) for i in range(c if one_sided else c - 4, c + CHUNK + 4)}
            for j in range(CHUNK):
                i = c + j
                total = (share * v_at(i, rows) + share * (-1.5 * COEFS[0] - centre)) * f[i]
                total = total + (-0.5 * share / SCALE) * yz[c // CHUNK, j * ny + r : j * ny + r + 8, :]
                for k in range(1, 5):
                    if one_sided:
                        total = total + (-0.5 * gain * COEFS[k]) * f[i + k]
                    else:
                        total = total + (-0.5 * gain * COEFS[k]) * (f[i - k] + f[i + k])
                emit(i, rows, total)


def places():
    m, place = lax.axis_index("mem"), lax.axis_index("orb")
    return m, place, m * lax.axis_size("orb") + place


def first_two(ymat, zmat, mine, ra, rb, rc, *refs):
    m = places()[0]
    mats = (ymat, zmat)
    n = rc.shape[1] if len(refs) == 7 else refs[0].shape[0]
    own, blocks = n + n * m, ((ra, 2 * n - n * m), (rb, 3 * n * m), (rc, 3 * n - 3 * n * m))
    if len(refs) == 7:
        v, lo_ref, hi_ref, y0_ref, y0, w, yz = refs
    else:
        potential, lo_ref, hi_ref, y0_ref, v, y0, w, yz = refs
        v[pl.ds(4 + n * m, n)] = potential[...]
        v[pl.ds(4 + n - n * m, n)] = ra[0, n:]
        v[pl.ds((2 * n + 4) * m, 4)] = rb[0, n:]
        v[pl.ds((2 * n + 4) * (1 - m), 4)] = rc[0, n:]
        lo_ref[0, n + 4 :] = v[8 : 4 + n]
    y0[pl.ds(own, n)] = mine[0, :n]
    for ref, at in blocks:
        y0[pl.ds(at, n)] = ref[0, :n]
    y0_ref[0] = y0[n : 3 * n + 4]

    def one(i, rows, total):
        w[i, rows, :] = total

    sweep(lambda i, r: y0[4 + i, r, :], 2 * n + 8, lambda i, r: v[i, r, :], 1.0 / HALF, CENTRE, one, mats, yz)

    def two(i, rows, total):
        y2 = total - (1.0 / T2) * y0[n + i, rows, :]
        if i < n + 4:
            lo_ref[0, i, rows, :] = y2
        if i >= n:
            hi_ref[0, i - n, rows, :] = y2

    sweep(
        lambda i, r: w[4 + i, r, :], 2 * n, lambda i, r: v[4 + i, r, :], 2.0 / (T2 * HALF), CENTRE, two, mats, yz
    )


def last_three(ymat, zmat, rlo, lo, hi, rhi, y0, v, v_above, *refs):
    outs, (both, u, f, yz) = refs[:-4], refs[-4:]
    mats = (ymat, zmat)
    n = hi.shape[1]

    def y2(i, rows):
        for ref, start in ((rlo, -n), (lo, 0), (hi, n)):
            if i < start + n:
                return ref[0, i - start, rows, :]
        return rhi[0, i - 2 * n, rows, :]

    def three(i, rows, total):
        u[i, rows, :] = total

    def v_at(i, rows):
        return v[i + 4, rows, :] if i < 2 * n + 4 else v_above[0, i - n, rows, :]

    sweep(lambda i, r: y2(i - 4, r), 2 * n + 12, lambda i, r: v_at(i - 4, r), 1.0 / HALF, CENTRE, three, mats, yz)

    def four(i, rows, total):
        f[i, rows, :] = total - (2.0 * T2 / T4) * y2(i, rows) - (1.0 / T4) * y0[0, i, rows, :]

    sweep(lambda i, r: u[4 + i, r, :], 2 * n + 4, v_at, 4.0 * T2 / (T4 * HALF), CENTRE, four, mats, yz)

    def five(i, rows, total):
        both[0, i, rows, :] = f[i, rows, :]
        both[1, i, rows, :] = total

    sweep(lambda i, r: f[i, r, :], 2 * n, v_at, 1.0, 0.0, five, mats, yz, one_sided=True)
    m, _, me = places()
    homes = (n * m, n - n * m)

    def cells(which, k, per):
        return both[which, pl.ds(per * jnp.bitwise_xor(me, k), per)]

    if len(outs) == 2:
        blocks, home = outs
        for k in range(blocks.shape[0]):
            for which in range(2):
                blocks[k, which] = cells(which, k, blocks.shape[2])
        for i, start in enumerate(homes):
            home[i] = both[0, pl.ds(start, n)]
    else:
        blocks_a, home_a, keep, send, *blocks = outs
        for k, block in enumerate(blocks):
            block[0] = blocks_a[k]
            for which in range(2):
                block[1, which] = cells(which, k, block.shape[2])
        for i, ref in enumerate((keep, send)):
            ref[0] = home_a[i]
            ref[1] = both[0, pl.ds(homes[i], n)]


def gram(*refs):
    *xs, out_ref, part = refs
    orbs = part.shape[1]
    half, _, per, ny, nz = xs[0].shape
    rows = per * ny // 2
    each = 4 * half
    size = len(xs) * each
    flat = [x.reshape(each * rows, nz) for x in xs]
    fields = jnp.concatenate(
        [
            jnp.concatenate([x[pl.ds(r, each, stride=rows), :] for x in flat], axis=0)
            for r in range(rows)
        ],
        axis=1,
    )

    def product(a, b, contract):
        return lax.dot_general(
            a, b, ((contract[:1], contract[1:]), ((), ())),
            precision=lax.Precision.HIGHEST, preferred_element_type=jnp.float32,
        )

    both = product(fields, fields, (1, 1))
    row = lax.broadcasted_iota(jnp.int32, (size, size), 0)
    col = lax.broadcasted_iota(jnp.int32, (size, size), 1)
    both = jnp.where(row % 2 == col % 2, both, 0.0)
    col = lax.broadcasted_iota(jnp.int32, (2 * orbs, size), 1)
    which_peer = col // each
    peer = jnp.zeros_like(col)
    for i, k in enumerate(PEERS):
        peer = jnp.where(which_peer == i, k, peer)
    peer = jnp.bitwise_xor(peer, places()[2])
    target = orbs * (col // 2 % 2) + 2 * half * (peer % 4) + half * (peer // 4) + col // 4 % half
    order = (lax.broadcasted_iota(jnp.int32, (2 * orbs, size), 0) == target).astype(jnp.float32)
    both = product(order, product(both, order, (1, 1)), (1, 0))
    part[...] = jnp.zeros_like(part)
    part[0, :, :orbs] = both[:orbs, :orbs]
    part[1, :, :orbs] = both[orbs:, :orbs] + both[:orbs, orbs:]
    own = nz // (2 * orbs)
    groups = orbs // own
    packed = part[0, pl.ds(0, groups, stride=own), :]
    for i in range(1, 2 * own):
        packed = packed + pltpu.roll(part[i // own, pl.ds(i % own, groups, stride=own), :], i * orbs, 1)

    def spread(g, _):
        out_ref[pl.ds(g * groups, groups)] = packed.reshape(groups, 1, nz)
        return 0

    lax.fori_loop(0, out_ref.shape[0] // groups, spread, 0)


def finish(cells, x_ref, c_ref, h_ref):
    sums = jnp.sum(x_ref[...], axis=0) * (1.0 / cells)
    own, count = c_ref.shape
    nz = sums.shape[1]
    for r in range(own):
        c_ref[r : r + 1, :] = pltpu.roll(sums, (nz - r * count) % nz, 1)[:, :count]
        h_ref[r : r + 1, :] = pltpu.roll(sums, (nz - (own + r) * count) % nz, 1)[:, :count]


VMEM = pl.BlockSpec(memory_space=pltpu.VMEM)


def call(body, operands, outs, scratch, us, name):
    return pl.pallas_call(
        body,
        out_shape=[s if isinstance(s, jax.ShapeDtypeStruct) else jax.ShapeDtypeStruct(s, jnp.float32) for s in outs],
        in_specs=[VMEM] * len(operands),
        out_specs=[VMEM] * len(outs),
        scratch_shapes=scratch,
        cost_estimate=pl.CostEstimate(flops=int(us * 1e9), bytes_accessed=int(us * 3.5e6), transcendentals=0),
        compiler_params=pltpu.CompilerParams(vmem_limit_bytes=32 << 20),
        name=name,
    )(*operands)


def per_device(cells_x, orbitals, potential):
    pairs, orbs = lax.axis_size("pair"), lax.axis_size("orb")
    size = 2 * pairs
    grid_axes = ("pair", "mem")
    m = lax.axis_index("mem")
    own_orbs, n, ny, nz = orbitals.shape
    half = own_orbs // 2
    count = orbs * own_orbs
    swap = [(g, g ^ 1) for g in range(size)]
    cross = [(g, (g + 1) % size if g % 2 else (g - 1) % size) for g in range(size)]
    along = [(g, (g + 2) % size if g % 2 else (g - 2) % size) for g in range(size)]
    up = [(g, (g + 2) % size) for g in range(size)]
    down = [(g, (g - 2) % size) for g in range(size)]
    f32, bf16 = jnp.float32, jnp.bfloat16
    rows = CHUNK * ny
    mats = call(
        functools.partial(lambda ring, ymat, zmat: matrices(ymat, zmat, ring), ny),
        (),
        [jax.ShapeDtypeStruct((rows, 3 * rows), bf16), jax.ShapeDtypeStruct((3 * nz, nz), bf16)],
        [],
        0.5,
        "matrices",
    )

    v = potential[None]
    v4 = jnp.where(m == 0, v[:, :4], v[:, n - 4 :])
    first = []
    for o in range(half):
        a = b = lax.dynamic_slice_in_dim(orbitals, half * (1 - m) + o, 1, 0)
        c = lax.dynamic_slice_in_dim(orbitals, half * m + o, 1, 0)
        if o == 0:
            a, b, c = jnp.concatenate([a, v], 1), jnp.concatenate([b, v4], 1), jnp.concatenate([c, v4], 1)
        ra = lax.ppermute(a, grid_axes, swap)
        rb = lax.ppermute(b, grid_axes, cross)
        rc = lax.ppermute(c, grid_axes, along)
        first.append((*mats, c, ra, rb, rc))

    def field(layers):
        return pltpu.VMEM((layers, ny, nz), f32)

    def products(layers):
        return pltpu.VMEM((layers // CHUNK, rows, nz), f32)

    second, v_above = [], None
    for o in range(half):
        outs = [(1, n + 4, ny, nz), (1, n, ny, nz), (1, 2 * n + 4, ny, nz)]
        scratch = [field(4 * n), field(2 * n + 8), products(2 * n + 8)]
        if o == 0:
            outs = [(1, 2 * n, ny, nz)] + outs[1:] + [(2 * n + 8, ny, nz)]
            lo, hi, y0, vext = call(first_two, first[o] + (potential,), outs, scratch, 1.0, "filter_1_2")
        else:
            lo, hi, y0 = call(first_two, first[o] + (vext,), outs, scratch, 10.0, "filter_1_2")
        rlo = lax.ppermute(hi, grid_axes, up)
        rhi = lax.ppermute(lo, grid_axes, down)
        v_above = rhi if o == 0 else v_above
        second.append((*mats, rlo, lo, hi, rhi, y0, vext, v_above))

    group = 2 * orbs
    per = 2 * n // group
    scratch = [pltpu.VMEM((2, 2 * n, ny, nz), f32), field(2 * n + 12), field(2 * n + 4), products(2 * n + 12)]
    outs = [(group, 2, per, ny, nz), (2, n, ny, nz)]
    results = call(last_three, second[0], outs, scratch, 1.5, "filter_3_4_hamiltonian")
    outs = [(half, n, ny, nz)] * 2 + [(half, 2, per, ny, nz)] * group
    results = call(last_three, (*second[1], *results), outs, scratch, 1.5, "filter_3_4_hamiltonian")
    keep, send, *blocks = results
    xs = [
        lax.ppermute(blocks[k], ("mem", "orb"), [(t, t ^ k) for t in range(group)]) if k else blocks[0] for k in PEERS
    ]
    (sums,) = call(
        gram,
        xs,
        [(size * orbs, 1, 2 * own_orbs * count)],
        [pltpu.VMEM((2, count, nz), f32)],
        1.3,
        "gram",
    )
    send, sums = lax.optimization_barrier((send, sums))
    back = lax.ppermute(send, grid_axes, swap)
    sums = lax.all_to_all(sums, ("pair", "mem", "orb"), 0, 0, tiled=True)
    filtered = jnp.where(m == 0, jnp.concatenate([keep, back]), jnp.concatenate([back, keep]))
    sums, filtered = lax.optimization_barrier((sums, filtered))
    corr, ham = call(
        functools.partial(finish, float(cells_x * ny * nz)), (sums,), [(own_orbs, count)] * 2, [], 0.3, "finish"
    )
    return filtered, corr, ham


def solution(mesh):
    devices = mesh.devices
    size, orbs = devices.shape
    fine = Mesh(devices.reshape(size // 2, 2, orbs), ("pair", "mem", "orb"))
    grid = ("pair", "mem")

    def whole(orbitals, potential):
        return jax.shard_map(
            functools.partial(per_device, orbitals.shape[1]),
            mesh=fine,
            in_specs=(P("orb", grid, None, None), P(grid, None, None)),
            out_specs=(P("orb", grid, None, None), P("orb", None), P("orb", None)),
            check_vma=False,
        )(orbitals, potential)

    return whole
```

```python
import functools

import jax
import jax.numpy as jnp
from jax import lax
from jax.experimental import pallas as pl
from jax.experimental.pallas import tpu as pltpu
from jax.sharding import Mesh, PartitionSpec as P

COEFS = (-205.0 / 72.0, 8.0 / 5.0, -1.0 / 5.0, 8.0 / 315.0, -1.0 / 560.0)
SCALE = 5040.0
WHOLE = (8064.0, -1008.0, 128.0, -9.0)
LOWER = -1.0
CUT = 4.0
UPPER = 10.0
HALF = (UPPER - CUT) / 2.0
CENTRE = (UPPER + CUT) / 2.0
S1 = HALF / (LOWER - CENTRE)
T2 = 2.0 / S1**2 - 1.0
T4 = 2.0 * T2 * T2 - 1.0
PEERS = (1, 6, 7, 4, 2, 5, 3, 0)
CHUNK = 4


def ring_matrix(rows, cols, ring):
    row = lax.broadcasted_iota(jnp.int32, (rows, cols), 0)
    col = lax.broadcasted_iota(jnp.int32, (rows, cols), 1)
    size = min(rows, cols)
    row, col = lax.rem(row, size), lax.rem(col, size)
    gap = jnp.abs(row - col)
    out = jnp.zeros((rows, cols), jnp.float32)
    for k, value in enumerate(WHOLE, 1):
        out = jnp.where((gap == k) | (gap == ring - k), value, out)
    return jnp.where(row // ring == col // ring, out, 0.0).astype(jnp.bfloat16)


def matrices(ymat, zmat, ring):
    ymat[...] = ring_matrix(*ymat.shape, ring)
    zmat[...] = ring_matrix(*zmat.shape, zmat.shape[1])


def sweep(at, count, v_at, gain, centre, emit, mats, yz, one_sided=False):
    ymat, zmat = mats
    ny, nz = ymat.shape[0] // CHUNK, zmat.shape[1]
    share = 0.5 * gain if one_sided else gain

    def along_yz(c):
        f = jnp.concatenate([at(c + j, slice(0, ny)) for j in range(CHUNK)], axis=0)
        high = f.astype(jnp.bfloat16)
        rest = f - high.astype(jnp.float32)
        mid = rest.astype(jnp.bfloat16)
        low = (rest - mid.astype(jnp.float32)).astype(jnp.bfloat16)
        z = jnp.dot(jnp.concatenate([high, mid, low], axis=1), zmat[...], preferred_element_type=jnp.float32)
        y = jnp.dot(ymat[...], jnp.concatenate([high, mid, low], axis=0), preferred_element_type=jnp.float32)
        yz[c // CHUNK] = y + z

    along_yz(0)
    for c in range(0, count, CHUNK):
        if c + CHUNK < count:
            along_yz(c + CHUNK)
        for r in range(0, ny, 8):
            rows = slice(r, r + 8)
            f = {i: at(i, rows) for i in range(c if one_sided else c - 4, c + CHUNK + 4)}
            for j in range(CHUNK):
                i = c + j
                total = (share * v_at(i, rows) + share * (-1.5 * COEFS[0] - centre)) * f[i]
                total = total + (-0.5 * share / SCALE) * yz[c // CHUNK, j * ny + r : j * ny + r + 8, :]
                for k in range(1, 5):
                    if one_sided:
                        total = total + (-0.5 * gain * COEFS[k]) * f[i + k]
                    else:
                        total = total + (-0.5 * gain * COEFS[k]) * (f[i - k] + f[i + k])
                emit(i, rows, total)


def places():
    m, place = lax.axis_index("mem"), lax.axis_index("orb")
    return m, place, m * lax.axis_size("orb") + place


def first_two(ymat, zmat, mine, ra, rb, rc, *refs):
    m = places()[0]
    mats = (ymat, zmat)
    n = rc.shape[1] if len(refs) == 7 else refs[0].shape[0]
    own, blocks = n + n * m, ((ra, 2 * n - n * m), (rb, 3 * n * m), (rc, 3 * n - 3 * n * m))
    if len(refs) == 7:
        v, lo_ref, hi_ref, y0_ref, y0, w, yz = refs
    else:
        potential, lo_ref, hi_ref, y0_ref, v, y0, w, yz = refs
        v[pl.ds(4 + n * m, n)] = potential[...]
        v[pl.ds(4 + n - n * m, n)] = ra[0, n:]
        v[pl.ds((2 * n + 4) * m, 4)] = rb[0, n:]
        v[pl.ds((2 * n + 4) * (1 - m), 4)] = rc[0, n:]
        lo_ref[0, n + 4 :] = v[8 : 4 + n]
    y0[pl.ds(own, n)] = mine[0, :n]
    for ref, at in blocks:
        y0[pl.ds(at, n)] = ref[0, :n]
    y0_ref[0] = y0[n : 3 * n + 4]

    def one(i, rows, total):
        w[i, rows, :] = total

    sweep(lambda i, r: y0[4 + i, r, :], 2 * n + 8, lambda i, r: v[i, r, :], 1.0 / HALF, CENTRE, one, mats, yz)

    def two(i, rows, total):
        y2 = total - (1.0 / T2) * y0[n + i, rows, :]
        if i < n + 4:
            lo_ref[0, i, rows, :] = y2
        if i >= n:
            hi_ref[0, i - n, rows, :] = y2

    sweep(
        lambda i, r: w[4 + i, r, :], 2 * n, lambda i, r: v[4 + i, r, :], 2.0 / (T2 * HALF), CENTRE, two, mats, yz
    )


def last_three(ymat, zmat, rlo, lo, hi, rhi, y0, v, v_above, *refs):
    outs, (both, u, f, yz) = refs[:-4], refs[-4:]
    mats = (ymat, zmat)
    n = hi.shape[1]

    def y2(i, rows):
        for ref, start in ((rlo, -n), (lo, 0), (hi, n)):
            if i < start + n:
                return ref[0, i - start, rows, :]
        return rhi[0, i - 2 * n, rows, :]

    def three(i, rows, total):
        u[i, rows, :] = total

    def v_at(i, rows):
        return v[i + 4, rows, :] if i < 2 * n + 4 else v_above[0, i - n, rows, :]

    sweep(lambda i, r: y2(i - 4, r), 2 * n + 12, lambda i, r: v_at(i - 4, r), 1.0 / HALF, CENTRE, three, mats, yz)

    def four(i, rows, total):
        f[i, rows, :] = total - (2.0 * T2 / T4) * y2(i, rows) - (1.0 / T4) * y0[0, i, rows, :]

    sweep(lambda i, r: u[4 + i, r, :], 2 * n + 4, v_at, 4.0 * T2 / (T4 * HALF), CENTRE, four, mats, yz)

    def five(i, rows, total):
        both[0, i, rows, :] = f[i, rows, :]
        both[1, i, rows, :] = total

    sweep(lambda i, r: f[i, r, :], 2 * n, v_at, 1.0, 0.0, five, mats, yz, one_sided=True)
    m, _, me = places()
    homes = (n * m, n - n * m)

    def cells(which, k, per):
        return both[which, pl.ds(per * jnp.bitwise_xor(me, k), per)]

    if len(outs) == 3:
        blocks, keep, to_y = outs
        per = blocks.shape[2]
        for k in range(blocks.shape[0]):
            for which in range(2):
                blocks[k, which] = cells(which, k, per)
        keep[...] = both[0, pl.ds(homes[0], n)]
        to_y[:n] = both[0, pl.ds(homes[1], n)]
        to_y[n:] = cells(1, 4, per)
    else:
        blocks_a, keep_a, keep, *blocks = outs
        per = blocks_a.shape[2]
        keep[0] = keep_a[...]
        keep[1] = both[0, pl.ds(homes[0], n)]
        for k, block in enumerate(blocks):
            if k == 4:
                block[:n] = both[0, pl.ds(homes[1], n)]
                block[n:] = cells(1, k, per)
            else:
                block[0] = blocks_a[k]
                for which in range(2):
                    block[1, which] = cells(which, k, per)


def gram(*refs):
    *xs, out_ref, part, from_y = refs
    orbs = part.shape[1]
    half, _, per, ny, nz = from_y.shape
    at_y = PEERS.index(4)
    n = xs[at_y].shape[0] - per
    for o, x in enumerate(xs[at_y : at_y + 2]):
        from_y[o, 0] = x[pl.ds(per * places()[1], per)]
        from_y[o, 1] = x[n:]
    xs[at_y : at_y + 2] = [from_y]
    rows = per * ny // 2
    each = 4 * half
    size = len(xs) * each
    flat = [x.reshape(each * rows, nz) for x in xs]
    fields = jnp.concatenate(
        [
            jnp.concatenate([x[pl.ds(r, each, stride=rows), :] for x in flat], axis=0)
            for r in range(rows)
        ],
        axis=1,
    )

    def product(a, b, contract):
        return lax.dot_general(
            a, b, ((contract[:1], contract[1:]), ((), ())),
            precision=lax.Precision.HIGHEST, preferred_element_type=jnp.float32,
        )

    both = product(fields, fields, (1, 1))
    row = lax.broadcasted_iota(jnp.int32, (size, size), 0)
    col = lax.broadcasted_iota(jnp.int32, (size, size), 1)
    both = jnp.where(row % 2 == col % 2, both, 0.0)
    col = lax.broadcasted_iota(jnp.int32, (2 * orbs, size), 1)
    which_peer = col // each
    peer = jnp.zeros_like(col)
    for i, k in enumerate(PEERS):
        peer = jnp.where(which_peer == i, k, peer)
    peer = jnp.bitwise_xor(peer, places()[2])
    target = orbs * (col // 2 % 2) + 2 * half * (peer % 4) + half * (peer // 4) + col // 4 % half
    order = (lax.broadcasted_iota(jnp.int32, (2 * orbs, size), 0) == target).astype(jnp.float32)
    both = product(order, product(both, order, (1, 1)), (1, 0))
    part[...] = jnp.zeros_like(part)
    part[0, :, :orbs] = both[:orbs, :orbs]
    part[1, :, :orbs] = both[orbs:, :orbs] + both[:orbs, orbs:]
    own = nz // (2 * orbs)
    groups = orbs // own
    packed = part[0, pl.ds(0, groups, stride=own), :]
    for i in range(1, 2 * own):
        packed = packed + pltpu.roll(part[i // own, pl.ds(i % own, groups, stride=own), :], i * orbs, 1)

    def spread(g, _):
        out_ref[pl.ds(g * groups, groups)] = packed.reshape(groups, 1, nz)
        return 0

    lax.fori_loop(0, out_ref.shape[0] // groups, spread, 0)


def finish(cells, x_ref, c_ref, h_ref):
    sums = jnp.sum(x_ref[...], axis=0) * (1.0 / cells)
    own, count = c_ref.shape
    nz = sums.shape[1]
    for r in range(own):
        c_ref[r : r + 1, :] = pltpu.roll(sums, (nz - r * count) % nz, 1)[:, :count]
        h_ref[r : r + 1, :] = pltpu.roll(sums, (nz - (own + r) * count) % nz, 1)[:, :count]


VMEM = pl.BlockSpec(memory_space=pltpu.VMEM)


def call(body, operands, outs, scratch, us, name):
    return pl.pallas_call(
        body,
        out_shape=[s if isinstance(s, jax.ShapeDtypeStruct) else jax.ShapeDtypeStruct(s, jnp.float32) for s in outs],
        in_specs=[VMEM] * len(operands),
        out_specs=[VMEM] * len(outs),
        scratch_shapes=scratch,
        cost_estimate=pl.CostEstimate(flops=int(us * 1e9), bytes_accessed=int(us * 3.5e6), transcendentals=0),
        compiler_params=pltpu.CompilerParams(vmem_limit_bytes=32 << 20),
        name=name,
    )(*operands)


def per_device(cells_x, orbitals, potential):
    pairs, orbs = lax.axis_size("pair"), lax.axis_size("orb")
    size = 2 * pairs
    grid_axes = ("pair", "mem")
    m = lax.axis_index("mem")
    own_orbs, n, ny, nz = orbitals.shape
    half = own_orbs // 2
    count = orbs * own_orbs
    swap = [(g, g ^ 1) for g in range(size)]
    cross = [(g, (g + 1) % size if g % 2 else (g - 1) % size) for g in range(size)]
    along = [(g, (g + 2) % size if g % 2 else (g - 2) % size) for g in range(size)]
    up = [(g, (g + 2) % size) for g in range(size)]
    down = [(g, (g - 2) % size) for g in range(size)]
    f32, bf16 = jnp.float32, jnp.bfloat16
    rows = CHUNK * ny
    mats = call(
        functools.partial(lambda ring, ymat, zmat: matrices(ymat, zmat, ring), ny),
        (),
        [jax.ShapeDtypeStruct((rows, 3 * rows), bf16), jax.ShapeDtypeStruct((3 * nz, nz), bf16)],
        [],
        0.5,
        "matrices",
    )

    v = potential[None]
    v4 = jnp.where(m == 0, v[:, :4], v[:, n - 4 :])
    first = []
    for o in range(half):
        a = b = lax.dynamic_slice_in_dim(orbitals, half * (1 - m) + o, 1, 0)
        c = lax.dynamic_slice_in_dim(orbitals, half * m + o, 1, 0)
        if o == 0:
            a, b, c = jnp.concatenate([a, v], 1), jnp.concatenate([b, v4], 1), jnp.concatenate([c, v4], 1)
        ra = lax.ppermute(a, grid_axes, swap)
        rb = lax.ppermute(b, grid_axes, cross)
        rc = lax.ppermute(c, grid_axes, along)
        first.append((*mats, c, ra, rb, rc))

    def field(layers):
        return pltpu.VMEM((layers, ny, nz), f32)

    def products(layers):
        return pltpu.VMEM((layers // CHUNK, rows, nz), f32)

    second, v_above = [], None
    for o in range(half):
        outs = [(1, n + 4, ny, nz), (1, n, ny, nz), (1, 2 * n + 4, ny, nz)]
        scratch = [field(4 * n), field(2 * n + 8), products(2 * n + 8)]
        if o == 0:
            outs = [(1, 2 * n, ny, nz)] + outs[1:] + [(2 * n + 8, ny, nz)]
            lo, hi, y0, vext = call(first_two, first[o] + (potential,), outs, scratch, 1.0, "filter_1_2")
        else:
            lo, hi, y0 = call(first_two, first[o] + (vext,), outs, scratch, 10.0, "filter_1_2")
        rlo = lax.ppermute(hi, grid_axes, up)
        rhi = lax.ppermute(lo, grid_axes, down)
        v_above = rhi if o == 0 else v_above
        second.append((*mats, rlo, lo, hi, rhi, y0, vext, v_above))

    group = 2 * orbs
    per = 2 * n // group
    scratch = [pltpu.VMEM((2, 2 * n, ny, nz), f32), field(2 * n + 12), field(2 * n + 4), products(2 * n + 12)]

    def peer(x, k):
        return lax.ppermute(x, ("mem", "orb"), [(t, t ^ k) for t in range(group)]) if k else x

    outs = [(group, 2, per, ny, nz), (n, ny, nz), (n + per, ny, nz)]
    blocks_a, keep, to_y = call(last_three, second[0], outs, scratch, 1.5, "filter_3_4_hamiltonian")
    y_a = peer(to_y, 4)
    shapes = [(half, 2, per, ny, nz)] * group
    shapes[4] = (n + per, ny, nz)
    keep, *blocks = call(
        last_three,
        (*second[1], blocks_a, keep),
        [(half, n, ny, nz)] + shapes,
        scratch,
        1.5,
        "filter_3_4_hamiltonian",
    )
    blocks[4], y_a = lax.optimization_barrier((blocks[4], y_a))
    xs = [peer(blocks[k], k) for k in PEERS]
    y_b = xs[PEERS.index(4)]
    xs.insert(PEERS.index(4), y_a)
    back = jnp.stack([y_a[:n], y_b[:n]])
    (sums,) = call(
        gram,
        xs,
        [(size * orbs, 1, 2 * own_orbs * count)],
        [pltpu.VMEM((2, count, nz), f32), pltpu.VMEM((half, 2, per, ny, nz), f32)],
        1.3,
        "gram",
    )
    sums = lax.all_to_all(sums, ("pair", "mem", "orb"), 0, 0, tiled=True)
    filtered = jnp.where(m == 0, jnp.concatenate([keep, back]), jnp.concatenate([back, keep]))
    sums, filtered = lax.optimization_barrier((sums, filtered))
    corr, ham = call(
        functools.partial(finish, float(cells_x * ny * nz)), (sums,), [(own_orbs, count)] * 2, [], 0.3, "finish"
    )
    return filtered, corr, ham


def solution(mesh):
    devices = mesh.devices
    size, orbs = devices.shape
    fine = Mesh(devices.reshape(size // 2, 2, orbs), ("pair", "mem", "orb"))
    grid = ("pair", "mem")

    def whole(orbitals, potential):
        return jax.shard_map(
            functools.partial(per_device, orbitals.shape[1]),
            mesh=fine,
            in_specs=(P("orb", grid, None, None), P(grid, None, None)),
            out_specs=(P("orb", grid, None, None), P("orb", None), P("orb", None)),
            check_vma=False,
        )(orbitals, potential)

    return whole
```

```python
import functools

import jax
import jax.numpy as jnp
from jax import lax
from jax.experimental import pallas as pl
from jax.experimental.pallas import tpu as pltpu
from jax.sharding import Mesh, PartitionSpec as P

COEFS = (-205.0 / 72.0, 8.0 / 5.0, -1.0 / 5.0, 8.0 / 315.0, -1.0 / 560.0)
SCALE = 5040.0
WHOLE = (8064.0, -1008.0, 128.0, -9.0)
LOWER = -1.0
CUT = 4.0
UPPER = 10.0
HALF = (UPPER - CUT) / 2.0
CENTRE = (UPPER + CUT) / 2.0
S1 = HALF / (LOWER - CENTRE)
T2 = 2.0 / S1**2 - 1.0
T4 = 2.0 * T2 * T2 - 1.0
PEERS = (6, 7, 4, 5, 2, 3, 1, 0)
CHUNK = 4


def ring_matrix(rows, cols, ring):
    row = lax.broadcasted_iota(jnp.int32, (rows, cols), 0)
    col = lax.broadcasted_iota(jnp.int32, (rows, cols), 1)
    size = min(rows, cols)
    row, col = lax.rem(row, size), lax.rem(col, size)
    gap = jnp.abs(row - col)
    out = jnp.zeros((rows, cols), jnp.float32)
    for k, value in enumerate(WHOLE, 1):
        out = jnp.where((gap == k) | (gap == ring - k), value, out)
    return jnp.where(row // ring == col // ring, out, 0.0).astype(jnp.bfloat16)


def matrices(ymat, zmat, ring):
    ymat[...] = ring_matrix(*ymat.shape, ring)
    zmat[...] = ring_matrix(*zmat.shape, zmat.shape[1])


def sweep(at, count, v_at, gain, centre, emit, mats, yz, one_sided=False):
    ymat, zmat = mats
    ny, nz = ymat.shape[0] // CHUNK, zmat.shape[1]
    share = 0.5 * gain if one_sided else gain

    def along_yz(c):
        f = jnp.concatenate([at(c + j, slice(0, ny)) for j in range(CHUNK)], axis=0)
        high = f.astype(jnp.bfloat16)
        rest = f - high.astype(jnp.float32)
        mid = rest.astype(jnp.bfloat16)
        low = (rest - mid.astype(jnp.float32)).astype(jnp.bfloat16)
        z = jnp.dot(jnp.concatenate([high, mid, low], axis=1), zmat[...], preferred_element_type=jnp.float32)
        y = jnp.dot(ymat[...], jnp.concatenate([high, mid, low], axis=0), preferred_element_type=jnp.float32)
        yz[c // CHUNK] = y + z

    along_yz(0)
    for c in range(0, count, CHUNK):
        if c + CHUNK < count:
            along_yz(c + CHUNK)
        for r in range(0, ny, 8):
            rows = slice(r, r + 8)
            f = {i: at(i, rows) for i in range(c if one_sided else c - 4, c + CHUNK + 4)}
            for j in range(CHUNK):
                i = c + j
                total = (share * v_at(i, rows) + share * (-1.5 * COEFS[0] - centre)) * f[i]
                total = total + (-0.5 * share / SCALE) * yz[c // CHUNK, j * ny + r : j * ny + r + 8, :]
                for k in range(1, 5):
                    if one_sided:
                        total = total + (-0.5 * gain * COEFS[k]) * f[i + k]
                    else:
                        total = total + (-0.5 * gain * COEFS[k]) * (f[i - k] + f[i + k])
                emit(i, rows, total)


def places():
    m, place = lax.axis_index("mem"), lax.axis_index("orb")
    return m, place, m * lax.axis_size("orb") + place


def first_two(ymat, zmat, mine, ra, rb, rc, *refs):
    m = places()[0]
    mats = (ymat, zmat)
    n = rc.shape[1] if len(refs) == 7 else refs[0].shape[0]
    own, blocks = n + n * m, ((ra, 2 * n - n * m), (rb, 3 * n * m), (rc, 3 * n - 3 * n * m))
    if len(refs) == 7:
        v, lo_ref, hi_ref, y0_ref, y0, w, yz = refs
    else:
        potential, lo_ref, hi_ref, y0_ref, v, y0, w, yz = refs
        v[pl.ds(4 + n * m, n)] = potential[...]
        v[pl.ds(4 + n - n * m, n)] = ra[0, n:]
        v[pl.ds((2 * n + 4) * m, 4)] = rb[0, n:]
        v[pl.ds((2 * n + 4) * (1 - m), 4)] = rc[0, n:]
        lo_ref[0, n + 4 :] = v[8 : 4 + n]
    y0[pl.ds(own, n)] = mine[0, :n]
    for ref, at in blocks:
        y0[pl.ds(at, n)] = ref[0, :n]
    y0_ref[0] = y0[n : 3 * n + 4]

    def one(i, rows, total):
        w[i, rows, :] = total

    sweep(lambda i, r: y0[4 + i, r, :], 2 * n + 8, lambda i, r: v[i, r, :], 1.0 / HALF, CENTRE, one, mats, yz)

    def two(i, rows, total):
        y2 = total - (1.0 / T2) * y0[n + i, rows, :]
        if i < n + 4:
            lo_ref[0, i, rows, :] = y2
        if i >= n:
            hi_ref[0, i - n, rows, :] = y2

    sweep(
        lambda i, r: w[4 + i, r, :], 2 * n, lambda i, r: v[4 + i, r, :], 2.0 / (T2 * HALF), CENTRE, two, mats, yz
    )


def last_three(ymat, zmat, rlo, lo, hi, rhi, y0, v, v_above, *refs):
    outs, (both, u, f, yz) = refs[:-4], refs[-4:]
    mats = (ymat, zmat)
    n = hi.shape[1]

    def y2(i, rows):
        for ref, start in ((rlo, -n), (lo, 0), (hi, n)):
            if i < start + n:
                return ref[0, i - start, rows, :]
        return rhi[0, i - 2 * n, rows, :]

    def three(i, rows, total):
        u[i, rows, :] = total

    def v_at(i, rows):
        return v[i + 4, rows, :] if i < 2 * n + 4 else v_above[0, i - n, rows, :]

    sweep(lambda i, r: y2(i - 4, r), 2 * n + 12, lambda i, r: v_at(i - 4, r), 1.0 / HALF, CENTRE, three, mats, yz)

    def four(i, rows, total):
        f[i, rows, :] = total - (2.0 * T2 / T4) * y2(i, rows) - (1.0 / T4) * y0[0, i, rows, :]

    sweep(lambda i, r: u[4 + i, r, :], 2 * n + 4, v_at, 4.0 * T2 / (T4 * HALF), CENTRE, four, mats, yz)

    def five(i, rows, total):
        both[0, i, rows, :] = f[i, rows, :]
        both[1, i, rows, :] = total

    sweep(lambda i, r: f[i, r, :], 2 * n, v_at, 1.0, 0.0, five, mats, yz, one_sided=True)
    m, _, me = places()
    homes = (n * m, n - n * m)

    def cells(which, k, per):
        return both[which, pl.ds(per * jnp.bitwise_xor(me, k), per)]

    keep, *outs = outs
    keep[...] = both[0, pl.ds(homes[0], n)]
    if len(outs) == 2:
        blocks, send = outs
        per = blocks.shape[2]
        for t in range(blocks.shape[0]):
            blocks[t] = both[:, per * t : per * (t + 1)]
        send[...] = both[0, pl.ds(homes[1], n)]
    else:
        per = outs[0].shape[1]
        for k, block in enumerate(outs):
            if k == 4:
                block[:n] = both[0, pl.ds(homes[1], n)]
                block[n:] = cells(1, k, per)
            else:
                for which in range(2):
                    block[which] = cells(which, k, per)


def gram(first, *refs):
    *xs, out_ref, part, second = refs
    orbs = part.shape[1]
    peers, _, per, ny, nz = first.shape
    _, place, me = places()
    for k, x in zip(PEERS, xs):
        peer = jnp.bitwise_xor(me, k)
        if k == 4:
            second[peer, 0] = x[pl.ds(per * place, per)]
            second[peer, 1] = x[x.shape[0] - per :]
        else:
            second[peer] = x[...]
    rows = per * ny
    flat = [x.reshape(peers * 2 * rows, nz) for x in (first, second)]
    fields = jnp.concatenate(
        [
            jnp.concatenate(
                [x[pl.ds(which * rows + r, peers, stride=2 * rows), :] for which in range(2) for x in flat], axis=0
            )
            for r in range(rows)
        ],
        axis=1,
    )

    def product(a, b, contract):
        return lax.dot_general(
            a, b, ((contract[:1], contract[1:]), ((), ())),
            precision=lax.Precision.HIGHEST, preferred_element_type=jnp.float32,
        )

    both = product(fields, fields, (1, 1))
    both = jnp.concatenate([both[:orbs, :orbs], both[orbs:, :orbs] + both[:orbs, orbs:]], axis=0)
    row = lax.broadcasted_iota(jnp.int32, (orbs, orbs), 0)
    quarter = peers // 2
    target = 4 * (row % quarter) + 2 * (row // quarter % 2) + row // peers
    order = (lax.broadcasted_iota(jnp.int32, (orbs, orbs), 1) == target).astype(jnp.float32)
    both = product(both, order, (1, 0))
    part[...] = jnp.zeros_like(part)
    for which in range(2):
        part[which, :, :orbs] = both[which * orbs : (which + 1) * orbs]
    own = nz // (2 * orbs)
    packed = jnp.zeros((quarter, nz), jnp.float32)
    for i in range(2 * own):
        start = i % 2 * peers + i % own // 2 * quarter
        rolled = part[i // own, start : start + quarter, :]
        packed = packed + (pltpu.roll(rolled, i * orbs, 1) if i else rolled)

    def spread(g, _):
        out_ref[pl.ds(g * quarter, quarter)] = packed.reshape(quarter, 1, nz)
        return 0

    lax.fori_loop(0, out_ref.shape[0] // quarter, spread, 0)


def finish(cells, x_ref, c_ref, h_ref):
    sums = jnp.sum(x_ref[...], axis=0) * (1.0 / cells)
    own, count = c_ref.shape
    nz = sums.shape[1]
    for r in range(own):
        c_ref[r : r + 1, :] = pltpu.roll(sums, (nz - r * count) % nz, 1)[:, :count]
        h_ref[r : r + 1, :] = pltpu.roll(sums, (nz - (own + r) * count) % nz, 1)[:, :count]


VMEM = pl.BlockSpec(memory_space=pltpu.VMEM)


def call(body, operands, outs, scratch, us, name):
    return pl.pallas_call(
        body,
        out_shape=[s if isinstance(s, jax.ShapeDtypeStruct) else jax.ShapeDtypeStruct(s, jnp.float32) for s in outs],
        in_specs=[VMEM] * len(operands),
        out_specs=[VMEM] * len(outs),
        scratch_shapes=scratch,
        cost_estimate=pl.CostEstimate(flops=int(us * 1e9), bytes_accessed=int(us * 3.5e6), transcendentals=0),
        compiler_params=pltpu.CompilerParams(vmem_limit_bytes=32 << 20),
        name=name,
    )(*operands)


def per_device(cells_x, orbitals, potential):
    pairs, orbs = lax.axis_size("pair"), lax.axis_size("orb")
    size = 2 * pairs
    grid_axes = ("pair", "mem")
    m = lax.axis_index("mem")
    own_orbs, n, ny, nz = orbitals.shape
    half = own_orbs // 2
    count = orbs * own_orbs
    swap = [(g, g ^ 1) for g in range(size)]
    cross = [(g, (g + 1) % size if g % 2 else (g - 1) % size) for g in range(size)]
    along = [(g, (g + 2) % size if g % 2 else (g - 2) % size) for g in range(size)]
    up = [(g, (g + 2) % size) for g in range(size)]
    down = [(g, (g - 2) % size) for g in range(size)]
    f32, bf16 = jnp.float32, jnp.bfloat16
    rows = CHUNK * ny
    mats = call(
        functools.partial(lambda ring, ymat, zmat: matrices(ymat, zmat, ring), ny),
        (),
        [jax.ShapeDtypeStruct((rows, 3 * rows), bf16), jax.ShapeDtypeStruct((3 * nz, nz), bf16)],
        [],
        0.5,
        "matrices",
    )

    v = potential[None]
    v4 = jnp.where(m == 0, v[:, :4], v[:, n - 4 :])
    first = []
    for o in range(half):
        a = b = lax.dynamic_slice_in_dim(orbitals, half * (1 - m) + o, 1, 0)
        c = lax.dynamic_slice_in_dim(orbitals, half * m + o, 1, 0)
        if o == 0:
            a, b, c = jnp.concatenate([a, v], 1), jnp.concatenate([b, v4], 1), jnp.concatenate([c, v4], 1)
        ra = lax.ppermute(a, grid_axes, swap)
        rb = lax.ppermute(b, grid_axes, cross)
        rc = lax.ppermute(c, grid_axes, along)
        first.append((*mats, c, ra, rb, rc))

    def field(layers):
        return pltpu.VMEM((layers, ny, nz), f32)

    def products(layers):
        return pltpu.VMEM((layers // CHUNK, rows, nz), f32)

    second, v_above = [], None
    for o in range(half):
        outs = [(1, n + 4, ny, nz), (1, n, ny, nz), (1, 2 * n + 4, ny, nz)]
        scratch = [field(4 * n), field(2 * n + 8), products(2 * n + 8)]
        if o == 0:
            outs = [(1, 2 * n, ny, nz)] + outs[1:] + [(2 * n + 8, ny, nz)]
            lo, hi, y0, vext = call(first_two, first[o] + (potential,), outs, scratch, 1.0, "filter_1_2")
        else:
            lo, hi, y0 = call(first_two, first[o] + (vext,), outs, scratch, 10.0, "filter_1_2")
        rlo = lax.ppermute(hi, grid_axes, up)
        rhi = lax.ppermute(lo, grid_axes, down)
        v_above = rhi if o == 0 else v_above
        second.append((*mats, rlo, lo, hi, rhi, y0, vext, v_above))

    group = 2 * orbs
    per = 2 * n // group
    scratch = [pltpu.VMEM((2, 2 * n, ny, nz), f32), field(2 * n + 12), field(2 * n + 4), products(2 * n + 12)]

    def peer(x, k):
        return lax.ppermute(x, ("mem", "orb"), [(t, t ^ k) for t in range(group)]) if k else x

    block = (2, per, ny, nz)
    outs = [(n, ny, nz), (group, *block), (n, ny, nz)]
    keep_a, blocks, send = call(last_three, second[0], outs, scratch, 1.5, "filter_3_4_hamiltonian")
    first = lax.all_to_all(blocks, ("mem", "orb"), 0, 0, tiled=True)
    back_a = peer(send, 4)
    hi, _ = lax.optimization_barrier((second[1][4], keep_a))
    outs = [(n, ny, nz)] + [block] * 4 + [(n + per, ny, nz)] + [block] * 3
    keep_b, *blocks = call(
        last_three, (*second[1][:4], hi, *second[1][5:]), outs, scratch, 1.5, "filter_3_4_hamiltonian"
    )
    blocks[1], first = lax.optimization_barrier((blocks[1], first))
    xs = [peer(blocks[k], k) for k in PEERS]
    back_b = xs[PEERS.index(4)][:n]
    (sums,) = call(
        gram,
        (first, *xs),
        [(size * orbs, 1, 2 * own_orbs * count)],
        [pltpu.VMEM((2, count, nz), f32), pltpu.VMEM((group, *block), f32)],
        1.3,
        "gram",
    )
    sums = lax.all_to_all(sums, ("pair", "mem", "orb"), 0, 0, tiled=True)
    keep, back = jnp.stack([keep_a, keep_b]), jnp.stack([back_a, back_b])
    filtered = jnp.where(m == 0, jnp.concatenate([keep, back]), jnp.concatenate([back, keep]))
    sums, filtered = lax.optimization_barrier((sums, filtered))
    corr, ham = call(
        functools.partial(finish, float(cells_x * ny * nz)), (sums,), [(own_orbs, count)] * 2, [], 0.3, "finish"
    )
    return filtered, corr, ham


def solution(mesh):
    devices = mesh.devices
    size, orbs = devices.shape
    fine = Mesh(devices.reshape(size // 2, 2, orbs), ("pair", "mem", "orb"))
    grid = ("pair", "mem")

    def whole(orbitals, potential):
        return jax.shard_map(
            functools.partial(per_device, orbitals.shape[1]),
            mesh=fine,
            in_specs=(P("orb", grid, None, None), P(grid, None, None)),
            out_specs=(P("orb", grid, None, None), P("orb", None), P("orb", None)),
            check_vma=False,
        )(orbitals, potential)

    return whole
```

```python
import functools

import jax
import jax.numpy as jnp
from jax import lax
from jax.experimental import pallas as pl
from jax.experimental.pallas import tpu as pltpu
from jax.sharding import Mesh, PartitionSpec as P

COEFS = (-205.0 / 72.0, 8.0 / 5.0, -1.0 / 5.0, 8.0 / 315.0, -1.0 / 560.0)
SCALE = 5040.0
WHOLE = (8064.0, -1008.0, 128.0, -9.0)
LOWER = -1.0
CUT = 4.0
UPPER = 10.0
HALF = (UPPER - CUT) / 2.0
CENTRE = (UPPER + CUT) / 2.0
S1 = HALF / (LOWER - CENTRE)
T2 = 2.0 / S1**2 - 1.0
T4 = 2.0 * T2 * T2 - 1.0
PEERS = (6, 4, 2, 7, 5, 3, 1, 0)
CHUNK = 4


def ring_matrix(rows, cols, ring):
    row = lax.broadcasted_iota(jnp.int32, (rows, cols), 0)
    col = lax.broadcasted_iota(jnp.int32, (rows, cols), 1)
    size = min(rows, cols)
    row, col = lax.rem(row, size), lax.rem(col, size)
    gap = jnp.abs(row - col)
    out = jnp.zeros((rows, cols), jnp.float32)
    for k, value in enumerate(WHOLE, 1):
        out = jnp.where((gap == k) | (gap == ring - k), value, out)
    return jnp.where(row // ring == col // ring, out, 0.0).astype(jnp.bfloat16)


def matrices(ymat, zmat, ring):
    ymat[...] = ring_matrix(*ymat.shape, ring)
    zmat[...] = ring_matrix(*zmat.shape, zmat.shape[1])


def sweep(at, count, v_at, gain, centre, emit, mats, yz, one_sided=False):
    ymat, zmat = mats
    ny, nz = ymat.shape[0] // CHUNK, zmat.shape[1]
    share = 0.5 * gain if one_sided else gain

    def along_yz(c):
        f = jnp.concatenate([at(c + j, slice(0, ny)) for j in range(CHUNK)], axis=0)
        high = f.astype(jnp.bfloat16)
        rest = f - high.astype(jnp.float32)
        mid = rest.astype(jnp.bfloat16)
        low = (rest - mid.astype(jnp.float32)).astype(jnp.bfloat16)
        z = jnp.dot(jnp.concatenate([high, mid, low], axis=1), zmat[...], preferred_element_type=jnp.float32)
        y = jnp.dot(ymat[...], jnp.concatenate([high, mid, low], axis=0), preferred_element_type=jnp.float32)
        yz[c // CHUNK] = y + z

    along_yz(0)
    for c in range(0, count, CHUNK):
        if c + CHUNK < count:
            along_yz(c + CHUNK)
        for r in range(0, ny, 8):
            rows = slice(r, r + 8)
            f = {i: at(i, rows) for i in range(c if one_sided else c - 4, c + CHUNK + 4)}
            for j in range(CHUNK):
                i = c + j
                total = (share * v_at(i, rows) + share * (-1.5 * COEFS[0] - centre)) * f[i]
                total = total + (-0.5 * share / SCALE) * yz[c // CHUNK, j * ny + r : j * ny + r + 8, :]
                for k in range(1, 5):
                    if one_sided:
                        total = total + (-0.5 * gain * COEFS[k]) * f[i + k]
                    else:
                        total = total + (-0.5 * gain * COEFS[k]) * (f[i - k] + f[i + k])
                emit(i, rows, total)


def places():
    m, place = lax.axis_index("mem"), lax.axis_index("orb")
    return m, place, m * lax.axis_size("orb") + place


def first_two(ymat, zmat, mine, ra, rb, rc, *refs):
    m = places()[0]
    mats = (ymat, zmat)
    n = rc.shape[1] if len(refs) == 7 else refs[0].shape[0]
    own, blocks = n + n * m, ((ra, 2 * n - n * m), (rb, 3 * n * m), (rc, 3 * n - 3 * n * m))
    if len(refs) == 7:
        v, lo_ref, hi_ref, y0_ref, y0, w, yz = refs
    else:
        potential, lo_ref, hi_ref, y0_ref, v, y0, w, yz = refs
        v[pl.ds(4 + n * m, n)] = potential[...]
        v[pl.ds(4 + n - n * m, n)] = ra[0, n:]
        v[pl.ds((2 * n + 4) * m, 4)] = rb[0, n:]
        v[pl.ds((2 * n + 4) * (1 - m), 4)] = rc[0, n:]
        lo_ref[0, n + 4 :] = v[8 : 4 + n]
    y0[pl.ds(own, n)] = mine[0, :n]
    for ref, at in blocks:
        y0[pl.ds(at, n)] = ref[0, :n]
    y0_ref[0] = y0[n : 3 * n + 4]

    def one(i, rows, total):
        w[i, rows, :] = total

    sweep(lambda i, r: y0[4 + i, r, :], 2 * n + 8, lambda i, r: v[i, r, :], 1.0 / HALF, CENTRE, one, mats, yz)

    def two(i, rows, total):
        y2 = total - (1.0 / T2) * y0[n + i, rows, :]
        if i < n + 4:
            lo_ref[0, i, rows, :] = y2
        if i >= n:
            hi_ref[0, i - n, rows, :] = y2

    sweep(
        lambda i, r: w[4 + i, r, :], 2 * n, lambda i, r: v[4 + i, r, :], 2.0 / (T2 * HALF), CENTRE, two, mats, yz
    )


def last_three(ymat, zmat, rlo, lo, hi, rhi, y0, v, v_above, *refs):
    outs, (both, u, f, yz) = refs[:-4], refs[-4:]
    mats = (ymat, zmat)
    n = hi.shape[1]

    def y2(i, rows):
        for ref, start in ((rlo, -n), (lo, 0), (hi, n)):
            if i < start + n:
                return ref[0, i - start, rows, :]
        return rhi[0, i - 2 * n, rows, :]

    def three(i, rows, total):
        u[i, rows, :] = total

    def v_at(i, rows):
        return v[i + 4, rows, :] if i < 2 * n + 4 else v_above[0, i - n, rows, :]

    sweep(lambda i, r: y2(i - 4, r), 2 * n + 12, lambda i, r: v_at(i - 4, r), 1.0 / HALF, CENTRE, three, mats, yz)

    def four(i, rows, total):
        f[i, rows, :] = total - (2.0 * T2 / T4) * y2(i, rows) - (1.0 / T4) * y0[0, i, rows, :]

    sweep(lambda i, r: u[4 + i, r, :], 2 * n + 4, v_at, 4.0 * T2 / (T4 * HALF), CENTRE, four, mats, yz)

    def five(i, rows, total):
        both[0, i, rows, :] = f[i, rows, :]
        both[1, i, rows, :] = total

    sweep(lambda i, r: f[i, r, :], 2 * n, v_at, 1.0, 0.0, five, mats, yz, one_sided=True)
    m, _, me = places()
    homes = (n * m, n - n * m)

    def cells(which, k, per):
        return both[which, pl.ds(per * jnp.bitwise_xor(me, k), per)]

    if len(outs) == 2:
        home, blocks = outs
        for i, start in enumerate(homes):
            home[i] = both[0, pl.ds(start, n)]
        for i, k in enumerate(PEERS):
            for which in range(2):
                blocks[i, which] = cells(which, k, blocks.shape[2])
    else:
        home_a, blocks_a, keep, send, *blocks = outs
        for i, ref in enumerate((keep, send)):
            ref[0] = home_a[i]
            ref[1] = both[0, pl.ds(homes[i], n)]
        for i, (k, block) in enumerate(zip(PEERS, blocks)):
            block[0] = blocks_a[i]
            for which in range(2):
                block[1, which] = cells(which, k, block.shape[2])


def gram(*refs):
    *xs, out_ref, part, blocks = refs
    orbs = part.shape[1]
    half, peers, _, per, ny, nz = blocks.shape
    me = places()[2]
    for k, x in zip(PEERS, xs):
        for o in range(half):
            blocks[o, jnp.bitwise_xor(me, k)] = x[o]
    rows = per * ny
    flat = blocks.reshape(half * peers * 2 * rows, nz)
    fields = jnp.concatenate(
        [
            jnp.concatenate(
                [
                    flat[pl.ds((o * peers * 2 + which) * rows + r, peers, stride=2 * rows), :]
                    for which in range(2)
                    for o in range(half)
                ],
                axis=0,
            )
            for r in range(rows)
        ],
        axis=1,
    )
    high = fields.astype(jnp.bfloat16)
    rest = fields - high.astype(jnp.float32)
    mid = rest.astype(jnp.bfloat16)
    low = (rest - mid.astype(jnp.float32)).astype(jnp.bfloat16)
    terms = jnp.concatenate([high, mid, low], axis=0)
    products = lax.dot_general(terms, terms, (((1,), (1,)), ((), ())), preferred_element_type=jnp.float32)
    size = 2 * orbs
    both = jnp.zeros((size, size), jnp.float32)
    for i in (2, 1, 0):
        for j in (2, 1, 0):
            both = both + products[i * size : (i + 1) * size, j * size : (j + 1) * size]
    both = jnp.concatenate([both[:orbs, :orbs], both[orbs:, :orbs] + both[:orbs, orbs:]], axis=0)
    row = lax.broadcasted_iota(jnp.int32, (orbs, orbs), 0)
    quarter = peers // 2
    target = 4 * (row % quarter) + 2 * (row // quarter % 2) + row // peers
    order = (lax.broadcasted_iota(jnp.int32, (orbs, orbs), 1) == target).astype(jnp.float32)
    both = jnp.dot(both, order, precision=lax.Precision.HIGHEST, preferred_element_type=jnp.float32)
    part[...] = jnp.zeros_like(part)
    for which in range(2):
        part[which, :, :orbs] = both[which * orbs : (which + 1) * orbs]
    own = nz // (2 * orbs)
    packed = jnp.zeros((quarter, nz), jnp.float32)
    for i in range(2 * own):
        start = i % 2 * peers + i % own // 2 * quarter
        rolled = part[i // own, start : start + quarter, :]
        packed = packed + (pltpu.roll(rolled, i * orbs, 1) if i else rolled)

    for g in range(out_ref.shape[0] // quarter):
        out_ref[g * quarter : (g + 1) * quarter] = packed.reshape(quarter, 1, nz)


def finish(cells, x_ref, c_ref, h_ref):
    sums = jnp.sum(x_ref[...], axis=0) * (1.0 / cells)
    own, count = c_ref.shape
    nz = sums.shape[1]
    for r in range(own):
        c_ref[r : r + 1, :] = pltpu.roll(sums, (nz - r * count) % nz, 1)[:, :count]
        h_ref[r : r + 1, :] = pltpu.roll(sums, (nz - (own + r) * count) % nz, 1)[:, :count]


VMEM = pl.BlockSpec(memory_space=pltpu.VMEM)


def call(body, operands, outs, scratch, us, name):
    return pl.pallas_call(
        body,
        out_shape=[s if isinstance(s, jax.ShapeDtypeStruct) else jax.ShapeDtypeStruct(s, jnp.float32) for s in outs],
        in_specs=[VMEM] * len(operands),
        out_specs=[VMEM] * len(outs),
        scratch_shapes=scratch,
        cost_estimate=pl.CostEstimate(flops=int(us * 1e9), bytes_accessed=int(us * 3.5e6), transcendentals=0),
        compiler_params=pltpu.CompilerParams(vmem_limit_bytes=32 << 20),
        name=name,
    )(*operands)


def per_device(cells_x, orbitals, potential):
    pairs, orbs = lax.axis_size("pair"), lax.axis_size("orb")
    size = 2 * pairs
    grid_axes = ("pair", "mem")
    m = lax.axis_index("mem")
    own_orbs, n, ny, nz = orbitals.shape
    half = own_orbs // 2
    count = orbs * own_orbs
    swap = [(g, g ^ 1) for g in range(size)]
    cross = [(g, (g + 1) % size if g % 2 else (g - 1) % size) for g in range(size)]
    along = [(g, (g + 2) % size if g % 2 else (g - 2) % size) for g in range(size)]
    up = [(g, (g + 2) % size) for g in range(size)]
    down = [(g, (g - 2) % size) for g in range(size)]
    f32, bf16 = jnp.float32, jnp.bfloat16
    rows = CHUNK * ny
    mats = call(
        functools.partial(lambda ring, ymat, zmat: matrices(ymat, zmat, ring), ny),
        (),
        [jax.ShapeDtypeStruct((rows, 3 * rows), bf16), jax.ShapeDtypeStruct((3 * nz, nz), bf16)],
        [],
        0.5,
        "matrices",
    )

    v = potential[None]
    v4 = jnp.where(m == 0, v[:, :4], v[:, n - 4 :])
    first = []
    for o in range(half):
        a = b = lax.dynamic_slice_in_dim(orbitals, half * (1 - m) + o, 1, 0)
        c = lax.dynamic_slice_in_dim(orbitals, half * m + o, 1, 0)
        if o == 0:
            a, b, c = jnp.concatenate([a, v], 1), jnp.concatenate([b, v4], 1), jnp.concatenate([c, v4], 1)
        ra = lax.ppermute(a, grid_axes, swap)
        rb = lax.ppermute(b, grid_axes, cross)
        rc = lax.ppermute(c, grid_axes, along)
        first.append((*mats, c, ra, rb, rc))

    def field(layers):
        return pltpu.VMEM((layers, ny, nz), f32)

    def products(layers):
        return pltpu.VMEM((layers // CHUNK, rows, nz), f32)

    second, v_above = [], None
    for o in range(half):
        outs = [(1, n + 4, ny, nz), (1, n, ny, nz), (1, 2 * n + 4, ny, nz)]
        scratch = [field(4 * n), field(2 * n + 8), products(2 * n + 8)]
        if o == 0:
            outs = [(1, 2 * n, ny, nz)] + outs[1:] + [(2 * n + 8, ny, nz)]
            lo, hi, y0, vext = call(first_two, first[o] + (potential,), outs, scratch, 1.0, "filter_1_2")
        else:
            lo, hi, y0 = call(first_two, first[o] + (vext,), outs, scratch, 10.0, "filter_1_2")
        rlo = lax.ppermute(hi, grid_axes, up)
        rhi = lax.ppermute(lo, grid_axes, down)
        v_above = rhi if o == 0 else v_above
        second.append((*mats, rlo, lo, hi, rhi, y0, vext, v_above))

    group = 2 * orbs
    per = 2 * n // group
    scratch = [pltpu.VMEM((2, 2 * n, ny, nz), f32), field(2 * n + 12), field(2 * n + 4), products(2 * n + 12)]

    def peer(x, k):
        return lax.ppermute(x, ("mem", "orb"), [(t, t ^ k) for t in range(group)]) if k else x

    block = (2, per, ny, nz)
    results = call(last_three, second[0], [(2, n, ny, nz), (group, *block)], scratch, 1.5, "filter_3_4_hamiltonian")
    outs = [(half, n, ny, nz)] * 2 + [(half, *block)] * group
    keep, send, *blocks = call(last_three, (*second[1], *results), outs, scratch, 1.5, "filter_3_4_hamiltonian")
    xs = [peer(x, k) for k, x in zip(PEERS, blocks)]
    (sums,) = call(
        gram,
        xs,
        [(size * orbs, 1, 2 * own_orbs * count)],
        [pltpu.VMEM((2, count, nz), f32), pltpu.VMEM((half, group, *block), f32)],
        1.3,
        "gram",
    )
    send, sums = lax.optimization_barrier((send, sums))
    back = lax.ppermute(send, grid_axes, swap)
    sums = lax.all_to_all(sums, ("pair", "mem", "orb"), 0, 0, tiled=True)
    filtered = jnp.where(m == 0, jnp.concatenate([keep, back]), jnp.concatenate([back, keep]))
    sums, filtered = lax.optimization_barrier((sums, filtered))
    corr, ham = call(
        functools.partial(finish, float(cells_x * ny * nz)), (sums,), [(own_orbs, count)] * 2, [], 0.3, "finish"
    )
    return filtered, corr, ham


def solution(mesh):
    devices = mesh.devices
    size, orbs = devices.shape
    fine = Mesh(devices.reshape(size // 2, 2, orbs), ("pair", "mem", "orb"))
    grid = ("pair", "mem")

    def whole(orbitals, potential):
        return jax.shard_map(
            functools.partial(per_device, orbitals.shape[1]),
            mesh=fine,
            in_specs=(P("orb", grid, None, None), P(grid, None, None)),
            out_specs=(P("orb", grid, None, None), P("orb", None), P("orb", None)),
            check_vma=False,
        )(orbitals, potential)

    return whole
```

```python
import functools

import jax
import jax.numpy as jnp
from jax import lax
from jax.experimental import pallas as pl
from jax.experimental.pallas import tpu as pltpu
from jax.sharding import Mesh, PartitionSpec as P

COEFS = (-205.0 / 72.0, 8.0 / 5.0, -1.0 / 5.0, 8.0 / 315.0, -1.0 / 560.0)
SCALE = 5040.0
WHOLE = (8064.0, -1008.0, 128.0, -9.0)
LOWER = -1.0
CUT = 4.0
UPPER = 10.0
HALF = (UPPER - CUT) / 2.0
CENTRE = (UPPER + CUT) / 2.0
S1 = HALF / (LOWER - CENTRE)
T2 = 2.0 / S1**2 - 1.0
T4 = 2.0 * T2 * T2 - 1.0
EARLY = (6, 4, 2)
LATE = (7, 5, 3, 1, 0)
CHUNK = 4


def ring_matrix(rows, cols, ring):
    row = lax.broadcasted_iota(jnp.int32, (rows, cols), 0)
    col = lax.broadcasted_iota(jnp.int32, (rows, cols), 1)
    size = min(rows, cols)
    row, col = lax.rem(row, size), lax.rem(col, size)
    gap = jnp.abs(row - col)
    out = jnp.zeros((rows, cols), jnp.float32)
    for k, value in enumerate(WHOLE, 1):
        out = jnp.where((gap == k) | (gap == ring - k), value, out)
    return jnp.where(row // ring == col // ring, out, 0.0).astype(jnp.bfloat16)


def matrices(ymat, zmat, ring):
    ymat[...] = ring_matrix(*ymat.shape, ring)
    zmat[...] = ring_matrix(*zmat.shape, zmat.shape[1])


def sweep(at, count, v_at, gain, centre, emit, mats, yz, one_sided=False):
    ymat, zmat = mats
    ny, nz = ymat.shape[0] // CHUNK, zmat.shape[1]
    share = 0.5 * gain if one_sided else gain

    def along_yz(c):
        f = jnp.concatenate([at(c + j, slice(0, ny)) for j in range(CHUNK)], axis=0)
        high = f.astype(jnp.bfloat16)
        rest = f - high.astype(jnp.float32)
        mid = rest.astype(jnp.bfloat16)
        low = (rest - mid.astype(jnp.float32)).astype(jnp.bfloat16)
        z = jnp.dot(jnp.concatenate([high, mid, low], axis=1), zmat[...], preferred_element_type=jnp.float32)
        y = jnp.dot(ymat[...], jnp.concatenate([high, mid, low], axis=0), preferred_element_type=jnp.float32)
        yz[c // CHUNK] = y + z

    along_yz(0)
    for c in range(0, count, CHUNK):
        if c + CHUNK < count:
            along_yz(c + CHUNK)
        for r in range(0, ny, 8):
            rows = slice(r, r + 8)
            f = {i: at(i, rows) for i in range(c if one_sided else c - 4, c + CHUNK + 4)}
            for j in range(CHUNK):
                i = c + j
                total = (share * v_at(i, rows) + share * (-1.5 * COEFS[0] - centre)) * f[i]
                total = total + (-0.5 * share / SCALE) * yz[c // CHUNK, j * ny + r : j * ny + r + 8, :]
                for k in range(1, 5):
                    if one_sided:
                        total = total + (-0.5 * gain * COEFS[k]) * f[i + k]
                    else:
                        total = total + (-0.5 * gain * COEFS[k]) * (f[i - k] + f[i + k])
                emit(i, rows, total)


def places():
    m, place = lax.axis_index("mem"), lax.axis_index("orb")
    return m, place, m * lax.axis_size("orb") + place


def first_two(ymat, zmat, mine, ra, rb, rc, *refs):
    m = places()[0]
    mats = (ymat, zmat)
    n = rc.shape[1] if len(refs) == 7 else refs[0].shape[0]
    own, blocks = n + n * m, ((ra, 2 * n - n * m), (rb, 3 * n * m), (rc, 3 * n - 3 * n * m))
    if len(refs) == 7:
        v, lo_ref, hi_ref, y0_ref, y0, w, yz = refs
    else:
        potential, lo_ref, hi_ref, y0_ref, v, y0, w, yz = refs
        v[pl.ds(4 + n * m, n)] = potential[...]
        v[pl.ds(4 + n - n * m, n)] = ra[0, n:]
        v[pl.ds((2 * n + 4) * m, 4)] = rb[0, n:]
        v[pl.ds((2 * n + 4) * (1 - m), 4)] = rc[0, n:]
        lo_ref[0, n + 4 :] = v[8 : 4 + n]
    y0[pl.ds(own, n)] = mine[0, :n]
    for ref, at in blocks:
        y0[pl.ds(at, n)] = ref[0, :n]
    y0_ref[0] = y0[n : 3 * n + 4]

    def one(i, rows, total):
        w[i, rows, :] = total

    sweep(lambda i, r: y0[4 + i, r, :], 2 * n + 8, lambda i, r: v[i, r, :], 1.0 / HALF, CENTRE, one, mats, yz)

    def two(i, rows, total):
        y2 = total - (1.0 / T2) * y0[n + i, rows, :]
        if i < n + 4:
            lo_ref[0, i, rows, :] = y2
        if i >= n:
            hi_ref[0, i - n, rows, :] = y2

    sweep(
        lambda i, r: w[4 + i, r, :], 2 * n, lambda i, r: v[4 + i, r, :], 2.0 / (T2 * HALF), CENTRE, two, mats, yz
    )


def last_three(ymat, zmat, rlo, lo, hi, rhi, y0, v, v_above, *refs):
    outs, (both, u, f, yz) = refs[:-4], refs[-4:]
    mats = (ymat, zmat)
    n = hi.shape[1]

    def y2(i, rows):
        for ref, start in ((rlo, -n), (lo, 0), (hi, n)):
            if i < start + n:
                return ref[0, i - start, rows, :]
        return rhi[0, i - 2 * n, rows, :]

    def three(i, rows, total):
        u[i, rows, :] = total

    def v_at(i, rows):
        return v[i + 4, rows, :] if i < 2 * n + 4 else v_above[0, i - n, rows, :]

    sweep(lambda i, r: y2(i - 4, r), 2 * n + 12, lambda i, r: v_at(i - 4, r), 1.0 / HALF, CENTRE, three, mats, yz)

    def four(i, rows, total):
        f[i, rows, :] = total - (2.0 * T2 / T4) * y2(i, rows) - (1.0 / T4) * y0[0, i, rows, :]

    sweep(lambda i, r: u[4 + i, r, :], 2 * n + 4, v_at, 4.0 * T2 / (T4 * HALF), CENTRE, four, mats, yz)

    def five(i, rows, total):
        both[0, i, rows, :] = f[i, rows, :]
        both[1, i, rows, :] = total

    sweep(lambda i, r: f[i, r, :], 2 * n, v_at, 1.0, 0.0, five, mats, yz, one_sided=True)
    m, _, me = places()
    homes = (n * m, n - n * m)

    def cells(which, k, per):
        return both[which, pl.ds(per * jnp.bitwise_xor(me, k), per)]

    early = len(EARLY)
    if len(outs) == 2 + early:
        home, late, *blocks = outs
        for i, start in enumerate(homes):
            home[i] = both[0, pl.ds(start, n)]
        for i, k in enumerate(LATE):
            for which in range(2):
                late[i, which] = cells(which, k, late.shape[2])
    else:
        home_a, late_a, keep, send, *blocks = outs
        for i, ref in enumerate((keep, send)):
            ref[0] = home_a[i]
            ref[1] = both[0, pl.ds(homes[i], n)]
        for i, (k, block) in enumerate(zip(LATE, blocks[early:])):
            block[0] = late_a[i]
            for which in range(2):
                block[1, which] = cells(which, k, block.shape[2])
    for k, block in zip(EARLY, blocks):
        for which in range(2):
            block[which] = cells(which, k, block.shape[1])


def gram(*refs):
    *xs, out_ref, part, blocks = refs
    orbs = part.shape[1]
    half, peers, _, per, ny, nz = blocks.shape
    me = places()[2]
    early = len(EARLY)
    for o in range(half):
        for k, x in zip(EARLY, xs[early * o :]):
            blocks[o, jnp.bitwise_xor(me, k)] = x[...]
        for k, x in zip(LATE, xs[early * half :]):
            blocks[o, jnp.bitwise_xor(me, k)] = x[o]
    rows = per * ny
    flat = blocks.reshape(half * peers * 2 * rows, nz)
    fields = jnp.concatenate(
        [
            jnp.concatenate(
                [
                    flat[pl.ds((o * peers * 2 + which) * rows + r, peers, stride=2 * rows), :]
                    for which in range(2)
                    for o in range(half)
                ],
                axis=0,
            )
            for r in range(rows)
        ],
        axis=1,
    )
    high = fields.astype(jnp.bfloat16)
    rest = fields - high.astype(jnp.float32)
    mid = rest.astype(jnp.bfloat16)
    low = (rest - mid.astype(jnp.float32)).astype(jnp.bfloat16)
    terms = jnp.concatenate([high, mid, low], axis=0)
    products = lax.dot_general(terms, terms, (((1,), (1,)), ((), ())), preferred_element_type=jnp.float32)
    size = 2 * orbs
    both = jnp.zeros((size, size), jnp.float32)
    for i in (2, 1, 0):
        for j in (2, 1, 0):
            both = both + products[i * size : (i + 1) * size, j * size : (j + 1) * size]
    both = jnp.concatenate([both[:orbs, :orbs], both[orbs:, :orbs] + both[:orbs, orbs:]], axis=0)
    row = lax.broadcasted_iota(jnp.int32, (orbs, orbs), 0)
    quarter = peers // 2
    target = 4 * (row % quarter) + 2 * (row // quarter % 2) + row // peers
    order = (lax.broadcasted_iota(jnp.int32, (orbs, orbs), 1) == target).astype(jnp.float32)
    both = jnp.dot(both, order, precision=lax.Precision.HIGHEST, preferred_element_type=jnp.float32)
    part[...] = jnp.zeros_like(part)
    for which in range(2):
        part[which, :, :orbs] = both[which * orbs : (which + 1) * orbs]
    own = nz // (2 * orbs)
    packed = jnp.zeros((quarter, nz), jnp.float32)
    for i in range(2 * own):
        start = i % 2 * peers + i % own // 2 * quarter
        rolled = part[i // own, start : start + quarter, :]
        packed = packed + (pltpu.roll(rolled, i * orbs, 1) if i else rolled)

    for g in range(out_ref.shape[0] // quarter):
        out_ref[g * quarter : (g + 1) * quarter] = packed.reshape(quarter, 1, nz)


def finish(cells, x_ref, c_ref, h_ref):
    sums = jnp.sum(x_ref[...], axis=0) * (1.0 / cells)
    own, count = c_ref.shape
    nz = sums.shape[1]
    for r in range(own):
        c_ref[r : r + 1, :] = pltpu.roll(sums, (nz - r * count) % nz, 1)[:, :count]
        h_ref[r : r + 1, :] = pltpu.roll(sums, (nz - (own + r) * count) % nz, 1)[:, :count]


VMEM = pl.BlockSpec(memory_space=pltpu.VMEM)


def call(body, operands, outs, scratch, us, name):
    return pl.pallas_call(
        body,
        out_shape=[s if isinstance(s, jax.ShapeDtypeStruct) else jax.ShapeDtypeStruct(s, jnp.float32) for s in outs],
        in_specs=[VMEM] * len(operands),
        out_specs=[VMEM] * len(outs),
        scratch_shapes=scratch,
        cost_estimate=pl.CostEstimate(flops=int(us * 1e9), bytes_accessed=int(us * 3.5e6), transcendentals=0),
        compiler_params=pltpu.CompilerParams(vmem_limit_bytes=32 << 20),
        name=name,
    )(*operands)


def per_device(cells_x, orbitals, potential):
    pairs, orbs = lax.axis_size("pair"), lax.axis_size("orb")
    size = 2 * pairs
    grid_axes = ("pair", "mem")
    m = lax.axis_index("mem")
    own_orbs, n, ny, nz = orbitals.shape
    half = own_orbs // 2
    count = orbs * own_orbs
    swap = [(g, g ^ 1) for g in range(size)]
    cross = [(g, (g + 1) % size if g % 2 else (g - 1) % size) for g in range(size)]
    along = [(g, (g + 2) % size if g % 2 else (g - 2) % size) for g in range(size)]
    up = [(g, (g + 2) % size) for g in range(size)]
    down = [(g, (g - 2) % size) for g in range(size)]
    f32, bf16 = jnp.float32, jnp.bfloat16
    rows = CHUNK * ny
    mats = call(
        functools.partial(lambda ring, ymat, zmat: matrices(ymat, zmat, ring), ny),
        (),
        [jax.ShapeDtypeStruct((rows, 3 * rows), bf16), jax.ShapeDtypeStruct((3 * nz, nz), bf16)],
        [],
        0.5,
        "matrices",
    )

    v = potential[None]
    v4 = jnp.where(m == 0, v[:, :4], v[:, n - 4 :])
    first = []
    for o in range(half):
        a = b = lax.dynamic_slice_in_dim(orbitals, half * (1 - m) + o, 1, 0)
        c = lax.dynamic_slice_in_dim(orbitals, half * m + o, 1, 0)
        if o == 0:
            a, b, c = jnp.concatenate([a, v], 1), jnp.concatenate([b, v4], 1), jnp.concatenate([c, v4], 1)
        ra = lax.ppermute(a, grid_axes, swap)
        rb = lax.ppermute(b, grid_axes, cross)
        rc = lax.ppermute(c, grid_axes, along)
        first.append((*mats, c, ra, rb, rc))

    def field(layers):
        return pltpu.VMEM((layers, ny, nz), f32)

    def products(layers):
        return pltpu.VMEM((layers // CHUNK, rows, nz), f32)

    second, v_above = [], None
    for o in range(half):
        outs = [(1, n + 4, ny, nz), (1, n, ny, nz), (1, 2 * n + 4, ny, nz)]
        scratch = [field(4 * n), field(2 * n + 8), products(2 * n + 8)]
        if o == 0:
            outs = [(1, 2 * n, ny, nz)] + outs[1:] + [(2 * n + 8, ny, nz)]
            lo, hi, y0, vext = call(first_two, first[o] + (potential,), outs, scratch, 1.0, "filter_1_2")
        else:
            lo, hi, y0 = call(first_two, first[o] + (vext,), outs, scratch, 10.0, "filter_1_2")
        rlo = lax.ppermute(hi, grid_axes, up)
        rhi = lax.ppermute(lo, grid_axes, down)
        v_above = rhi if o == 0 else v_above
        second.append((*mats, rlo, lo, hi, rhi, y0, vext, v_above))

    group = 2 * orbs
    per = 2 * n // group
    scratch = [pltpu.VMEM((2, 2 * n, ny, nz), f32), field(2 * n + 12), field(2 * n + 4), products(2 * n + 12)]

    def peer(x, k):
        return lax.ppermute(x, ("mem", "orb"), [(t, t ^ k) for t in range(group)]) if k else x

    block = (2, per, ny, nz)
    early = len(EARLY)
    outs = [(2, n, ny, nz), (len(LATE), *block)] + [block] * early
    home, late, *early_a = call(last_three, second[0], outs, scratch, 1.5, "filter_3_4_hamiltonian")
    early_a = [peer(x, k) for k, x in zip(EARLY, early_a)]
    outs = [(half, n, ny, nz)] * 2 + [block] * early + [(half, *block)] * len(LATE)
    keep, send, *blocks = call(
        last_three, (*second[1], home, late), outs, scratch, 1.5, "filter_3_4_hamiltonian"
    )
    tied = lax.optimization_barrier((*blocks[early:-1], *early_a))
    late = [peer(x, k) for k, x in zip(LATE[:-1], tied)] + blocks[-1:]
    early_b = [peer(x, k) for k, x in zip(EARLY, blocks)]
    xs = [*tied[-early:], *early_b, *late]
    (sums,) = call(
        gram,
        xs,
        [(size * orbs, 1, 2 * own_orbs * count)],
        [pltpu.VMEM((2, count, nz), f32), pltpu.VMEM((half, group, *block), f32)],
        1.3,
        "gram",
    )
    send, sums = lax.optimization_barrier((send, sums))
    back = lax.ppermute(send, grid_axes, swap)
    sums = lax.all_to_all(sums, ("pair", "mem", "orb"), 0, 0, tiled=True)
    filtered = jnp.where(m == 0, jnp.concatenate([keep, back]), jnp.concatenate([back, keep]))
    sums, filtered = lax.optimization_barrier((sums, filtered))
    corr, ham = call(
        functools.partial(finish, float(cells_x * ny * nz)), (sums,), [(own_orbs, count)] * 2, [], 0.3, "finish"
    )
    return filtered, corr, ham


def solution(mesh):
    devices = mesh.devices
    size, orbs = devices.shape
    fine = Mesh(devices.reshape(size // 2, 2, orbs), ("pair", "mem", "orb"))
    grid = ("pair", "mem")

    def whole(orbitals, potential):
        return jax.shard_map(
            functools.partial(per_device, orbitals.shape[1]),
            mesh=fine,
            in_specs=(P("orb", grid, None, None), P(grid, None, None)),
            out_specs=(P("orb", grid, None, None), P("orb", None), P("orb", None)),
            check_vma=False,
        )(orbitals, potential)

    return whole
```

```python
import functools

import jax
import jax.numpy as jnp
from jax import lax
from jax.experimental import pallas as pl
from jax.experimental.pallas import tpu as pltpu
from jax.sharding import Mesh, PartitionSpec as P

COEFS = (-205.0 / 72.0, 8.0 / 5.0, -1.0 / 5.0, 8.0 / 315.0, -1.0 / 560.0)
SCALE = 5040.0
WHOLE = (8064.0, -1008.0, 128.0, -9.0)
LOWER = -1.0
CUT = 4.0
UPPER = 10.0
HALF = (UPPER - CUT) / 2.0
CENTRE = (UPPER + CUT) / 2.0
S1 = HALF / (LOWER - CENTRE)
T2 = 2.0 / S1**2 - 1.0
T4 = 2.0 * T2 * T2 - 1.0
EARLY = (6, 4)
LATE = (2, 7, 5, 3, 1, 0)
CHUNK = 4


def ring_matrix(rows, cols, ring):
    row = lax.broadcasted_iota(jnp.int32, (rows, cols), 0)
    col = lax.broadcasted_iota(jnp.int32, (rows, cols), 1)
    size = min(rows, cols)
    row, col = lax.rem(row, size), lax.rem(col, size)
    gap = jnp.abs(row - col)
    out = jnp.zeros((rows, cols), jnp.float32)
    for k, value in enumerate(WHOLE, 1):
        out = jnp.where((gap == k) | (gap == ring - k), value, out)
    return jnp.where(row // ring == col // ring, out, 0.0).astype(jnp.bfloat16)


def matrices(ymat, zmat, ring):
    ymat[...] = ring_matrix(*ymat.shape, ring)
    zmat[...] = ring_matrix(*zmat.shape, zmat.shape[1])


def sweep(at, count, v_at, gain, centre, emit, mats, yz, one_sided=False):
    ymat, zmat = mats
    ny, nz = ymat.shape[0] // CHUNK, zmat.shape[1]
    share = 0.5 * gain if one_sided else gain

    def along_yz(c):
        f = jnp.concatenate([at(c + j, slice(0, ny)) for j in range(CHUNK)], axis=0)
        high = f.astype(jnp.bfloat16)
        rest = f - high.astype(jnp.float32)
        mid = rest.astype(jnp.bfloat16)
        low = (rest - mid.astype(jnp.float32)).astype(jnp.bfloat16)
        z = jnp.dot(jnp.concatenate([high, mid, low], axis=1), zmat[...], preferred_element_type=jnp.float32)
        y = jnp.dot(ymat[...], jnp.concatenate([high, mid, low], axis=0), preferred_element_type=jnp.float32)
        yz[c // CHUNK] = y + z

    along_yz(0)
    for c in range(0, count, CHUNK):
        if c + CHUNK < count:
            along_yz(c + CHUNK)
        for r in range(0, ny, 8):
            rows = slice(r, r + 8)
            f = {i: at(i, rows) for i in range(c if one_sided else c - 4, c + CHUNK + 4)}
            for j in range(CHUNK):
                i = c + j
                total = (share * v_at(i, rows) + share * (-1.5 * COEFS[0] - centre)) * f[i]
                total = total + (-0.5 * share / SCALE) * yz[c // CHUNK, j * ny + r : j * ny + r + 8, :]
                for k in range(1, 5):
                    if one_sided:
                        total = total + (-0.5 * gain * COEFS[k]) * f[i + k]
                    else:
                        total = total + (-0.5 * gain * COEFS[k]) * (f[i - k] + f[i + k])
                emit(i, rows, total)


def places():
    m, place = lax.axis_index("mem"), lax.axis_index("orb")
    return m, place, m * lax.axis_size("orb") + place


def first_two(ymat, zmat, mine, ra, rb, rc, *refs):
    m = places()[0]
    mats = (ymat, zmat)
    n = rc.shape[1] if len(refs) == 7 else refs[0].shape[0]
    own, blocks = n + n * m, ((ra, 2 * n - n * m), (rb, 3 * n * m), (rc, 3 * n - 3 * n * m))
    if len(refs) == 7:
        v, lo_ref, hi_ref, y0_ref, y0, w, yz = refs
    else:
        potential, lo_ref, hi_ref, y0_ref, v, y0, w, yz = refs
        v[pl.ds(4 + n * m, n)] = potential[...]
        v[pl.ds(4 + n - n * m, n)] = ra[0, n:]
        v[pl.ds((2 * n + 4) * m, 4)] = rb[0, n:]
        v[pl.ds((2 * n + 4) * (1 - m), 4)] = rc[0, n:]
        lo_ref[0, n + 4 :] = v[8 : 4 + n]
    y0[pl.ds(own, n)] = mine[0, :n]
    for ref, at in blocks:
        y0[pl.ds(at, n)] = ref[0, :n]
    y0_ref[0] = y0[n : 3 * n + 4]

    def one(i, rows, total):
        w[i, rows, :] = total

    sweep(lambda i, r: y0[4 + i, r, :], 2 * n + 8, lambda i, r: v[i, r, :], 1.0 / HALF, CENTRE, one, mats, yz)

    def two(i, rows, total):
        y2 = total - (1.0 / T2) * y0[n + i, rows, :]
        if i < n + 4:
            lo_ref[0, i, rows, :] = y2
        if i >= n:
            hi_ref[0, i - n, rows, :] = y2

    sweep(
        lambda i, r: w[4 + i, r, :], 2 * n, lambda i, r: v[4 + i, r, :], 2.0 / (T2 * HALF), CENTRE, two, mats, yz
    )


def last_three(ymat, zmat, rlo, lo, hi, rhi, y0, v, v_above, *refs):
    outs, (both, u, f, yz) = refs[:-4], refs[-4:]
    mats = (ymat, zmat)
    n = hi.shape[1]

    def y2(i, rows):
        for ref, start in ((rlo, -n), (lo, 0), (hi, n)):
            if i < start + n:
                return ref[0, i - start, rows, :]
        return rhi[0, i - 2 * n, rows, :]

    def three(i, rows, total):
        u[i, rows, :] = total

    def v_at(i, rows):
        return v[i + 4, rows, :] if i < 2 * n + 4 else v_above[0, i - n, rows, :]

    sweep(lambda i, r: y2(i - 4, r), 2 * n + 12, lambda i, r: v_at(i - 4, r), 1.0 / HALF, CENTRE, three, mats, yz)

    def four(i, rows, total):
        f[i, rows, :] = total - (2.0 * T2 / T4) * y2(i, rows) - (1.0 / T4) * y0[0, i, rows, :]

    sweep(lambda i, r: u[4 + i, r, :], 2 * n + 4, v_at, 4.0 * T2 / (T4 * HALF), CENTRE, four, mats, yz)

    def five(i, rows, total):
        both[0, i, rows, :] = f[i, rows, :]
        both[1, i, rows, :] = total

    sweep(lambda i, r: f[i, r, :], 2 * n, v_at, 1.0, 0.0, five, mats, yz, one_sided=True)
    m, _, me = places()
    homes = (n * m, n - n * m)

    def cells(which, k, per):
        return both[which, pl.ds(per * jnp.bitwise_xor(me, k), per)]

    early = len(EARLY)
    if len(outs) == 2 + early:
        home, late, *blocks = outs
        for i, start in enumerate(homes):
            home[i] = both[0, pl.ds(start, n)]
        for i, k in enumerate(LATE):
            for which in range(2):
                late[i, which] = cells(which, k, late.shape[2])
    else:
        home_a, late_a, keep, send, *blocks = outs
        for i, ref in enumerate((keep, send)):
            ref[0] = home_a[i]
            ref[1] = both[0, pl.ds(homes[i], n)]
        for i, (k, block) in enumerate(zip(LATE, blocks[early:])):
            block[0] = late_a[i]
            for which in range(2):
                block[1, which] = cells(which, k, block.shape[2])
    for k, block in zip(EARLY, blocks):
        for which in range(2):
            block[which] = cells(which, k, block.shape[1])


def gram(*refs):
    *xs, out_ref, part, blocks = refs
    orbs = part.shape[1]
    half, peers, _, per, ny, nz = blocks.shape
    me = places()[2]
    early = len(EARLY)
    for o in range(half):
        for k, x in zip(EARLY, xs[early * o :]):
            blocks[o, jnp.bitwise_xor(me, k)] = x[...]
        for k, x in zip(LATE, xs[early * half :]):
            blocks[o, jnp.bitwise_xor(me, k)] = x[o]
    rows = per * ny
    flat = blocks.reshape(half * peers * 2 * rows, nz)
    fields = jnp.concatenate(
        [
            jnp.concatenate(
                [
                    flat[pl.ds((o * peers * 2 + which) * rows + r, peers, stride=2 * rows), :]
                    for which in range(2)
                    for o in range(half)
                ],
                axis=0,
            )
            for r in range(rows)
        ],
        axis=1,
    )
    high = fields.astype(jnp.bfloat16)
    rest = fields - high.astype(jnp.float32)
    mid = rest.astype(jnp.bfloat16)
    low = (rest - mid.astype(jnp.float32)).astype(jnp.bfloat16)
    terms = jnp.concatenate([high, mid, low], axis=0)
    products = lax.dot_general(terms, terms, (((1,), (1,)), ((), ())), preferred_element_type=jnp.float32)
    size = 2 * orbs
    both = jnp.zeros((size, size), jnp.float32)
    for i in (2, 1, 0):
        for j in (2, 1, 0):
            both = both + products[i * size : (i + 1) * size, j * size : (j + 1) * size]
    both = jnp.concatenate([both[:orbs, :orbs], both[orbs:, :orbs] + both[:orbs, orbs:]], axis=0)
    row = lax.broadcasted_iota(jnp.int32, (orbs, orbs), 0)
    quarter = peers // 2
    target = 4 * (row % quarter) + 2 * (row // quarter % 2) + row // peers
    order = (lax.broadcasted_iota(jnp.int32, (orbs, orbs), 1) == target).astype(jnp.float32)
    both = jnp.dot(both, order, precision=lax.Precision.HIGHEST, preferred_element_type=jnp.float32)
    part[...] = jnp.zeros_like(part)
    for which in range(2):
        part[which, :, :orbs] = both[which * orbs : (which + 1) * orbs]
    own = nz // (2 * orbs)
    packed = jnp.zeros((quarter, nz), jnp.float32)
    for i in range(2 * own):
        start = i % 2 * peers + i % own // 2 * quarter
        rolled = part[i // own, start : start + quarter, :]
        packed = packed + (pltpu.roll(rolled, i * orbs, 1) if i else rolled)

    for g in range(out_ref.shape[0] // quarter):
        out_ref[g * quarter : (g + 1) * quarter] = packed.reshape(quarter, 1, nz)


def finish(cells, x_ref, c_ref, h_ref):
    sums = jnp.sum(x_ref[...], axis=0) * (1.0 / cells)
    own, count = c_ref.shape
    nz = sums.shape[1]
    for r in range(own):
        c_ref[r : r + 1, :] = pltpu.roll(sums, (nz - r * count) % nz, 1)[:, :count]
        h_ref[r : r + 1, :] = pltpu.roll(sums, (nz - (own + r) * count) % nz, 1)[:, :count]


VMEM = pl.BlockSpec(memory_space=pltpu.VMEM)


def call(body, operands, outs, scratch, us, name):
    return pl.pallas_call(
        body,
        out_shape=[s if isinstance(s, jax.ShapeDtypeStruct) else jax.ShapeDtypeStruct(s, jnp.float32) for s in outs],
        in_specs=[VMEM] * len(operands),
        out_specs=[VMEM] * len(outs),
        scratch_shapes=scratch,
        cost_estimate=pl.CostEstimate(flops=int(us * 1e9), bytes_accessed=int(us * 3.5e6), transcendentals=0),
        compiler_params=pltpu.CompilerParams(vmem_limit_bytes=32 << 20),
        name=name,
    )(*operands)


def per_device(cells_x, orbitals, potential):
    pairs, orbs = lax.axis_size("pair"), lax.axis_size("orb")
    size = 2 * pairs
    grid_axes = ("pair", "mem")
    m = lax.axis_index("mem")
    own_orbs, n, ny, nz = orbitals.shape
    half = own_orbs // 2
    count = orbs * own_orbs
    swap = [(g, g ^ 1) for g in range(size)]
    cross = [(g, (g + 1) % size if g % 2 else (g - 1) % size) for g in range(size)]
    along = [(g, (g + 2) % size if g % 2 else (g - 2) % size) for g in range(size)]
    up = [(g, (g + 2) % size) for g in range(size)]
    down = [(g, (g - 2) % size) for g in range(size)]
    f32, bf16 = jnp.float32, jnp.bfloat16
    rows = CHUNK * ny
    mats = call(
        functools.partial(lambda ring, ymat, zmat: matrices(ymat, zmat, ring), ny),
        (),
        [jax.ShapeDtypeStruct((rows, 3 * rows), bf16), jax.ShapeDtypeStruct((3 * nz, nz), bf16)],
        [],
        0.5,
        "matrices",
    )

    v = potential[None]
    v4 = jnp.where(m == 0, v[:, :4], v[:, n - 4 :])
    first = []
    for o in range(half):
        a = b = lax.dynamic_slice_in_dim(orbitals, half * (1 - m) + o, 1, 0)
        c = lax.dynamic_slice_in_dim(orbitals, half * m + o, 1, 0)
        if o == 0:
            a, b, c = jnp.concatenate([a, v], 1), jnp.concatenate([b, v4], 1), jnp.concatenate([c, v4], 1)
        ra = lax.ppermute(a, grid_axes, swap)
        rb = lax.ppermute(b, grid_axes, cross)
        rc = lax.ppermute(c, grid_axes, along)
        first.append((*mats, c, ra, rb, rc))

    def field(layers):
        return pltpu.VMEM((layers, ny, nz), f32)

    def products(layers):
        return pltpu.VMEM((layers // CHUNK, rows, nz), f32)

    second, v_above = [], None
    for o in range(half):
        outs = [(1, n + 4, ny, nz), (1, n, ny, nz), (1, 2 * n + 4, ny, nz)]
        scratch = [field(4 * n), field(2 * n + 8), products(2 * n + 8)]
        if o == 0:
            outs = [(1, 2 * n, ny, nz)] + outs[1:] + [(2 * n + 8, ny, nz)]
            lo, hi, y0, vext = call(first_two, first[o] + (potential,), outs, scratch, 1.0, "filter_1_2")
        else:
            lo, hi, y0 = call(first_two, first[o] + (vext,), outs, scratch, 10.0, "filter_1_2")
        rlo = lax.ppermute(hi, grid_axes, up)
        rhi = lax.ppermute(lo, grid_axes, down)
        v_above = rhi if o == 0 else v_above
        second.append((*mats, rlo, lo, hi, rhi, y0, vext, v_above))

    group = 2 * orbs
    per = 2 * n // group
    scratch = [pltpu.VMEM((2, 2 * n, ny, nz), f32), field(2 * n + 12), field(2 * n + 4), products(2 * n + 12)]

    def peer(x, k):
        return lax.ppermute(x, ("mem", "orb"), [(t, t ^ k) for t in range(group)]) if k else x

    block = (2, per, ny, nz)
    early = len(EARLY)
    outs = [(2, n, ny, nz), (len(LATE), *block)] + [block] * early
    home, late, *early_a = call(last_three, second[0], outs, scratch, 1.5, "filter_3_4_hamiltonian")
    early_a = [peer(x, k) for k, x in zip(EARLY, early_a)]
    outs = [(half, n, ny, nz)] * 2 + [block] * early + [(half, *block)] * len(LATE)
    keep, send, *blocks = call(
        last_three, (*second[1], home, late), outs, scratch, 1.5, "filter_3_4_hamiltonian"
    )
    tied = lax.optimization_barrier((*blocks[early:-1], *early_a))
    late = [peer(x, k) for k, x in zip(LATE[:-1], tied)] + blocks[-1:]
    early_b = [peer(x, k) for k, x in zip(EARLY, blocks)]
    xs = [*tied[-early:], *early_b, *late]
    (sums,) = call(
        gram,
        xs,
        [(size * orbs, 1, 2 * own_orbs * count)],
        [pltpu.VMEM((2, count, nz), f32), pltpu.VMEM((half, group, *block), f32)],
        1.3,
        "gram",
    )
    send, sums = lax.optimization_barrier((send, sums))
    back = lax.ppermute(send, grid_axes, swap)
    sums = lax.all_to_all(sums, ("pair", "mem", "orb"), 0, 0, tiled=True)
    filtered = jnp.where(m == 0, jnp.concatenate([keep, back]), jnp.concatenate([back, keep]))
    sums, filtered = lax.optimization_barrier((sums, filtered))
    corr, ham = call(
        functools.partial(finish, float(cells_x * ny * nz)), (sums,), [(own_orbs, count)] * 2, [], 0.3, "finish"
    )
    return filtered, corr, ham


def solution(mesh):
    devices = mesh.devices
    size, orbs = devices.shape
    fine = Mesh(devices.reshape(size // 2, 2, orbs), ("pair", "mem", "orb"))
    grid = ("pair", "mem")

    def whole(orbitals, potential):
        return jax.shard_map(
            functools.partial(per_device, orbitals.shape[1]),
            mesh=fine,
            in_specs=(P("orb", grid, None, None), P(grid, None, None)),
            out_specs=(P("orb", grid, None, None), P("orb", None), P("orb", None)),
            check_vma=False,
        )(orbitals, potential)

    return whole
```

```python
import functools

import jax
import jax.numpy as jnp
from jax import lax
from jax.experimental import pallas as pl
from jax.experimental.pallas import tpu as pltpu
from jax.sharding import Mesh, PartitionSpec as P

COEFS = (-205.0 / 72.0, 8.0 / 5.0, -1.0 / 5.0, 8.0 / 315.0, -1.0 / 560.0)
SCALE = 5040.0
WHOLE = (8064.0, -1008.0, 128.0, -9.0)
LOWER = -1.0
CUT = 4.0
UPPER = 10.0
HALF = (UPPER - CUT) / 2.0
CENTRE = (UPPER + CUT) / 2.0
S1 = HALF / (LOWER - CENTRE)
T2 = 2.0 / S1**2 - 1.0
T4 = 2.0 * T2 * T2 - 1.0
PEERS = (6, 4, 2, 7, 5, 3, 1, 0)
CHUNK = 4


def ring_matrix(rows, cols, ring):
    row = lax.broadcasted_iota(jnp.int32, (rows, cols), 0)
    col = lax.broadcasted_iota(jnp.int32, (rows, cols), 1)
    size = min(rows, cols)
    row, col = lax.rem(row, size), lax.rem(col, size)
    gap = jnp.abs(row - col)
    out = jnp.zeros((rows, cols), jnp.float32)
    for k, value in enumerate(WHOLE, 1):
        out = jnp.where((gap == k) | (gap == ring - k), value, out)
    return jnp.where(row // ring == col // ring, out, 0.0).astype(jnp.bfloat16)


def matrices(ymat, zmat, ring):
    ymat[...] = ring_matrix(*ymat.shape, ring)
    zmat[...] = ring_matrix(*zmat.shape, zmat.shape[1])


def sweep(at, count, v_at, gain, centre, emit, mats, yz, one_sided=False):
    ymat, zmat = mats
    ny, nz = ymat.shape[0] // CHUNK, zmat.shape[1]
    share = 0.5 * gain if one_sided else gain

    def along_yz(c):
        f = jnp.concatenate([at(c + j, slice(0, ny)) for j in range(CHUNK)], axis=0)
        high = f.astype(jnp.bfloat16)
        rest = f - high.astype(jnp.float32)
        mid = rest.astype(jnp.bfloat16)
        low = (rest - mid.astype(jnp.float32)).astype(jnp.bfloat16)
        z = jnp.dot(jnp.concatenate([high, mid, low], axis=1), zmat[...], preferred_element_type=jnp.float32)
        y = jnp.dot(ymat[...], jnp.concatenate([high, mid, low], axis=0), preferred_element_type=jnp.float32)
        yz[c // CHUNK] = y + z

    along_yz(0)
    for c in range(0, count, CHUNK):
        if c + CHUNK < count:
            along_yz(c + CHUNK)
        for r in range(0, ny, 8):
            rows = slice(r, r + 8)
            f = {i: at(i, rows) for i in range(c if one_sided else c - 4, c + CHUNK + 4)}
            for j in range(CHUNK):
                i = c + j
                total = (share * v_at(i, rows) + share * (-1.5 * COEFS[0] - centre)) * f[i]
                total = total + (-0.5 * share / SCALE) * yz[c // CHUNK, j * ny + r : j * ny + r + 8, :]
                for k in range(1, 5):
                    if one_sided:
                        total = total + (-0.5 * gain * COEFS[k]) * f[i + k]
                    else:
                        total = total + (-0.5 * gain * COEFS[k]) * (f[i - k] + f[i + k])
                emit(i, rows, total)


def places():
    m, place = lax.axis_index("mem"), lax.axis_index("orb")
    return m, place, m * lax.axis_size("orb") + place


def first_two(ymat, zmat, mine, ra, rb, rc, *refs):
    m = places()[0]
    mats = (ymat, zmat)
    n = rc.shape[1] if len(refs) == 7 else refs[0].shape[0]
    own, blocks = n + n * m, ((ra, 2 * n - n * m), (rb, 3 * n * m), (rc, 3 * n - 3 * n * m))
    if len(refs) == 7:
        v, lo_ref, hi_ref, y0_ref, y0, w, yz = refs
    else:
        potential, lo_ref, hi_ref, y0_ref, v, y0, w, yz = refs
        v[pl.ds(4 + n * m, n)] = potential[...]
        v[pl.ds(4 + n - n * m, n)] = ra[0, n:]
        v[pl.ds((2 * n + 4) * m, 4)] = rb[0, n:]
        v[pl.ds((2 * n + 4) * (1 - m), 4)] = rc[0, n:]
        lo_ref[0, n + 4 :] = v[8 : 4 + n]
    y0[pl.ds(own, n)] = mine[0, :n]
    for ref, at in blocks:
        y0[pl.ds(at, n)] = ref[0, :n]
    y0_ref[0] = y0[n : 3 * n + 4]

    def one(i, rows, total):
        w[i, rows, :] = total

    sweep(lambda i, r: y0[4 + i, r, :], 2 * n + 8, lambda i, r: v[i, r, :], 1.0 / HALF, CENTRE, one, mats, yz)

    def two(i, rows, total):
        y2 = total - (1.0 / T2) * y0[n + i, rows, :]
        if i < n + 4:
            lo_ref[0, i, rows, :] = y2
        if i >= n:
            hi_ref[0, i - n, rows, :] = y2

    sweep(
        lambda i, r: w[4 + i, r, :], 2 * n, lambda i, r: v[4 + i, r, :], 2.0 / (T2 * HALF), CENTRE, two, mats, yz
    )


def last_three(ymat, zmat, rlo, lo, hi, rhi, y0, v, v_above, *refs):
    outs, (both, u, f, yz) = refs[:-4], refs[-4:]
    mats = (ymat, zmat)
    n = hi.shape[1]

    def y2(i, rows):
        for ref, start in ((rlo, -n), (lo, 0), (hi, n)):
            if i < start + n:
                return ref[0, i - start, rows, :]
        return rhi[0, i - 2 * n, rows, :]

    def three(i, rows, total):
        u[i, rows, :] = total

    def v_at(i, rows):
        return v[i + 4, rows, :] if i < 2 * n + 4 else v_above[0, i - n, rows, :]

    sweep(lambda i, r: y2(i - 4, r), 2 * n + 12, lambda i, r: v_at(i - 4, r), 1.0 / HALF, CENTRE, three, mats, yz)

    def four(i, rows, total):
        f[i, rows, :] = total - (2.0 * T2 / T4) * y2(i, rows) - (1.0 / T4) * y0[0, i, rows, :]

    sweep(lambda i, r: u[4 + i, r, :], 2 * n + 4, v_at, 4.0 * T2 / (T4 * HALF), CENTRE, four, mats, yz)

    def five(i, rows, total):
        both[0, i, rows, :] = f[i, rows, :]
        both[1, i, rows, :] = total

    sweep(lambda i, r: f[i, r, :], 2 * n, v_at, 1.0, 0.0, five, mats, yz, one_sided=True)
    m, _, me = places()
    homes = (n * m, n - n * m)

    def cells(which, k, per):
        return both[which, pl.ds(per * jnp.bitwise_xor(me, k), per)]

    if len(outs) == 2:
        home, blocks = outs
        for i, start in enumerate(homes):
            home[i] = both[0, pl.ds(start, n)]
        for i, k in enumerate(PEERS):
            for which in range(2):
                blocks[i, which] = cells(which, k, blocks.shape[2])
    else:
        home_a, blocks_a, keep, send, *blocks = outs
        for i, ref in enumerate((keep, send)):
            ref[0] = home_a[i]
            ref[1] = both[0, pl.ds(homes[i], n)]
        for i, (k, block) in enumerate(zip(PEERS, blocks)):
            block[0] = blocks_a[i]
            for which in range(2):
                block[1, which] = cells(which, k, block.shape[2])


def gram(*refs):
    *xs, out_ref, part, blocks = refs
    orbs = part.shape[1]
    half, peers, _, per, ny, nz = blocks.shape
    me = places()[2]
    for k, x in zip(PEERS, xs):
        for o in range(half):
            blocks[o, jnp.bitwise_xor(me, k)] = x[o]
    rows = per * ny
    flat = blocks.reshape(half * peers * 2 * rows, nz)
    fields = jnp.concatenate(
        [
            jnp.concatenate(
                [
                    flat[pl.ds((o * peers * 2 + which) * rows + r, peers, stride=2 * rows), :]
                    for which in range(2)
                    for o in range(half)
                ],
                axis=0,
            )
            for r in range(rows)
        ],
        axis=1,
    )
    high = fields.astype(jnp.bfloat16)
    rest = fields - high.astype(jnp.float32)
    mid = rest.astype(jnp.bfloat16)
    low = (rest - mid.astype(jnp.float32)).astype(jnp.bfloat16)
    terms = jnp.concatenate([high, mid, low], axis=0)
    products = lax.dot_general(terms, terms, (((1,), (1,)), ((), ())), preferred_element_type=jnp.float32)
    size = 2 * orbs
    both = jnp.zeros((size, size), jnp.float32)
    for i in (2, 1, 0):
        for j in (2, 1, 0):
            both = both + products[i * size : (i + 1) * size, j * size : (j + 1) * size]
    both = jnp.concatenate([both[:orbs, :orbs], both[orbs:, :orbs] + both[:orbs, orbs:]], axis=0)
    row = lax.broadcasted_iota(jnp.int32, (orbs, orbs), 0)
    quarter = peers // 2
    target = 4 * (row % quarter) + 2 * (row // quarter % 2) + row // peers
    order = (lax.broadcasted_iota(jnp.int32, (orbs, orbs), 1) == target).astype(jnp.float32)
    both = jnp.dot(both, order, precision=lax.Precision.HIGHEST, preferred_element_type=jnp.float32)
    part[...] = jnp.zeros_like(part)
    for which in range(2):
        part[which, :, :orbs] = both[which * orbs : (which + 1) * orbs]
    own = nz // (2 * orbs)
    packed = jnp.zeros((quarter, nz), jnp.float32)
    for i in range(2 * own):
        start = i % 2 * peers + i % own // 2 * quarter
        rolled = part[i // own, start : start + quarter, :]
        packed = packed + (pltpu.roll(rolled, i * orbs, 1) if i else rolled)

    for g in range(out_ref.shape[0] // quarter):
        out_ref[g * quarter : (g + 1) * quarter] = packed.reshape(quarter, 1, nz)


def finish(cells, x_ref, c_ref, h_ref):
    sums = jnp.sum(x_ref[...], axis=0) * (1.0 / cells)
    own, count = c_ref.shape
    nz = sums.shape[1]
    for r in range(own):
        c_ref[r : r + 1, :] = pltpu.roll(sums, (nz - r * count) % nz, 1)[:, :count]
        h_ref[r : r + 1, :] = pltpu.roll(sums, (nz - (own + r) * count) % nz, 1)[:, :count]


VMEM = pl.BlockSpec(memory_space=pltpu.VMEM)


def call(body, operands, outs, scratch, us, name):
    return pl.pallas_call(
        body,
        out_shape=[s if isinstance(s, jax.ShapeDtypeStruct) else jax.ShapeDtypeStruct(s, jnp.float32) for s in outs],
        in_specs=[VMEM] * len(operands),
        out_specs=[VMEM] * len(outs),
        scratch_shapes=scratch,
        cost_estimate=pl.CostEstimate(flops=int(us * 1e9), bytes_accessed=int(us * 3.5e6), transcendentals=0),
        compiler_params=pltpu.CompilerParams(vmem_limit_bytes=32 << 20),
        name=name,
    )(*operands)


def per_device(cells_x, orbitals, potential):
    pairs, orbs = lax.axis_size("pair"), lax.axis_size("orb")
    size = 2 * pairs
    grid_axes = ("pair", "mem")
    m = lax.axis_index("mem")
    own_orbs, n, ny, nz = orbitals.shape
    half = own_orbs // 2
    count = orbs * own_orbs
    swap = [(g, g ^ 1) for g in range(size)]
    cross = [(g, (g + 1) % size if g % 2 else (g - 1) % size) for g in range(size)]
    along = [(g, (g + 2) % size if g % 2 else (g - 2) % size) for g in range(size)]
    up = [(g, (g + 2) % size) for g in range(size)]
    down = [(g, (g - 2) % size) for g in range(size)]
    f32, bf16 = jnp.float32, jnp.bfloat16
    rows = CHUNK * ny
    mats = call(
        functools.partial(lambda ring, ymat, zmat: matrices(ymat, zmat, ring), ny),
        (),
        [jax.ShapeDtypeStruct((rows, 3 * rows), bf16), jax.ShapeDtypeStruct((3 * nz, nz), bf16)],
        [],
        0.5,
        "matrices",
    )

    v = potential[None]
    v4 = jnp.where(m == 0, v[:, :4], v[:, n - 4 :])
    first = []
    for o in range(half):
        a = b = lax.dynamic_slice_in_dim(orbitals, half * (1 - m) + o, 1, 0)
        c = lax.dynamic_slice_in_dim(orbitals, half * m + o, 1, 0)
        if o == 0:
            a, b, c = jnp.concatenate([a, v], 1), jnp.concatenate([b, v4], 1), jnp.concatenate([c, v4], 1)
        ra = lax.ppermute(a, grid_axes, swap)
        rb = lax.ppermute(b, grid_axes, cross)
        rc = lax.ppermute(c, grid_axes, along)
        first.append((*mats, c, ra, rb, rc))

    def field(layers):
        return pltpu.VMEM((layers, ny, nz), f32)

    def products(layers):
        return pltpu.VMEM((layers // CHUNK, rows, nz), f32)

    second, v_above = [], None
    for o in range(half):
        outs = [(1, n + 4, ny, nz), (1, n, ny, nz), (1, 2 * n + 4, ny, nz)]
        scratch = [field(4 * n), field(2 * n + 8), products(2 * n + 8)]
        if o == 0:
            outs = [(1, 2 * n, ny, nz)] + outs[1:] + [(2 * n + 8, ny, nz)]
            lo, hi, y0, vext = call(first_two, first[o] + (potential,), outs, scratch, 1.0, "filter_1_2")
        else:
            lo, hi, y0 = call(first_two, first[o] + (vext,), outs, scratch, 10.0, "filter_1_2")
        rlo = lax.ppermute(hi, grid_axes, up)
        rhi = lax.ppermute(lo, grid_axes, down)
        v_above = rhi if o == 0 else v_above
        second.append((*mats, rlo, lo, hi, rhi, y0, vext, v_above))

    group = 2 * orbs
    per = 2 * n // group
    scratch = [pltpu.VMEM((2, 2 * n, ny, nz), f32), field(2 * n + 12), field(2 * n + 4), products(2 * n + 12)]

    def peer(x, k):
        return lax.ppermute(x, ("mem", "orb"), [(t, t ^ k) for t in range(group)]) if k else x

    block = (2, per, ny, nz)
    results = call(last_three, second[0], [(2, n, ny, nz), (group, *block)], scratch, 1.5, "filter_3_4_hamiltonian")
    outs = [(half, n, ny, nz)] * 2 + [(half, *block)] * group
    keep, send, *blocks = call(last_three, (*second[1], *results), outs, scratch, 1.5, "filter_3_4_hamiltonian")
    xs = [peer(x, k) for k, x in zip(PEERS, blocks)]
    (sums,) = call(
        gram,
        xs,
        [(size * orbs, 1, 2 * own_orbs * count)],
        [pltpu.VMEM((2, count, nz), f32), pltpu.VMEM((half, group, *block), f32)],
        1.3,
        "gram",
    )
    back = lax.ppermute(send, grid_axes, swap)
    sums = lax.all_to_all(sums, ("pair", "mem", "orb"), 0, 0, tiled=True)
    filtered = jnp.where(m == 0, jnp.concatenate([keep, back]), jnp.concatenate([back, keep]))
    sums, filtered = lax.optimization_barrier((sums, filtered))
    corr, ham = call(
        functools.partial(finish, float(cells_x * ny * nz)), (sums,), [(own_orbs, count)] * 2, [], 0.3, "finish"
    )
    return filtered, corr, ham


def solution(mesh):
    devices = mesh.devices
    size, orbs = devices.shape
    fine = Mesh(devices.reshape(size // 2, 2, orbs), ("pair", "mem", "orb"))
    grid = ("pair", "mem")

    def whole(orbitals, potential):
        return jax.shard_map(
            functools.partial(per_device, orbitals.shape[1]),
            mesh=fine,
            in_specs=(P("orb", grid, None, None), P(grid, None, None)),
            out_specs=(P("orb", grid, None, None), P("orb", None), P("orb", None)),
            check_vma=False,
        )(orbitals, potential)

    return whole
```

```python
import functools

import jax
import jax.numpy as jnp
from jax import lax
from jax.experimental import pallas as pl
from jax.experimental.pallas import tpu as pltpu
from jax.sharding import Mesh, PartitionSpec as P

COEFS = (-205.0 / 72.0, 8.0 / 5.0, -1.0 / 5.0, 8.0 / 315.0, -1.0 / 560.0)
SCALE = 5040.0
WHOLE = (8064.0, -1008.0, 128.0, -9.0)
LOWER = -1.0
CUT = 4.0
UPPER = 10.0
HALF = (UPPER - CUT) / 2.0
CENTRE = (UPPER + CUT) / 2.0
S1 = HALF / (LOWER - CENTRE)
T2 = 2.0 / S1**2 - 1.0
T4 = 2.0 * T2 * T2 - 1.0
PEERS = (6, 4, 2, 7, 5, 3, 1, 0)
CHUNK = 4


def ring_matrix(rows, cols, ring):
    row = lax.broadcasted_iota(jnp.int32, (rows, cols), 0)
    col = lax.broadcasted_iota(jnp.int32, (rows, cols), 1)
    size = min(rows, cols)
    row, col = lax.rem(row, size), lax.rem(col, size)
    gap = jnp.abs(row - col)
    out = jnp.zeros((rows, cols), jnp.float32)
    for k, value in enumerate(WHOLE, 1):
        out = jnp.where((gap == k) | (gap == ring - k), value, out)
    return jnp.where(row // ring == col // ring, out, 0.0).astype(jnp.bfloat16)


def matrices(ymat, zmat, ring):
    ymat[...] = ring_matrix(*ymat.shape, ring)
    zmat[...] = ring_matrix(*zmat.shape, zmat.shape[1])


def sweep(at, count, v_at, gain, centre, emit, mats, yz, one_sided=False):
    ymat, zmat = mats
    ny, nz = ymat.shape[0] // CHUNK, zmat.shape[1]
    share = 0.5 * gain if one_sided else gain

    def along_yz(c):
        f = jnp.concatenate([at(c + j, slice(0, ny)) for j in range(CHUNK)], axis=0)
        high = f.astype(jnp.bfloat16)
        rest = f - high.astype(jnp.float32)
        mid = rest.astype(jnp.bfloat16)
        low = (rest - mid.astype(jnp.float32)).astype(jnp.bfloat16)
        z = jnp.dot(jnp.concatenate([high, mid, low], axis=1), zmat[...], preferred_element_type=jnp.float32)
        y = jnp.dot(ymat[...], jnp.concatenate([high, mid, low], axis=0), preferred_element_type=jnp.float32)
        yz[c // CHUNK] = y + z

    along_yz(0)
    for c in range(0, count, CHUNK):
        if c + CHUNK < count:
            along_yz(c + CHUNK)
        for r in range(0, ny, 8):
            rows = slice(r, r + 8)
            f = {i: at(i, rows) for i in range(c if one_sided else c - 4, c + CHUNK + 4)}
            for j in range(CHUNK):
                i = c + j
                total = (share * v_at(i, rows) + share * (-1.5 * COEFS[0] - centre)) * f[i]
                total = total + (-0.5 * share / SCALE) * yz[c // CHUNK, j * ny + r : j * ny + r + 8, :]
                for k in range(1, 5):
                    if one_sided:
                        total = total + (-0.5 * gain * COEFS[k]) * f[i + k]
                    else:
                        total = total + (-0.5 * gain * COEFS[k]) * (f[i - k] + f[i + k])
                emit(i, rows, total)


def places():
    m, place = lax.axis_index("mem"), lax.axis_index("orb")
    return m, place, m * lax.axis_size("orb") + place


def first_two(ymat, zmat, mine, ra, rb, rc, *refs):
    m = places()[0]
    mats = (ymat, zmat)
    n = rc.shape[1] if len(refs) == 7 else refs[0].shape[0]
    own, blocks = n + n * m, ((ra, 2 * n - n * m), (rb, 3 * n * m), (rc, 3 * n - 3 * n * m))
    if len(refs) == 7:
        v, lo_ref, hi_ref, y0_ref, y0, w, yz = refs
    else:
        potential, lo_ref, hi_ref, y0_ref, v, y0, w, yz = refs
        v[pl.ds(4 + n * m, n)] = potential[...]
        v[pl.ds(4 + n - n * m, n)] = ra[0, n:]
        v[pl.ds((2 * n + 4) * m, 4)] = rb[0, n:]
        v[pl.ds((2 * n + 4) * (1 - m), 4)] = rc[0, n:]
        lo_ref[0, n + 4 :] = v[8 : 4 + n]
    y0[pl.ds(own, n)] = mine[0, :n]
    for ref, at in blocks:
        y0[pl.ds(at, n)] = ref[0, :n]
    y0_ref[0] = y0[n : 3 * n + 4]

    def one(i, rows, total):
        w[i, rows, :] = total

    sweep(lambda i, r: y0[4 + i, r, :], 2 * n + 8, lambda i, r: v[i, r, :], 1.0 / HALF, CENTRE, one, mats, yz)

    def two(i, rows, total):
        y2 = total - (1.0 / T2) * y0[n + i, rows, :]
        if i < n + 4:
            lo_ref[0, i, rows, :] = y2
        if i >= n:
            hi_ref[0, i - n, rows, :] = y2

    sweep(
        lambda i, r: w[4 + i, r, :], 2 * n, lambda i, r: v[4 + i, r, :], 2.0 / (T2 * HALF), CENTRE, two, mats, yz
    )


def last_three(ymat, zmat, rlo, lo, hi, rhi, y0, v, v_above, *refs):
    outs, (both, u, f, yz) = refs[:-4], refs[-4:]
    mats = (ymat, zmat)
    n = hi.shape[1]

    def y2(i, rows):
        for ref, start in ((rlo, -n), (lo, 0), (hi, n)):
            if i < start + n:
                return ref[0, i - start, rows, :]
        return rhi[0, i - 2 * n, rows, :]

    def three(i, rows, total):
        u[i, rows, :] = total

    def v_at(i, rows):
        return v[i + 4, rows, :] if i < 2 * n + 4 else v_above[0, i - n, rows, :]

    sweep(lambda i, r: y2(i - 4, r), 2 * n + 12, lambda i, r: v_at(i - 4, r), 1.0 / HALF, CENTRE, three, mats, yz)

    def four(i, rows, total):
        f[i, rows, :] = total - (2.0 * T2 / T4) * y2(i, rows) - (1.0 / T4) * y0[0, i, rows, :]

    sweep(lambda i, r: u[4 + i, r, :], 2 * n + 4, v_at, 4.0 * T2 / (T4 * HALF), CENTRE, four, mats, yz)

    def five(i, rows, total):
        both[0, i, rows, :] = f[i, rows, :]
        both[1, i, rows, :] = total

    sweep(lambda i, r: f[i, r, :], 2 * n, v_at, 1.0, 0.0, five, mats, yz, one_sided=True)
    m, _, me = places()
    homes = (n * m, n - n * m)

    def cells(which, k, per):
        return both[which, pl.ds(per * jnp.bitwise_xor(me, k), per)]

    if len(outs) == 2:
        home, blocks = outs
        for i, start in enumerate(homes):
            home[i] = both[0, pl.ds(start, n)]
        for i, k in enumerate(PEERS):
            for which in range(2):
                blocks[i, which] = cells(which, k, blocks.shape[2])
    else:
        home_a, blocks_a, keep, send, *blocks = outs
        for i, ref in enumerate((keep, send)):
            ref[0] = home_a[i]
            ref[1] = both[0, pl.ds(homes[i], n)]
        for i, (k, block) in enumerate(zip(PEERS, blocks)):
            block[0] = blocks_a[i]
            for which in range(2):
                block[1, which] = cells(which, k, block.shape[2])


def gram(*refs):
    *xs, out_ref, part, blocks = refs
    orbs = part.shape[1]
    half, peers, reach, nz = blocks.shape
    rows = xs[0].shape[2] * xs[0].shape[3]
    me = places()[2]
    for k, x in zip(PEERS, xs):
        for o in range(half):
            blocks[o, jnp.bitwise_xor(me, k), : 2 * rows] = x[o].reshape(2 * rows, nz)
    flat = blocks.reshape(half * peers * reach, nz)
    fields = jnp.concatenate(
        [
            jnp.concatenate(
                [
                    flat[pl.ds(o * peers * reach + which * rows + r, peers, stride=reach), :]
                    for which in range(2)
                    for o in range(half)
                ],
                axis=0,
            )
            for r in range(rows)
        ],
        axis=1,
    )
    high = fields.astype(jnp.bfloat16)
    rest = fields - high.astype(jnp.float32)
    mid = rest.astype(jnp.bfloat16)
    low = (rest - mid.astype(jnp.float32)).astype(jnp.bfloat16)
    terms = jnp.concatenate([high, mid, low], axis=0)
    products = lax.dot_general(terms, terms, (((1,), (1,)), ((), ())), preferred_element_type=jnp.float32)
    size = 2 * orbs
    both = jnp.zeros((size, size), jnp.float32)
    for i in (2, 1, 0):
        for j in (2, 1, 0):
            both = both + products[i * size : (i + 1) * size, j * size : (j + 1) * size]
    both = jnp.concatenate([both[:orbs, :orbs], both[orbs:, :orbs] + both[:orbs, orbs:]], axis=0)
    row = lax.broadcasted_iota(jnp.int32, (orbs, orbs), 0)
    quarter = peers // 2
    target = 4 * (row % quarter) + 2 * (row // quarter % 2) + row // peers
    order = (lax.broadcasted_iota(jnp.int32, (orbs, orbs), 1) == target).astype(jnp.float32)
    both = jnp.dot(both, order, precision=lax.Precision.HIGHEST, preferred_element_type=jnp.float32)
    part[...] = jnp.zeros_like(part)
    for which in range(2):
        part[which, :, :orbs] = both[which * orbs : (which + 1) * orbs]
    own = nz // (2 * orbs)
    packed = jnp.zeros((quarter, nz), jnp.float32)
    for i in range(2 * own):
        start = i % 2 * peers + i % own // 2 * quarter
        rolled = part[i // own, start : start + quarter, :]
        packed = packed + (pltpu.roll(rolled, i * orbs, 1) if i else rolled)

    for g in range(out_ref.shape[0] // quarter):
        out_ref[g * quarter : (g + 1) * quarter] = packed.reshape(quarter, 1, nz)


def finish(cells, x_ref, c_ref, h_ref):
    sums = jnp.sum(x_ref[...], axis=0) * (1.0 / cells)
    own, count = c_ref.shape
    nz = sums.shape[1]
    for r in range(own):
        c_ref[r : r + 1, :] = pltpu.roll(sums, (nz - r * count) % nz, 1)[:, :count]
        h_ref[r : r + 1, :] = pltpu.roll(sums, (nz - (own + r) * count) % nz, 1)[:, :count]


VMEM = pl.BlockSpec(memory_space=pltpu.VMEM)


def call(body, operands, outs, scratch, us, name):
    return pl.pallas_call(
        body,
        out_shape=[s if isinstance(s, jax.ShapeDtypeStruct) else jax.ShapeDtypeStruct(s, jnp.float32) for s in outs],
        in_specs=[VMEM] * len(operands),
        out_specs=[VMEM] * len(outs),
        scratch_shapes=scratch,
        cost_estimate=pl.CostEstimate(flops=int(us * 1e9), bytes_accessed=int(us * 3.5e6), transcendentals=0),
        compiler_params=pltpu.CompilerParams(vmem_limit_bytes=32 << 20),
        name=name,
    )(*operands)


def per_device(cells_x, orbitals, potential):
    pairs, orbs = lax.axis_size("pair"), lax.axis_size("orb")
    size = 2 * pairs
    grid_axes = ("pair", "mem")
    m = lax.axis_index("mem")
    own_orbs, n, ny, nz = orbitals.shape
    half = own_orbs // 2
    count = orbs * own_orbs
    swap = [(g, g ^ 1) for g in range(size)]
    cross = [(g, (g + 1) % size if g % 2 else (g - 1) % size) for g in range(size)]
    along = [(g, (g + 2) % size if g % 2 else (g - 2) % size) for g in range(size)]
    up = [(g, (g + 2) % size) for g in range(size)]
    down = [(g, (g - 2) % size) for g in range(size)]
    f32, bf16 = jnp.float32, jnp.bfloat16
    rows = CHUNK * ny
    mats = call(
        functools.partial(lambda ring, ymat, zmat: matrices(ymat, zmat, ring), ny),
        (),
        [jax.ShapeDtypeStruct((rows, 3 * rows), bf16), jax.ShapeDtypeStruct((3 * nz, nz), bf16)],
        [],
        0.5,
        "matrices",
    )

    v = potential[None]
    v4 = jnp.where(m == 0, v[:, :4], v[:, n - 4 :])
    first = []
    for o in range(half):
        a = b = lax.dynamic_slice_in_dim(orbitals, half * (1 - m) + o, 1, 0)
        c = lax.dynamic_slice_in_dim(orbitals, half * m + o, 1, 0)
        if o == 0:
            a, b, c = jnp.concatenate([a, v], 1), jnp.concatenate([b, v4], 1), jnp.concatenate([c, v4], 1)
        ra = lax.ppermute(a, grid_axes, swap)
        rb = lax.ppermute(b, grid_axes, cross)
        rc = lax.ppermute(c, grid_axes, along)
        first.append((*mats, c, ra, rb, rc))

    def field(layers):
        return pltpu.VMEM((layers, ny, nz), f32)

    def products(layers):
        return pltpu.VMEM((layers // CHUNK, rows, nz), f32)

    second, v_above = [], None
    for o in range(half):
        outs = [(1, n + 4, ny, nz), (1, n, ny, nz), (1, 2 * n + 4, ny, nz)]
        scratch = [field(4 * n), field(2 * n + 8), products(2 * n + 8)]
        if o == 0:
            outs = [(1, 2 * n, ny, nz)] + outs[1:] + [(2 * n + 8, ny, nz)]
            lo, hi, y0, vext = call(first_two, first[o] + (potential,), outs, scratch, 1.0, "filter_1_2")
        else:
            lo, hi, y0 = call(first_two, first[o] + (vext,), outs, scratch, 10.0, "filter_1_2")
        rlo = lax.ppermute(hi, grid_axes, up)
        rhi = lax.ppermute(lo, grid_axes, down)
        v_above = rhi if o == 0 else v_above
        second.append((*mats, rlo, lo, hi, rhi, y0, vext, v_above))

    group = 2 * orbs
    per = 2 * n // group
    scratch = [pltpu.VMEM((2, 2 * n, ny, nz), f32), field(2 * n + 12), field(2 * n + 4), products(2 * n + 12)]

    def peer(x, k):
        return lax.ppermute(x, ("mem", "orb"), [(t, t ^ k) for t in range(group)]) if k else x

    block = (2, per, ny, nz)
    results = call(last_three, second[0], [(2, n, ny, nz), (group, *block)], scratch, 1.5, "filter_3_4_hamiltonian")
    outs = [(half, n, ny, nz)] * 2 + [(half, *block)] * group
    keep, send, *blocks = call(last_three, (*second[1], *results), outs, scratch, 1.5, "filter_3_4_hamiltonian")
    xs = [peer(x, k) for k, x in zip(PEERS, blocks)]
    (sums,) = call(
        gram,
        xs,
        [(size * orbs, 1, 2 * own_orbs * count)],
        [pltpu.VMEM((2, count, nz), f32), pltpu.VMEM((half, group, 2 * per * ny + 8, nz), f32)],
        1.3,
        "gram",
    )
    send, sums = lax.optimization_barrier((send, sums))
    back = lax.ppermute(send, grid_axes, swap)
    sums = lax.all_to_all(sums, ("pair", "mem", "orb"), 0, 0, tiled=True)
    filtered = jnp.where(m == 0, jnp.concatenate([keep, back]), jnp.concatenate([back, keep]))
    sums, filtered = lax.optimization_barrier((sums, filtered))
    corr, ham = call(
        functools.partial(finish, float(cells_x * ny * nz)), (sums,), [(own_orbs, count)] * 2, [], 0.3, "finish"
    )
    return filtered, corr, ham


def solution(mesh):
    devices = mesh.devices
    size, orbs = devices.shape
    fine = Mesh(devices.reshape(size // 2, 2, orbs), ("pair", "mem", "orb"))
    grid = ("pair", "mem")

    def whole(orbitals, potential):
        return jax.shard_map(
            functools.partial(per_device, orbitals.shape[1]),
            mesh=fine,
            in_specs=(P("orb", grid, None, None), P(grid, None, None)),
            out_specs=(P("orb", grid, None, None), P("orb", None), P("orb", None)),
            check_vma=False,
        )(orbitals, potential)

    return whole
```

```python
import functools

import jax
import jax.numpy as jnp
from jax import lax
from jax.experimental import pallas as pl
from jax.experimental.pallas import tpu as pltpu
from jax.sharding import Mesh, PartitionSpec as P

COEFS = (-205.0 / 72.0, 8.0 / 5.0, -1.0 / 5.0, 8.0 / 315.0, -1.0 / 560.0)
SCALE = 5040.0
WHOLE = (8064.0, -1008.0, 128.0, -9.0)
LOWER = -1.0
CUT = 4.0
UPPER = 10.0
HALF = (UPPER - CUT) / 2.0
CENTRE = (UPPER + CUT) / 2.0
S1 = HALF / (LOWER - CENTRE)
T2 = 2.0 / S1**2 - 1.0
T4 = 2.0 * T2 * T2 - 1.0
PEERS = (4, 2, 6, 7, 5, 3, 1, 0)
CHUNK = 4


def ring_matrix(rows, cols, ring):
    row = lax.broadcasted_iota(jnp.int32, (rows, cols), 0)
    col = lax.broadcasted_iota(jnp.int32, (rows, cols), 1)
    size = min(rows, cols)
    row, col = lax.rem(row, size), lax.rem(col, size)
    gap = jnp.abs(row - col)
    out = jnp.zeros((rows, cols), jnp.float32)
    for k, value in enumerate(WHOLE, 1):
        out = jnp.where((gap == k) | (gap == ring - k), value, out)
    return jnp.where(row // ring == col // ring, out, 0.0).astype(jnp.bfloat16)


def matrices(ymat, zmat, ring):
    ymat[...] = ring_matrix(*ymat.shape, ring)
    zmat[...] = ring_matrix(*zmat.shape, zmat.shape[1])


def sweep(at, count, v_at, gain, centre, emit, mats, yz, one_sided=False):
    ymat, zmat = mats
    ny, nz = ymat.shape[0] // CHUNK, zmat.shape[1]
    share = 0.5 * gain if one_sided else gain

    def along_yz(c):
        f = jnp.concatenate([at(c + j, slice(0, ny)) for j in range(CHUNK)], axis=0)
        high = f.astype(jnp.bfloat16)
        rest = f - high.astype(jnp.float32)
        mid = rest.astype(jnp.bfloat16)
        low = (rest - mid.astype(jnp.float32)).astype(jnp.bfloat16)
        z = jnp.dot(jnp.concatenate([high, mid, low], axis=1), zmat[...], preferred_element_type=jnp.float32)
        y = jnp.dot(ymat[...], jnp.concatenate([high, mid, low], axis=0), preferred_element_type=jnp.float32)
        yz[c // CHUNK] = y + z

    along_yz(0)
    for c in range(0, count, CHUNK):
        if c + CHUNK < count:
            along_yz(c + CHUNK)
        for r in range(0, ny, 8):
            rows = slice(r, r + 8)
            f = {i: at(i, rows) for i in range(c if one_sided else c - 4, c + CHUNK + 4)}
            for j in range(CHUNK):
                i = c + j
                total = (share * v_at(i, rows) + share * (-1.5 * COEFS[0] - centre)) * f[i]
                total = total + (-0.5 * share / SCALE) * yz[c // CHUNK, j * ny + r : j * ny + r + 8, :]
                for k in range(1, 5):
                    if one_sided:
                        total = total + (-0.5 * gain * COEFS[k]) * f[i + k]
                    else:
                        total = total + (-0.5 * gain * COEFS[k]) * (f[i - k] + f[i + k])
                emit(i, rows, total)


def places():
    m, place = lax.axis_index("mem"), lax.axis_index("orb")
    return m, place, m * lax.axis_size("orb") + place


def first_two(ymat, zmat, mine, ra, rb, rc, *refs):
    m = places()[0]
    mats = (ymat, zmat)
    n = rc.shape[1] if len(refs) == 7 else refs[0].shape[0]
    own, blocks = n + n * m, ((ra, 2 * n - n * m), (rb, 3 * n * m), (rc, 3 * n - 3 * n * m))
    if len(refs) == 7:
        v, lo_ref, hi_ref, y0_ref, y0, w, yz = refs
    else:
        potential, lo_ref, hi_ref, y0_ref, v, y0, w, yz = refs
        v[pl.ds(4 + n * m, n)] = potential[...]
        v[pl.ds(4 + n - n * m, n)] = ra[0, n:]
        v[pl.ds((2 * n + 4) * m, 4)] = rb[0, n:]
        v[pl.ds((2 * n + 4) * (1 - m), 4)] = rc[0, n:]
        lo_ref[0, n + 4 :] = v[8 : 4 + n]
    y0[pl.ds(own, n)] = mine[0, :n]
    for ref, at in blocks:
        y0[pl.ds(at, n)] = ref[0, :n]
    y0_ref[0] = y0[n : 3 * n + 4]

    def one(i, rows, total):
        w[i, rows, :] = total

    sweep(lambda i, r: y0[4 + i, r, :], 2 * n + 8, lambda i, r: v[i, r, :], 1.0 / HALF, CENTRE, one, mats, yz)

    def two(i, rows, total):
        y2 = total - (1.0 / T2) * y0[n + i, rows, :]
        if i < n + 4:
            lo_ref[0, i, rows, :] = y2
        if i >= n:
            hi_ref[0, i - n, rows, :] = y2

    sweep(
        lambda i, r: w[4 + i, r, :], 2 * n, lambda i, r: v[4 + i, r, :], 2.0 / (T2 * HALF), CENTRE, two, mats, yz
    )


def last_three(ymat, zmat, rlo, lo, hi, rhi, y0, v, v_above, *refs):
    outs, (both, u, f, yz) = refs[:-4], refs[-4:]
    mats = (ymat, zmat)
    n = hi.shape[1]

    def y2(i, rows):
        for ref, start in ((rlo, -n), (lo, 0), (hi, n)):
            if i < start + n:
                return ref[0, i - start, rows, :]
        return rhi[0, i - 2 * n, rows, :]

    def three(i, rows, total):
        u[i, rows, :] = total

    def v_at(i, rows):
        return v[i + 4, rows, :] if i < 2 * n + 4 else v_above[0, i - n, rows, :]

    sweep(lambda i, r: y2(i - 4, r), 2 * n + 12, lambda i, r: v_at(i - 4, r), 1.0 / HALF, CENTRE, three, mats, yz)

    def four(i, rows, total):
        f[i, rows, :] = total - (2.0 * T2 / T4) * y2(i, rows) - (1.0 / T4) * y0[0, i, rows, :]

    sweep(lambda i, r: u[4 + i, r, :], 2 * n + 4, v_at, 4.0 * T2 / (T4 * HALF), CENTRE, four, mats, yz)

    def five(i, rows, total):
        both[0, i, rows, :] = f[i, rows, :]
        both[1, i, rows, :] = total

    sweep(lambda i, r: f[i, r, :], 2 * n, v_at, 1.0, 0.0, five, mats, yz, one_sided=True)
    m, _, me = places()
    homes = (n * m, n - n * m)

    def cells(which, k, per):
        return both[which, pl.ds(per * jnp.bitwise_xor(me, k), per)]

    if len(outs) == 2:
        home, blocks = outs
        for i, start in enumerate(homes):
            home[i] = both[0, pl.ds(start, n)]
        for i, k in enumerate(PEERS):
            for which in range(2):
                blocks[i, which] = cells(which, k, blocks.shape[2])
    else:
        home_a, blocks_a, keep, send, *blocks = outs
        for i, ref in enumerate((keep, send)):
            ref[0] = home_a[i]
            ref[1] = both[0, pl.ds(homes[i], n)]
        for i, (k, block) in enumerate(zip(PEERS, blocks)):
            block[0] = blocks_a[i]
            for which in range(2):
                block[1, which] = cells(which, k, block.shape[2])


def gram(*refs):
    *xs, out_ref, part, blocks = refs
    orbs = part.shape[1]
    half, peers, reach, nz = blocks.shape
    rows = xs[0].shape[2] * xs[0].shape[3]
    me = places()[2]
    for k, x in zip(PEERS, xs):
        for o in range(half):
            blocks[o, jnp.bitwise_xor(me, k), : 2 * rows] = x[o].reshape(2 * rows, nz)
    flat = blocks.reshape(half * peers * reach, nz)
    fields = jnp.concatenate(
        [
            jnp.concatenate(
                [
                    flat[pl.ds(o * peers * reach + which * rows + r, peers, stride=reach), :]
                    for which in range(2)
                    for o in range(half)
                ],
                axis=0,
            )
            for r in range(rows)
        ],
        axis=1,
    )
    high = fields.astype(jnp.bfloat16)
    rest = fields - high.astype(jnp.float32)
    mid = rest.astype(jnp.bfloat16)
    low = (rest - mid.astype(jnp.float32)).astype(jnp.bfloat16)
    terms = jnp.concatenate([high, mid, low], axis=0)
    products = lax.dot_general(terms, terms, (((1,), (1,)), ((), ())), preferred_element_type=jnp.float32)
    size = 2 * orbs
    both = jnp.zeros((size, size), jnp.float32)
    for i in (2, 1, 0):
        for j in (2, 1, 0):
            both = both + products[i * size : (i + 1) * size, j * size : (j + 1) * size]
    both = jnp.concatenate([both[:orbs, :orbs], both[orbs:, :orbs] + both[:orbs, orbs:]], axis=0)
    row = lax.broadcasted_iota(jnp.int32, (orbs, orbs), 0)
    quarter = peers // 2
    target = 4 * (row % quarter) + 2 * (row // quarter % 2) + row // peers
    order = (lax.broadcasted_iota(jnp.int32, (orbs, orbs), 1) == target).astype(jnp.float32)
    both = jnp.dot(both, order, precision=lax.Precision.HIGHEST, preferred_element_type=jnp.float32)
    part[...] = jnp.zeros_like(part)
    for which in range(2):
        part[which, :, :orbs] = both[which * orbs : (which + 1) * orbs]
    own = nz // (2 * orbs)
    packed = jnp.zeros((quarter, nz), jnp.float32)
    for i in range(2 * own):
        start = i % 2 * peers + i % own // 2 * quarter
        rolled = part[i // own, start : start + quarter, :]
        packed = packed + (pltpu.roll(rolled, i * orbs, 1) if i else rolled)

    for g in range(out_ref.shape[0] // quarter):
        out_ref[g * quarter : (g + 1) * quarter] = packed.reshape(quarter, 1, nz)


def finish(cells, x_ref, c_ref, h_ref):
    sums = jnp.sum(x_ref[...], axis=0) * (1.0 / cells)
    own, count = c_ref.shape
    nz = sums.shape[1]
    for r in range(own):
        c_ref[r : r + 1, :] = pltpu.roll(sums, (nz - r * count) % nz, 1)[:, :count]
        h_ref[r : r + 1, :] = pltpu.roll(sums, (nz - (own + r) * count) % nz, 1)[:, :count]


VMEM = pl.BlockSpec(memory_space=pltpu.VMEM)


def call(body, operands, outs, scratch, us, name):
    return pl.pallas_call(
        body,
        out_shape=[s if isinstance(s, jax.ShapeDtypeStruct) else jax.ShapeDtypeStruct(s, jnp.float32) for s in outs],
        in_specs=[VMEM] * len(operands),
        out_specs=[VMEM] * len(outs),
        scratch_shapes=scratch,
        cost_estimate=pl.CostEstimate(flops=int(us * 1e9), bytes_accessed=int(us * 3.5e6), transcendentals=0),
        compiler_params=pltpu.CompilerParams(vmem_limit_bytes=32 << 20),
        name=name,
    )(*operands)


def per_device(cells_x, orbitals, potential):
    pairs, orbs = lax.axis_size("pair"), lax.axis_size("orb")
    size = 2 * pairs
    grid_axes = ("pair", "mem")
    m = lax.axis_index("mem")
    own_orbs, n, ny, nz = orbitals.shape
    half = own_orbs // 2
    count = orbs * own_orbs
    swap = [(g, g ^ 1) for g in range(size)]
    cross = [(g, (g + 1) % size if g % 2 else (g - 1) % size) for g in range(size)]
    along = [(g, (g + 2) % size if g % 2 else (g - 2) % size) for g in range(size)]
    up = [(g, (g + 2) % size) for g in range(size)]
    down = [(g, (g - 2) % size) for g in range(size)]
    f32, bf16 = jnp.float32, jnp.bfloat16
    rows = CHUNK * ny
    mats = call(
        functools.partial(lambda ring, ymat, zmat: matrices(ymat, zmat, ring), ny),
        (),
        [jax.ShapeDtypeStruct((rows, 3 * rows), bf16), jax.ShapeDtypeStruct((3 * nz, nz), bf16)],
        [],
        0.5,
        "matrices",
    )

    v = potential[None]
    v4 = jnp.where(m == 0, v[:, :4], v[:, n - 4 :])
    first = []
    for o in range(half):
        a = b = lax.dynamic_slice_in_dim(orbitals, half * (1 - m) + o, 1, 0)
        c = lax.dynamic_slice_in_dim(orbitals, half * m + o, 1, 0)
        if o == 0:
            a, b, c = jnp.concatenate([a, v], 1), jnp.concatenate([b, v4], 1), jnp.concatenate([c, v4], 1)
        ra = lax.ppermute(a, grid_axes, swap)
        rb = lax.ppermute(b, grid_axes, cross)
        rc = lax.ppermute(c, grid_axes, along)
        first.append((*mats, c, ra, rb, rc))
        orbitals, _ = lax.optimization_barrier((orbitals, a))

    def field(layers):
        return pltpu.VMEM((layers, ny, nz), f32)

    def products(layers):
        return pltpu.VMEM((layers // CHUNK, rows, nz), f32)

    second, v_above = [], None
    for o in range(half):
        outs = [(1, n + 4, ny, nz), (1, n, ny, nz), (1, 2 * n + 4, ny, nz)]
        scratch = [field(4 * n), field(2 * n + 8), products(2 * n + 8)]
        if o == 0:
            outs = [(1, 2 * n, ny, nz)] + outs[1:] + [(2 * n + 8, ny, nz)]
            lo, hi, y0, vext = call(first_two, first[o] + (potential,), outs, scratch, 1.0, "filter_1_2")
        else:
            lo, hi, y0 = call(first_two, first[o] + (vext,), outs, scratch, 10.0, "filter_1_2")
        rlo = lax.ppermute(hi, grid_axes, up)
        rhi = lax.ppermute(lo, grid_axes, down)
        v_above = rhi if o == 0 else v_above
        second.append((*mats, rlo, lo, hi, rhi, y0, vext, v_above))

    group = 2 * orbs
    per = 2 * n // group
    scratch = [pltpu.VMEM((2, 2 * n, ny, nz), f32), field(2 * n + 12), field(2 * n + 4), products(2 * n + 12)]

    def peer(x, k):
        return lax.ppermute(x, ("mem", "orb"), [(t, t ^ k) for t in range(group)]) if k else x

    block = (2, per, ny, nz)
    results = call(last_three, second[0], [(2, n, ny, nz), (group, *block)], scratch, 1.5, "filter_3_4_hamiltonian")
    outs = [(half, n, ny, nz)] * 2 + [(half, *block)] * group
    keep, send, *blocks = call(last_three, (*second[1], *results), outs, scratch, 1.5, "filter_3_4_hamiltonian")
    xs = [peer(x, k) for k, x in zip(PEERS, blocks)]
    (sums,) = call(
        gram,
        xs,
        [(size * orbs, 1, 2 * own_orbs * count)],
        [pltpu.VMEM((2, count, nz), f32), pltpu.VMEM((half, group, 2 * per * ny + 8, nz), f32)],
        1.3,
        "gram",
    )
    send, sums = lax.optimization_barrier((send, sums))
    back = lax.ppermute(send, grid_axes, swap)
    sums = lax.all_to_all(sums, ("pair", "mem", "orb"), 0, 0, tiled=True)
    filtered = jnp.where(m == 0, jnp.concatenate([keep, back]), jnp.concatenate([back, keep]))
    sums, filtered = lax.optimization_barrier((sums, filtered))
    corr, ham = call(
        functools.partial(finish, float(cells_x * ny * nz)), (sums,), [(own_orbs, count)] * 2, [], 0.3, "finish"
    )
    return filtered, corr, ham


def solution(mesh):
    devices = mesh.devices
    size, orbs = devices.shape
    fine = Mesh(devices.reshape(size // 2, 2, orbs), ("pair", "mem", "orb"))
    grid = ("pair", "mem")

    def whole(orbitals, potential):
        return jax.shard_map(
            functools.partial(per_device, orbitals.shape[1]),
            mesh=fine,
            in_specs=(P("orb", grid, None, None), P(grid, None, None)),
            out_specs=(P("orb", grid, None, None), P("orb", None), P("orb", None)),
            check_vma=False,
        )(orbitals, potential)

    return whole
```

```python
import functools

import jax
import jax.numpy as jnp
from jax import lax
from jax.experimental import pallas as pl
from jax.experimental.pallas import tpu as pltpu
from jax.sharding import Mesh, PartitionSpec as P

COEFS = (-205.0 / 72.0, 8.0 / 5.0, -1.0 / 5.0, 8.0 / 315.0, -1.0 / 560.0)
SCALE = 5040.0
WHOLE = (8064.0, -1008.0, 128.0, -9.0)
LOWER = -1.0
CUT = 4.0
UPPER = 10.0
HALF = (UPPER - CUT) / 2.0
CENTRE = (UPPER + CUT) / 2.0
S1 = HALF / (LOWER - CENTRE)
T2 = 2.0 / S1**2 - 1.0
T4 = 2.0 * T2 * T2 - 1.0
EARLY = (6, 4, 2)
LATE = (7, 5, 3, 1, 0)
CHUNK = 4


def ring_matrix(rows, cols, ring):
    row = lax.broadcasted_iota(jnp.int32, (rows, cols), 0)
    col = lax.broadcasted_iota(jnp.int32, (rows, cols), 1)
    size = min(rows, cols)
    row, col = lax.rem(row, size), lax.rem(col, size)
    gap = jnp.abs(row - col)
    out = jnp.zeros((rows, cols), jnp.float32)
    for k, value in enumerate(WHOLE, 1):
        out = jnp.where((gap == k) | (gap == ring - k), value, out)
    return jnp.where(row // ring == col // ring, out, 0.0).astype(jnp.bfloat16)


def matrices(ymat, zmat, ring):
    ymat[...] = ring_matrix(*ymat.shape, ring)
    zmat[...] = ring_matrix(*zmat.shape, zmat.shape[1])


def sweep(at, count, v_at, gain, centre, emit, mats, yz, one_sided=False):
    ymat, zmat = mats
    ny, nz = ymat.shape[0] // CHUNK, zmat.shape[1]
    share = 0.5 * gain if one_sided else gain

    def along_yz(c):
        f = jnp.concatenate([at(c + j, slice(0, ny)) for j in range(CHUNK)], axis=0)
        high = f.astype(jnp.bfloat16)
        rest = f - high.astype(jnp.float32)
        mid = rest.astype(jnp.bfloat16)
        low = (rest - mid.astype(jnp.float32)).astype(jnp.bfloat16)
        z = jnp.dot(jnp.concatenate([high, mid, low], axis=1), zmat[...], preferred_element_type=jnp.float32)
        y = jnp.dot(ymat[...], jnp.concatenate([high, mid, low], axis=0), preferred_element_type=jnp.float32)
        yz[c // CHUNK] = y + z

    along_yz(0)
    for c in range(0, count, CHUNK):
        if c + CHUNK < count:
            along_yz(c + CHUNK)
        for r in range(0, ny, 8):
            rows = slice(r, r + 8)
            f = {i: at(i, rows) for i in range(c if one_sided else c - 4, c + CHUNK + 4)}
            for j in range(CHUNK):
                i = c + j
                total = (share * v_at(i, rows) + share * (-1.5 * COEFS[0] - centre)) * f[i]
                total = total + (-0.5 * share / SCALE) * yz[c // CHUNK, j * ny + r : j * ny + r + 8, :]
                for k in range(1, 5):
                    if one_sided:
                        total = total + (-0.5 * gain * COEFS[k]) * f[i + k]
                    else:
                        total = total + (-0.5 * gain * COEFS[k]) * (f[i - k] + f[i + k])
                emit(i, rows, total)


def places():
    m, place = lax.axis_index("mem"), lax.axis_index("orb")
    return m, place, m * lax.axis_size("orb") + place


def first_two(ymat, zmat, mine, ra, rb, rc, *refs):
    m = places()[0]
    mats = (ymat, zmat)
    n = rc.shape[1] if len(refs) == 7 else refs[0].shape[0]
    own, blocks = n + n * m, ((ra, 2 * n - n * m), (rb, 3 * n * m), (rc, 3 * n - 3 * n * m))
    if len(refs) == 7:
        v, lo_ref, hi_ref, y0_ref, y0, w, yz = refs
    else:
        potential, lo_ref, hi_ref, y0_ref, v, y0, w, yz = refs
        v[pl.ds(4 + n * m, n)] = potential[...]
        v[pl.ds(4 + n - n * m, n)] = ra[0, n:]
        v[pl.ds((2 * n + 4) * m, 4)] = rb[0, n:]
        v[pl.ds((2 * n + 4) * (1 - m), 4)] = rc[0, n:]
        lo_ref[0, n + 4 :] = v[8 : 4 + n]
    y0[pl.ds(own, n)] = mine[0, :n]
    for ref, at in blocks:
        y0[pl.ds(at, n)] = ref[0, :n]
    y0_ref[0] = y0[n : 3 * n + 4]

    def one(i, rows, total):
        w[i, rows, :] = total

    sweep(lambda i, r: y0[4 + i, r, :], 2 * n + 8, lambda i, r: v[i, r, :], 1.0 / HALF, CENTRE, one, mats, yz)

    def two(i, rows, total):
        y2 = total - (1.0 / T2) * y0[n + i, rows, :]
        if i < n + 4:
            lo_ref[0, i, rows, :] = y2
        if i >= n:
            hi_ref[0, i - n, rows, :] = y2

    sweep(
        lambda i, r: w[4 + i, r, :], 2 * n, lambda i, r: v[4 + i, r, :], 2.0 / (T2 * HALF), CENTRE, two, mats, yz
    )


def last_three(ymat, zmat, rlo, lo, hi, rhi, y0, v, v_above, *refs):
    outs, (both, u, f, yz) = refs[:-4], refs[-4:]
    mats = (ymat, zmat)
    n = hi.shape[1]

    def y2(i, rows):
        for ref, start in ((rlo, -n), (lo, 0), (hi, n)):
            if i < start + n:
                return ref[0, i - start, rows, :]
        return rhi[0, i - 2 * n, rows, :]

    def three(i, rows, total):
        u[i, rows, :] = total

    def v_at(i, rows):
        return v[i + 4, rows, :] if i < 2 * n + 4 else v_above[0, i - n, rows, :]

    sweep(lambda i, r: y2(i - 4, r), 2 * n + 12, lambda i, r: v_at(i - 4, r), 1.0 / HALF, CENTRE, three, mats, yz)

    def four(i, rows, total):
        f[i, rows, :] = total - (2.0 * T2 / T4) * y2(i, rows) - (1.0 / T4) * y0[0, i, rows, :]

    sweep(lambda i, r: u[4 + i, r, :], 2 * n + 4, v_at, 4.0 * T2 / (T4 * HALF), CENTRE, four, mats, yz)

    def five(i, rows, total):
        both[0, i, rows, :] = f[i, rows, :]
        both[1, i, rows, :] = total

    sweep(lambda i, r: f[i, r, :], 2 * n, v_at, 1.0, 0.0, five, mats, yz, one_sided=True)
    m, _, me = places()
    homes = (n * m, n - n * m)

    def cells(which, k, per):
        return both[which, pl.ds(per * jnp.bitwise_xor(me, k), per)]

    early = len(EARLY)
    if len(outs) == 2 + early:
        home, late, *blocks = outs
        for i, start in enumerate(homes):
            home[i] = both[0, pl.ds(start, n)]
        for i, k in enumerate(LATE):
            for which in range(2):
                late[i, which] = cells(which, k, late.shape[2])
    else:
        home_a, late_a, keep, send, *blocks = outs
        for i, ref in enumerate((keep, send)):
            ref[0] = home_a[i]
            ref[1] = both[0, pl.ds(homes[i], n)]
        for i, (k, block) in enumerate(zip(LATE, blocks[early:])):
            block[0] = late_a[i]
            for which in range(2):
                block[1, which] = cells(which, k, block.shape[2])
    for k, block in zip(EARLY, blocks):
        for which in range(2):
            block[which] = cells(which, k, block.shape[1])


def gram(*refs):
    *xs, out_ref, part, blocks = refs
    orbs = part.shape[1]
    half, peers, reach, nz = blocks.shape
    rows = xs[0].shape[1] * xs[0].shape[2]
    me = places()[2]
    early = len(EARLY)
    for o in range(half):
        for k, x in zip(EARLY, xs[early * o :]):
            blocks[o, jnp.bitwise_xor(me, k), : 2 * rows] = x[...].reshape(2 * rows, nz)
        for k, x in zip(LATE, xs[early * half :]):
            blocks[o, jnp.bitwise_xor(me, k), : 2 * rows] = x[o].reshape(2 * rows, nz)
    flat = blocks.reshape(half * peers * reach, nz)
    fields = jnp.concatenate(
        [
            jnp.concatenate(
                [
                    flat[pl.ds(o * peers * reach + which * rows + r, peers, stride=reach), :]
                    for which in range(2)
                    for o in range(half)
                ],
                axis=0,
            )
            for r in range(rows)
        ],
        axis=1,
    )
    high = fields.astype(jnp.bfloat16)
    rest = fields - high.astype(jnp.float32)
    mid = rest.astype(jnp.bfloat16)
    low = (rest - mid.astype(jnp.float32)).astype(jnp.bfloat16)
    terms = jnp.concatenate([high, mid, low], axis=0)
    products = lax.dot_general(terms, terms, (((1,), (1,)), ((), ())), preferred_element_type=jnp.float32)
    size = 2 * orbs
    both = jnp.zeros((size, size), jnp.float32)
    for i in (2, 1, 0):
        for j in (2, 1, 0):
            both = both + products[i * size : (i + 1) * size, j * size : (j + 1) * size]
    both = jnp.concatenate([both[:orbs, :orbs], both[orbs:, :orbs] + both[:orbs, orbs:]], axis=0)
    row = lax.broadcasted_iota(jnp.int32, (orbs, orbs), 0)
    quarter = peers // 2
    target = 4 * (row % quarter) + 2 * (row // quarter % 2) + row // peers
    order = (lax.broadcasted_iota(jnp.int32, (orbs, orbs), 1) == target).astype(jnp.float32)
    both = jnp.dot(both, order, precision=lax.Precision.HIGHEST, preferred_element_type=jnp.float32)
    part[...] = jnp.zeros_like(part)
    for which in range(2):
        part[which, :, :orbs] = both[which * orbs : (which + 1) * orbs]
    own = nz // (2 * orbs)
    packed = jnp.zeros((quarter, nz), jnp.float32)
    for i in range(2 * own):
        start = i % 2 * peers + i % own // 2 * quarter
        rolled = part[i // own, start : start + quarter, :]
        packed = packed + (pltpu.roll(rolled, i * orbs, 1) if i else rolled)

    for g in range(out_ref.shape[0] // quarter):
        out_ref[g * quarter : (g + 1) * quarter] = packed.reshape(quarter, 1, nz)


def finish(cells, x_ref, c_ref, h_ref):
    sums = jnp.sum(x_ref[...], axis=0) * (1.0 / cells)
    own, count = c_ref.shape
    nz = sums.shape[1]
    for r in range(own):
        c_ref[r : r + 1, :] = pltpu.roll(sums, (nz - r * count) % nz, 1)[:, :count]
        h_ref[r : r + 1, :] = pltpu.roll(sums, (nz - (own + r) * count) % nz, 1)[:, :count]


VMEM = pl.BlockSpec(memory_space=pltpu.VMEM)


def call(body, operands, outs, scratch, us, name):
    return pl.pallas_call(
        body,
        out_shape=[s if isinstance(s, jax.ShapeDtypeStruct) else jax.ShapeDtypeStruct(s, jnp.float32) for s in outs],
        in_specs=[VMEM] * len(operands),
        out_specs=[VMEM] * len(outs),
        scratch_shapes=scratch,
        cost_estimate=pl.CostEstimate(flops=int(us * 1e9), bytes_accessed=int(us * 3.5e6), transcendentals=0),
        compiler_params=pltpu.CompilerParams(vmem_limit_bytes=32 << 20),
        name=name,
    )(*operands)


def per_device(cells_x, orbitals, potential):
    pairs, orbs = lax.axis_size("pair"), lax.axis_size("orb")
    size = 2 * pairs
    grid_axes = ("pair", "mem")
    m = lax.axis_index("mem")
    own_orbs, n, ny, nz = orbitals.shape
    half = own_orbs // 2
    count = orbs * own_orbs
    swap = [(g, g ^ 1) for g in range(size)]
    cross = [(g, (g + 1) % size if g % 2 else (g - 1) % size) for g in range(size)]
    along = [(g, (g + 2) % size if g % 2 else (g - 2) % size) for g in range(size)]
    up = [(g, (g + 2) % size) for g in range(size)]
    down = [(g, (g - 2) % size) for g in range(size)]
    f32, bf16 = jnp.float32, jnp.bfloat16
    rows = CHUNK * ny
    mats = call(
        functools.partial(lambda ring, ymat, zmat: matrices(ymat, zmat, ring), ny),
        (),
        [jax.ShapeDtypeStruct((rows, 3 * rows), bf16), jax.ShapeDtypeStruct((3 * nz, nz), bf16)],
        [],
        0.5,
        "matrices",
    )

    v = potential[None]
    v4 = jnp.where(m == 0, v[:, :4], v[:, n - 4 :])
    first = []
    for o in range(half):
        a = b = lax.dynamic_slice_in_dim(orbitals, half * (1 - m) + o, 1, 0)
        c = lax.dynamic_slice_in_dim(orbitals, half * m + o, 1, 0)
        if o == 0:
            a, b, c = jnp.concatenate([a, v], 1), jnp.concatenate([b, v4], 1), jnp.concatenate([c, v4], 1)
        ra = lax.ppermute(a, grid_axes, swap)
        rb = lax.ppermute(b, grid_axes, cross)
        rc = lax.ppermute(c, grid_axes, along)
        first.append((*mats, c, ra, rb, rc))

    def field(layers):
        return pltpu.VMEM((layers, ny, nz), f32)

    def products(layers):
        return pltpu.VMEM((layers // CHUNK, rows, nz), f32)

    second, v_above = [], None
    for o in range(half):
        outs = [(1, n + 4, ny, nz), (1, n, ny, nz), (1, 2 * n + 4, ny, nz)]
        scratch = [field(4 * n), field(2 * n + 8), products(2 * n + 8)]
        if o == 0:
            outs = [(1, 2 * n, ny, nz)] + outs[1:] + [(2 * n + 8, ny, nz)]
            lo, hi, y0, vext = call(first_two, first[o] + (potential,), outs, scratch, 1.0, "filter_1_2")
        else:
            lo, hi, y0 = call(first_two, first[o] + (vext,), outs, scratch, 10.0, "filter_1_2")
        rlo = lax.ppermute(hi, grid_axes, up)
        rhi = lax.ppermute(lo, grid_axes, down)
        v_above = rhi if o == 0 else v_above
        second.append((*mats, rlo, lo, hi, rhi, y0, vext, v_above))

    group = 2 * orbs
    per = 2 * n // group
    scratch = [pltpu.VMEM((2, 2 * n, ny, nz), f32), field(2 * n + 12), field(2 * n + 4), products(2 * n + 12)]

    def peer(x, k):
        return lax.ppermute(x, ("mem", "orb"), [(t, t ^ k) for t in range(group)]) if k else x

    block = (2, per, ny, nz)
    early = len(EARLY)
    outs = [(2, n, ny, nz), (len(LATE), *block)] + [block] * early
    home, late, *early_a = call(last_three, second[0], outs, scratch, 1.5, "filter_3_4_hamiltonian")
    early_a = [peer(x, k) for k, x in zip(EARLY, early_a)]
    outs = [(half, n, ny, nz)] * 2 + [block] * early + [(half, *block)] * len(LATE)
    keep, send, *blocks = call(
        last_three, (*second[1], home, late), outs, scratch, 1.5, "filter_3_4_hamiltonian"
    )
    tied = lax.optimization_barrier((*blocks[early:-1], *early_a))
    early_b = [peer(x, k) for k, x in zip(EARLY, blocks)]
    to_sibling, early_b[-1] = lax.optimization_barrier((tied[LATE.index(1)], early_b[-1]))
    late = [peer(to_sibling if k == 1 else x, k) for k, x in zip(LATE[:-1], tied)] + blocks[-1:]
    xs = [*tied[-early:], *early_b, *late]
    (sums,) = call(
        gram,
        xs,
        [(size * orbs, 1, 2 * own_orbs * count)],
        [pltpu.VMEM((2, count, nz), f32), pltpu.VMEM((half, group, 2 * per * ny + 8, nz), f32)],
        1.3,
        "gram",
    )
    send, sums = lax.optimization_barrier((send, sums))
    back = lax.ppermute(send, grid_axes, swap)
    sums = lax.all_to_all(sums, ("pair", "mem", "orb"), 0, 0, tiled=True)
    filtered = jnp.where(m == 0, jnp.concatenate([keep, back]), jnp.concatenate([back, keep]))
    sums, filtered = lax.optimization_barrier((sums, filtered))
    corr, ham = call(
        functools.partial(finish, float(cells_x * ny * nz)), (sums,), [(own_orbs, count)] * 2, [], 0.3, "finish"
    )
    return filtered, corr, ham


def solution(mesh):
    devices = mesh.devices
    size, orbs = devices.shape
    fine = Mesh(devices.reshape(size // 2, 2, orbs), ("pair", "mem", "orb"))
    grid = ("pair", "mem")

    def whole(orbitals, potential):
        return jax.shard_map(
            functools.partial(per_device, orbitals.shape[1]),
            mesh=fine,
            in_specs=(P("orb", grid, None, None), P(grid, None, None)),
            out_specs=(P("orb", grid, None, None), P("orb", None), P("orb", None)),
            check_vma=False,
        )(orbitals, potential)

    return whole
```

```python
import functools

import jax
import jax.numpy as jnp
from jax import lax
from jax.experimental import pallas as pl
from jax.experimental.pallas import tpu as pltpu
from jax.sharding import Mesh, PartitionSpec as P

COEFS = (-205.0 / 72.0, 8.0 / 5.0, -1.0 / 5.0, 8.0 / 315.0, -1.0 / 560.0)
SCALE = 5040.0
WHOLE = (8064.0, -1008.0, 128.0, -9.0)
LOWER = -1.0
CUT = 4.0
UPPER = 10.0
HALF = (UPPER - CUT) / 2.0
CENTRE = (UPPER + CUT) / 2.0
S1 = HALF / (LOWER - CENTRE)
T2 = 2.0 / S1**2 - 1.0
T4 = 2.0 * T2 * T2 - 1.0
PEERS = (6, 4, 2, 7, 5, 3, 1, 0)
CHUNK = 4


def ring_matrix(rows, cols, ring):
    row = lax.broadcasted_iota(jnp.int32, (rows, cols), 0)
    col = lax.broadcasted_iota(jnp.int32, (rows, cols), 1)
    size = min(rows, cols)
    row, col = lax.rem(row, size), lax.rem(col, size)
    gap = jnp.abs(row - col)
    out = jnp.zeros((rows, cols), jnp.float32)
    for k, value in enumerate(WHOLE, 1):
        out = jnp.where((gap == k) | (gap == ring - k), value, out)
    return jnp.where(row // ring == col // ring, out, 0.0).astype(jnp.bfloat16)


def matrices(ymat, zmat, ring):
    ymat[...] = ring_matrix(*ymat.shape, ring)
    zmat[...] = ring_matrix(*zmat.shape, zmat.shape[1])


def sweep(at, count, v_at, gain, centre, emit, mats, yz, one_sided=False):
    ymat, zmat = mats
    ny, nz = ymat.shape[0] // CHUNK, zmat.shape[1]
    share = 0.5 * gain if one_sided else gain

    def along_yz(c):
        f = jnp.concatenate([at(c + j, slice(0, ny)) for j in range(CHUNK)], axis=0)
        high = f.astype(jnp.bfloat16)
        rest = f - high.astype(jnp.float32)
        mid = rest.astype(jnp.bfloat16)
        low = (rest - mid.astype(jnp.float32)).astype(jnp.bfloat16)
        z = jnp.dot(jnp.concatenate([high, mid, low], axis=1), zmat[...], preferred_element_type=jnp.float32)
        y = jnp.dot(ymat[...], jnp.concatenate([high, mid, low], axis=0), preferred_element_type=jnp.float32)
        yz[c // CHUNK] = y + z

    along_yz(0)
    for c in range(0, count, CHUNK):
        if c + CHUNK < count:
            along_yz(c + CHUNK)
        for r in range(0, ny, 8):
            rows = slice(r, r + 8)
            f = {i: at(i, rows) for i in range(c if one_sided else c - 4, c + CHUNK + 4)}
            for j in range(CHUNK):
                i = c + j
                total = (share * v_at(i, rows) + share * (-1.5 * COEFS[0] - centre)) * f[i]
                total = total + (-0.5 * share / SCALE) * yz[c // CHUNK, j * ny + r : j * ny + r + 8, :]
                for k in range(1, 5):
                    if one_sided:
                        total = total + (-0.5 * gain * COEFS[k]) * f[i + k]
                    else:
                        total = total + (-0.5 * gain * COEFS[k]) * (f[i - k] + f[i + k])
                emit(i, rows, total)


def places():
    m, place = lax.axis_index("mem"), lax.axis_index("orb")
    return m, place, m * lax.axis_size("orb") + place


def first_two(ymat, zmat, mine, ra, rb, rc, *refs):
    m = places()[0]
    mats = (ymat, zmat)
    n = rc.shape[1] if len(refs) == 7 else refs[0].shape[0]
    own, blocks = n + n * m, ((ra, 2 * n - n * m), (rb, 3 * n * m), (rc, 3 * n - 3 * n * m))
    if len(refs) == 7:
        v, lo_ref, hi_ref, y0_ref, y0, w, yz = refs
    else:
        potential, lo_ref, hi_ref, y0_ref, v, y0, w, yz = refs
        v[pl.ds(4 + n * m, n)] = potential[...]
        v[pl.ds(4 + n - n * m, n)] = ra[0, n:]
        v[pl.ds((2 * n + 4) * m, 4)] = rb[0, n:]
        v[pl.ds((2 * n + 4) * (1 - m), 4)] = rc[0, n:]
        lo_ref[0, n + 4 :] = v[8 : 4 + n]
    y0[pl.ds(own, n)] = mine[0, :n]
    for ref, at in blocks:
        y0[pl.ds(at, n)] = ref[0, :n]
    y0_ref[0] = y0[n : 3 * n + 4]

    def one(i, rows, total):
        w[i, rows, :] = total

    sweep(lambda i, r: y0[4 + i, r, :], 2 * n + 8, lambda i, r: v[i, r, :], 1.0 / HALF, CENTRE, one, mats, yz)

    def two(i, rows, total):
        y2 = total - (1.0 / T2) * y0[n + i, rows, :]
        if i < n + 4:
            lo_ref[0, i, rows, :] = y2
        if i >= n:
            hi_ref[0, i - n, rows, :] = y2

    sweep(
        lambda i, r: w[4 + i, r, :], 2 * n, lambda i, r: v[4 + i, r, :], 2.0 / (T2 * HALF), CENTRE, two, mats, yz
    )


def last_three(ymat, zmat, rlo, lo, hi, rhi, y0, v, v_above, *refs):
    outs, (both, u, f, yz) = refs[:-4], refs[-4:]
    mats = (ymat, zmat)
    n = hi.shape[1]

    def y2(i, rows):
        for ref, start in ((rlo, -n), (lo, 0), (hi, n)):
            if i < start + n:
                return ref[0, i - start, rows, :]
        return rhi[0, i - 2 * n, rows, :]

    def three(i, rows, total):
        u[i, rows, :] = total

    def v_at(i, rows):
        return v[i + 4, rows, :] if i < 2 * n + 4 else v_above[0, i - n, rows, :]

    sweep(lambda i, r: y2(i - 4, r), 2 * n + 12, lambda i, r: v_at(i - 4, r), 1.0 / HALF, CENTRE, three, mats, yz)

    def four(i, rows, total):
        f[i, rows, :] = total - (2.0 * T2 / T4) * y2(i, rows) - (1.0 / T4) * y0[0, i, rows, :]

    sweep(lambda i, r: u[4 + i, r, :], 2 * n + 4, v_at, 4.0 * T2 / (T4 * HALF), CENTRE, four, mats, yz)

    def five(i, rows, total):
        both[0, i, rows, :] = f[i, rows, :]
        both[1, i, rows, :] = total

    sweep(lambda i, r: f[i, r, :], 2 * n, v_at, 1.0, 0.0, five, mats, yz, one_sided=True)
    m, _, me = places()
    homes = (n * m, n - n * m)

    def cells(which, k, per):
        return both[which, pl.ds(per * jnp.bitwise_xor(me, k), per)]

    if len(outs) == 2:
        home, blocks = outs
        for i, start in enumerate(homes):
            home[i] = both[0, pl.ds(start, n)]
        for i, k in enumerate(PEERS):
            for which in range(2):
                blocks[i, which] = cells(which, k, blocks.shape[2])
    else:
        home_a, blocks_a, keep, send, *blocks = outs
        for i, ref in enumerate((keep, send)):
            ref[0] = home_a[i]
            ref[1] = both[0, pl.ds(homes[i], n)]
        for i, (k, block) in enumerate(zip(PEERS, blocks)):
            block[0] = blocks_a[i]
            for which in range(2):
                block[1, which] = cells(which, k, block.shape[2])


def gram(*refs):
    *xs, out_ref, part, blocks = refs
    orbs = part.shape[1]
    half, peers, reach, nz = blocks.shape
    rows = xs[0].shape[2] * xs[0].shape[3]
    me = places()[2]
    for k, x in zip(PEERS, xs):
        for o in range(half):
            blocks[o, jnp.bitwise_xor(me, k), : 2 * rows] = x[o].reshape(2 * rows, nz)
    flat = blocks.reshape(half * peers * reach, nz)
    fields = jnp.concatenate(
        [
            jnp.concatenate(
                [
                    flat[pl.ds(o * peers * reach + which * rows + r, peers, stride=reach), :]
                    for which in range(2)
                    for o in range(half)
                ],
                axis=0,
            )
            for r in range(rows)
        ],
        axis=1,
    )
    high = fields.astype(jnp.bfloat16)
    rest = fields - high.astype(jnp.float32)
    mid = rest.astype(jnp.bfloat16)
    low = (rest - mid.astype(jnp.float32)).astype(jnp.bfloat16)
    terms = jnp.concatenate([high, mid, low], axis=0)
    products = lax.dot_general(terms, terms, (((1,), (1,)), ((), ())), preferred_element_type=jnp.float32)
    size = 2 * orbs
    both = jnp.zeros((size, size), jnp.float32)
    for i in (2, 1, 0):
        for j in (2, 1, 0):
            both = both + products[i * size : (i + 1) * size, j * size : (j + 1) * size]
    both = jnp.concatenate([both[:orbs, :orbs], both[orbs:, :orbs] + both[:orbs, orbs:]], axis=0)
    row = lax.broadcasted_iota(jnp.int32, (orbs, orbs), 0)
    quarter = peers // 2
    target = 4 * (row % quarter) + 2 * (row // quarter % 2) + row // peers
    order = (lax.broadcasted_iota(jnp.int32, (orbs, orbs), 1) == target).astype(jnp.float32)
    both = jnp.dot(both, order, precision=lax.Precision.HIGHEST, preferred_element_type=jnp.float32)
    part[...] = jnp.zeros_like(part)
    for which in range(2):
        part[which, :, :orbs] = both[which * orbs : (which + 1) * orbs]
    own = nz // (2 * orbs)
    packed = jnp.zeros((quarter, nz), jnp.float32)
    for i in range(2 * own):
        start = i % 2 * peers + i % own // 2 * quarter
        rolled = part[i // own, start : start + quarter, :]
        packed = packed + (pltpu.roll(rolled, i * orbs, 1) if i else rolled)

    for g in range(out_ref.shape[0] // quarter):
        out_ref[g * quarter : (g + 1) * quarter] = packed.reshape(quarter, 1, nz)


def finish(cells, x_ref, c_ref, h_ref):
    sums = jnp.sum(x_ref[...], axis=0) * (1.0 / cells)
    own, count = c_ref.shape
    nz = sums.shape[1]
    for r in range(own):
        c_ref[r : r + 1, :] = pltpu.roll(sums, (nz - r * count) % nz, 1)[:, :count]
        h_ref[r : r + 1, :] = pltpu.roll(sums, (nz - (own + r) * count) % nz, 1)[:, :count]


VMEM = pl.BlockSpec(memory_space=pltpu.VMEM)


def call(body, operands, outs, scratch, us, name):
    return pl.pallas_call(
        body,
        out_shape=[s if isinstance(s, jax.ShapeDtypeStruct) else jax.ShapeDtypeStruct(s, jnp.float32) for s in outs],
        in_specs=[VMEM] * len(operands),
        out_specs=[VMEM] * len(outs),
        scratch_shapes=scratch,
        cost_estimate=pl.CostEstimate(flops=int(us * 1e9), bytes_accessed=int(us * 3.5e6), transcendentals=0),
        compiler_params=pltpu.CompilerParams(vmem_limit_bytes=32 << 20),
        name=name,
    )(*operands)


def per_device(cells_x, orbitals, potential):
    pairs, orbs = lax.axis_size("pair"), lax.axis_size("orb")
    size = 2 * pairs
    grid_axes = ("pair", "mem")
    m = lax.axis_index("mem")
    own_orbs, n, ny, nz = orbitals.shape
    half = own_orbs // 2
    count = orbs * own_orbs
    swap = [(g, g ^ 1) for g in range(size)]
    cross = [(g, (g + 1) % size if g % 2 else (g - 1) % size) for g in range(size)]
    along = [(g, (g + 2) % size if g % 2 else (g - 2) % size) for g in range(size)]
    up = [(g, (g + 2) % size) for g in range(size)]
    down = [(g, (g - 2) % size) for g in range(size)]
    f32, bf16 = jnp.float32, jnp.bfloat16
    rows = CHUNK * ny
    mats = call(
        functools.partial(lambda ring, ymat, zmat: matrices(ymat, zmat, ring), ny),
        (),
        [jax.ShapeDtypeStruct((rows, 3 * rows), bf16), jax.ShapeDtypeStruct((3 * nz, nz), bf16)],
        [],
        0.5,
        "matrices",
    )

    v = potential[None]
    v4 = jnp.where(m == 0, v[:, :4], v[:, n - 4 :])
    first = []
    for o in range(half):
        a = b = lax.dynamic_slice_in_dim(orbitals, half * (1 - m) + o, 1, 0)
        c = lax.dynamic_slice_in_dim(orbitals, half * m + o, 1, 0)
        if o == 0:
            a, b, c = jnp.concatenate([a, v], 1), jnp.concatenate([b, v4], 1), jnp.concatenate([c, v4], 1)
        ra = lax.ppermute(a, grid_axes, swap)
        rb = lax.ppermute(b, grid_axes, cross)
        rc = lax.ppermute(c, grid_axes, along)
        first.append((*mats, c, ra, rb, rc))

    def field(layers):
        return pltpu.VMEM((layers, ny, nz), f32)

    def products(layers):
        return pltpu.VMEM((layers // CHUNK, rows, nz), f32)

    second, v_above = [], None
    for o in range(half):
        outs = [(1, n + 4, ny, nz), (1, n, ny, nz), (1, 2 * n + 4, ny, nz)]
        scratch = [field(4 * n), field(2 * n + 8), products(2 * n + 8)]
        if o == 0:
            outs = [(1, 2 * n, ny, nz)] + outs[1:] + [(2 * n + 8, ny, nz)]
            lo, hi, y0, vext = call(first_two, first[o] + (potential,), outs, scratch, 1.0, "filter_1_2")
        else:
            lo, hi, y0 = call(first_two, first[o] + (vext,), outs, scratch, 10.0, "filter_1_2")
        rlo = lax.ppermute(hi, grid_axes, up)
        rhi = lax.ppermute(lo, grid_axes, down)
        v_above = rhi if o == 0 else v_above
        second.append((*mats, rlo, lo, hi, rhi, y0, vext, v_above))

    group = 2 * orbs
    per = 2 * n // group
    scratch = [pltpu.VMEM((2, 2 * n, ny, nz), f32), field(2 * n + 12), field(2 * n + 4), products(2 * n + 12)]

    def peer(x, k):
        return lax.ppermute(x, ("mem", "orb"), [(t, t ^ k) for t in range(group)]) if k else x

    block = (2, per, ny, nz)
    results = call(last_three, second[0], [(2, n, ny, nz), (group, *block)], scratch, 1.5, "filter_3_4_hamiltonian")
    outs = [(half, n, ny, nz)] * 2 + [(half, *block)] * group
    keep, send, *blocks = call(last_three, (*second[1], *results), outs, scratch, 1.5, "filter_3_4_hamiltonian")
    xs = [peer(x, k) for k, x in zip(PEERS, blocks)]
    (sums,) = call(
        gram,
        xs,
        [(size * orbs, 1, 2 * own_orbs * count)],
        [pltpu.VMEM((2, count, nz), f32), pltpu.VMEM((half, group, 2 * per * ny + 8, nz), f32)],
        1.3,
        "gram",
    )
    send, sums = lax.optimization_barrier((send, sums))
    back = lax.ppermute(send, grid_axes, swap)
    sums = lax.all_to_all(sums, ("pair", "mem", "orb"), 0, 0, tiled=True)
    filtered = jnp.where(m == 0, jnp.concatenate([keep, back]), jnp.concatenate([back, keep]))
    corr, ham = call(
        functools.partial(finish, float(cells_x * ny * nz)), (sums,), [(own_orbs, count)] * 2, [], 0.3, "finish"
    )
    return filtered, corr, ham


def solution(mesh):
    devices = mesh.devices
    size, orbs = devices.shape
    fine = Mesh(devices.reshape(size // 2, 2, orbs), ("pair", "mem", "orb"))
    grid = ("pair", "mem")

    def whole(orbitals, potential):
        return jax.shard_map(
            functools.partial(per_device, orbitals.shape[1]),
            mesh=fine,
            in_specs=(P("orb", grid, None, None), P(grid, None, None)),
            out_specs=(P("orb", grid, None, None), P("orb", None), P("orb", None)),
            check_vma=False,
        )(orbitals, potential)

    return whole
```
